32 devices in a mesh: expert: 4 (over z), ctx: 2 (over core), dp: 4 (over y, x).
Axes of the slice: x: 2, y: 2, z: 4, core: 2. Of those that a mesh axis runs over, the one named last changes fastest.
Arguments:
- tokens: bfloat16 [16, 2048, 768], P(('expert', 'dp'), 'ctx'), may hold values from -6 to 6
- cotangent: bfloat16 [16, 2048, 768], P(('expert', 'dp'), 'ctx'), may hold values from -6 to 6
- router_noise: float32 [16, 2048, 16], P(('expert', 'dp'), 'ctx'), may hold values from -2.4 to 2.4
- expert_ids: int32 [16, 2048, 2], P(('expert', 'dp'), 'ctx'), may hold values from 0 to 15, all different within a row
- seat_order: int32 [16, 2048], P(('expert', 'dp'), 'ctx'), may hold values from 0 to 63
- gain_attn: float32 [768], replicated, may hold values from 0.5 to 1.5
- w_qkv: bfloat16 [768, 2304], replicated, may hold values from -0.21875 to 0.21875
- w_out: bfloat16 [768, 768], replicated, may hold values from -2 to 2
- gain_moe: float32 [768], replicated, may hold values from 0.5 to 1.5
- w_router: bfloat16 [768, 16], replicated, may hold values from -0.15625 to 0.15625
- w_up: bfloat16 [16, 768, 3072], P('expert'), may hold values from -0.21875 to 0.21875
- w_down: bfloat16 [16, 3072, 768], P('expert'), may hold values from -1.75 to 1.75
Outputs:
- out_tokens: bfloat16 [16, 2048, 768], P(('expert', 'dp'), 'ctx')
- grad_tokens: float32 [16, 2048, 768], P(('expert', 'dp'), 'ctx')
- grad_gain_attn: float32 [768], replicated
- grad_w_qkv: float32 [768, 2304], replicated
- grad_w_out: float32 [768, 768], replicated
- grad_gain_moe: float32 [768], replicated
- grad_w_router: float32 [768, 16], replicated
- grad_w_up: float32 [16, 768, 3072], P('expert', None, ('ctx', 'dp'))
- grad_w_down: float32 [16, 3072, 768], P('expert', ('ctx', 'dp'))
The draws below stay inside these ranges and needn't reach their ends.
Inputs may be any that keep to these rules, and one draw needn't show every extreme that they name: `expert_ids`: each token names two different experts; every expert is named by some token.
All inputs are finite; a program needn't handle non-finite values.
Results may differ from the reference program's by a relative error of at most 0.015.
Values may be sent and summed in bfloat16 or wider, within the bound.
No kernel may reach another device: no remote copies, remote signals or barrier semaphores. Data moves between devices by JAX's collectives and lax.ppermute only.
A program may use at most 576 MiB of HBM per device.

```python
from functools import partial
import jax
import jax.numpy as jnp
from jax import lax

D = 768
HEADS = 12
HEAD_DIM = 64
FF = 3072
SEQ = 2048
IMG_DEV = 1
EXPERTS = 16
IMAGES = 16
TOK_DEV = 1024
CAP = 128
N_CTX = 2


def set_ends(array, rng, least, largest):
    spot = [jax.random.randint(jax.random.fold_in(rng, axis), (), 0, length) for axis, length in enumerate(array.shape)]
    longest = array.shape.index(max(array.shape))
    beside = spot[:longest] + [(spot[longest] + 1) % array.shape[longest]] + spot[longest + 1:]
    return array.at[tuple(spot)].set(least).at[tuple(beside)].set(largest)


def block_levels(key, dims, cuts, low, top_value):
    def one(axis_at, parts):
        draws = jax.random.uniform(jax.random.fold_in(jax.random.fold_in(key, 6), axis_at), (parts,), jnp.float32, low / len(cuts), top_value / len(cuts))
        return jnp.repeat(jnp.exp(draws), dims[axis_at] // parts).reshape((-1,) + (1,) * (len(dims) - axis_at - 1))

    factor_of = one(*cuts[0])
    for cut in cuts[1:]:
        factor_of = factor_of * one(*cut)
    return factor_of


def distinct(rng, rows, count, top, lift):
    sequence = jax.random.permutation(jax.random.fold_in(rng, 1), count)
    boost = sequence
    for power in range(3):
        boost = boost * boost // count
    boost = boost * lift // count
    lots = jax.random.randint(jax.random.fold_in(rng, 2), (rows, count), 0, 4096) + boost
    sure = jax.random.permutation(jax.random.fold_in(rng, 3), rows)[jnp.arange(count) % rows]
    lots = jnp.where(jnp.arange(rows)[:, None] == sure[None, :], 1 << 14, lots)
    merit = lots * count + jnp.arange(count)
    return lax.top_k(merit.astype(jnp.int32), top)[1].astype(jnp.int32)


def bell_draw(rng, shape, width, bound, cuts=(), kind=jnp.bfloat16):
    drawn = width * jax.random.normal(rng, shape, jnp.float32)
    if cuts:
        drawn = drawn * block_levels(rng, shape, cuts, -0.22, 0.18)
    return jnp.clip(drawn, -bound, bound).astype(kind)


def setup_inputs(seed: int = 0) -> dict:
    arg_keys = jax.random.split(jax.random.key(seed), 13)
    tokens = bell_draw(arg_keys[0], (IMAGES, SEQ, D), 1.0, 6.0, ((0, 16), (1, 2)))
    cotangent = bell_draw(arg_keys[1], (IMAGES, SEQ, D), 1.0, 6.0, ((0, 16), (1, 2)))
    router_noise = bell_draw(arg_keys[2], (IMAGES, SEQ, EXPERTS), 0.4, 2.4, ((0, 16), (1, 2)), jnp.float32)
    expert_ids = distinct(arg_keys[3], IMAGES * SEQ, EXPERTS, 2, 1024).reshape((IMAGES, SEQ, 2))
    seat_order = set_ends(jax.random.randint(arg_keys[4], (IMAGES, SEQ), 0, 64), jax.random.fold_in(arg_keys[4], 1), 0, 63).astype(jnp.int32)
    gain_attn = jnp.clip(1.0 + 0.1 * jax.random.normal(arg_keys[5], (D,), jnp.float32), 0.5, 1.5)
    w_qkv = bell_draw(arg_keys[6], (D, 3 * D), D ** -0.5, 0.21875)
    w_out = bell_draw(arg_keys[7], (D, D), (max(D // 96, 1)) ** -0.5, 2.0)
    gain_moe = jnp.clip(1.0 + 0.1 * jax.random.normal(arg_keys[8], (D,), jnp.float32), 0.5, 1.5)
    w_router = bell_draw(arg_keys[9], (D, EXPERTS), (2 * D) ** -0.5, 0.15625)
    w_up = bell_draw(arg_keys[10], (EXPERTS, D, FF), D ** -0.5, 0.21875, ((0, 4),))
    w_down = bell_draw(arg_keys[11], (EXPERTS, FF, D), (max(FF // 256, 1)) ** -0.5, 1.75, ((0, 4),))
    return {"tokens": tokens, "cotangent": cotangent, "router_noise": router_noise, "expert_ids": expert_ids, "seat_order": seat_order, "gain_attn": gain_attn, "w_qkv": w_qkv, "w_out": w_out, "gain_moe": gain_moe, "w_router": w_router, "w_up": w_up, "w_down": w_down}


HIGHEST_PREC = lax.Precision.HIGHEST
NORM_EPS = 1e-06

@jax.custom_vjp
def low(v):
    return lax.optimization_barrier(v.astype(jnp.bfloat16)).astype(jnp.float32)

@jax.custom_vjp
def low_back(v):
    return v

def low_keep(v):
    return (low(v), None)

def low_pass(kept, grad):
    return (grad,)

def back_keep(v):
    return (v, None)

def back_low(kept, grad):
    return (low(grad),)
low.defvjp(low_keep, low_pass)
low_back.defvjp(back_keep, back_low)

def layer_norm(values_in, gain_vec):
    centred = values_in - lax.optimization_barrier(jnp.mean(values_in, axis=-1, keepdims=True))
    return centred * lax.rsqrt(lax.optimization_barrier(jnp.mean(centred * centred, axis=-1, keepdims=True)) + NORM_EPS) * gain_vec

def matmul(left_in, right_in):
    return jnp.einsum('...d,df->...f', left_in, right_in, precision=HIGHEST_PREC)

def seating(group_ids, group_order):
    token_count = group_ids.shape[0]
    places = jnp.arange(token_count, dtype=jnp.int32)
    earlier = (group_order[:, None] < group_order[None, :]) | (group_order[:, None] == group_order[None, :]) & (places[:, None] < places[None, :])
    earlier = earlier.astype(jnp.float32)
    lane_ids = jnp.arange(EXPERTS, dtype=jnp.int32)
    first_hot = (group_ids[:, 0:1] == lane_ids[None, :]).astype(jnp.float32)
    second_hot = (group_ids[:, 1:2] == lane_ids[None, :]).astype(jnp.float32)
    rank_first = lax.optimization_barrier(jnp.sum(jnp.einsum('st,se->te', earlier, first_hot, precision=HIGHEST_PREC) * first_hot, axis=-1))
    ahead_second = jnp.einsum('st,se->te', earlier, second_hot, precision=HIGHEST_PREC) + lax.optimization_barrier(jnp.sum(first_hot, axis=0))[None, :]
    rank_second = lax.optimization_barrier(jnp.sum(ahead_second * second_hot, axis=-1))
    slot_ids = jnp.arange(EXPERTS * CAP, dtype=jnp.int32)

    def slot_table(picked, rank_of):
        target = picked * CAP + rank_of.astype(jnp.int32)
        is_live = rank_of < CAP
        return ((slot_ids[:, None] == target[None, :]) & is_live[None, :]).astype(jnp.float32)
    return (slot_table(group_ids[:, 0], rank_first), slot_table(group_ids[:, 1], rank_second), first_hot, second_hot)

def grouped(values_in):
    trailing = values_in.shape[2:]
    blocks = values_in.reshape((IMAGES // IMG_DEV, IMG_DEV, N_CTX, SEQ // N_CTX) + trailing)
    blocks = jnp.moveaxis(blocks, 2, 1)
    return blocks.reshape((IMAGES // IMG_DEV * N_CTX, TOK_DEV) + trailing)

def ungrouped(values_in):
    trailing = values_in.shape[2:]
    blocks = values_in.reshape((IMAGES // IMG_DEV, N_CTX, IMG_DEV, SEQ // N_CTX) + trailing)
    blocks = jnp.moveaxis(blocks, 1, 2)
    return blocks.reshape((IMAGES, SEQ) + trailing)

def attend(item_in):
    queries, keys_in, values_in = item_in
    scores = low_back(jnp.einsum('iqhd,ikhd->ihqk', queries, keys_in, precision=HIGHEST_PREC) * HEAD_DIM ** (-0.5))
    attn_probs = jax.nn.softmax(scores, axis=-1)
    mixed_out = jnp.einsum('ihqk,ikhd->iqhd', low(attn_probs), values_in, precision=HIGHEST_PREC)
    return low(low_back(mixed_out))

def dispatch_rows(item_in):
    row_block, group_ids, group_order = item_in
    first_table, second_table, first_hot, second_hot = seating(group_ids, group_order)
    return jnp.einsum('pt,td->pd', first_table + second_table, row_block, precision=HIGHEST_PREC)

def expert(item_in):
    row_block, up_weight, down_weight = item_in
    hidden_pre = low_back(matmul(row_block, up_weight))
    active = low(jax.nn.gelu(hidden_pre, approximate=True))
    return low(low_back(matmul(active, down_weight)))

def receive(item_in):
    returned, gate_rows, group_ids, group_order = item_in
    first_table, second_table, first_hot, second_hot = seating(group_ids, group_order)
    gate_first = lax.optimization_barrier(jnp.sum(gate_rows * first_hot, axis=-1, keepdims=True))
    gate_second = lax.optimization_barrier(jnp.sum(gate_rows * second_hot, axis=-1, keepdims=True))
    top_part = gate_first * jnp.einsum('pt,pd->td', first_table, returned, precision=HIGHEST_PREC)
    other_part = gate_second * jnp.einsum('pt,pd->td', second_table, returned, precision=HIGHEST_PREC)
    return top_part + other_part

def forward(tokens, gain_attn, w_qkv, w_out, gain_moe, w_router, w_up, w_down, router_noise, expert_ids, seat_order):
    normed = low(layer_norm(tokens, gain_attn))
    qkv_rows = low(low_back(matmul(normed, w_qkv)))
    blocks = qkv_rows.reshape(IMAGES // IMG_DEV, IMG_DEV, SEQ, 3, HEADS, HEAD_DIM)
    mixed_out = lax.map(jax.checkpoint(attend), (blocks[:, :, :, 0], blocks[:, :, :, 1], blocks[:, :, :, 2]))
    mixed_out = mixed_out.reshape(IMAGES, SEQ, D)
    branch = low_back(matmul(mixed_out, w_out))
    middle = tokens + branch
    routed = low(layer_norm(middle, gain_moe))
    gate_probs = jax.nn.softmax(matmul(routed, w_router) + router_noise, axis=-1)
    group_ids = grouped(expert_ids)
    group_order = grouped(seat_order)
    buffers = low_back(lax.map(jax.checkpoint(dispatch_rows), (grouped(routed), group_ids, group_order)))
    groups = buffers.shape[0]
    per_expert = jnp.moveaxis(buffers.reshape(groups, EXPERTS, CAP, D), 1, 0).reshape(EXPERTS, groups * CAP, D)
    results = lax.map(jax.checkpoint(expert), (per_expert, w_up, w_down))
    results = jnp.moveaxis(results.reshape(EXPERTS, groups, CAP, D), 0, 1).reshape(groups, EXPERTS * CAP, D)
    combined = lax.map(jax.checkpoint(receive), (results, grouped(gate_probs), group_ids, group_order))
    return middle + ungrouped(combined)

def reference(tokens, cotangent, router_noise, expert_ids, seat_order, gain_attn, w_qkv, w_out, gain_moe, w_router, w_up, w_down):
    closed = partial(forward, router_noise=router_noise.astype(jnp.float32), expert_ids=expert_ids, seat_order=seat_order)
    float_args = (tokens.astype(jnp.float32), gain_attn.astype(jnp.float32), w_qkv.astype(jnp.float32), w_out.astype(jnp.float32), gain_moe.astype(jnp.float32), w_router.astype(jnp.float32), w_up.astype(jnp.float32), w_down.astype(jnp.float32))
    output, pullback = jax.vjp(closed, *float_args)
    gradients = pullback(cotangent.astype(jnp.float32))
    return (output.astype(jnp.bfloat16), gradients[0], gradients[1], gradients[2], gradients[3], gradients[4], gradients[5], gradients[6], gradients[7])
```

```python
import functools
import math

import jax
import jax.numpy as jnp
from jax import lax
from jax.experimental import pallas as pl
from jax.experimental.pallas import tpu as pltpu
from jax.sharding import PartitionSpec as P

HEADS = 12
NORM_EPS = 1e-06
BF = jnp.bfloat16
F32 = jnp.float32
NN = (((1,), (0,)), ((), ()))
NT = (((1,), (1,)), ((), ()))
VMEM_BYTES = 60 << 20
EXTRA = 8
SMALL = 128


def estimate(flops, moved, slow=0):
    return pl.CostEstimate(flops=flops // 4, bytes_accessed=moved // 4, transcendentals=slow // 4)


def mm(left, right, dims=NN):
    return lax.dot_general(left, right, dims, preferred_element_type=F32)


def norm_forward(values_in, gain_vec):
    centre_mean = jnp.mean(values_in, axis=-1, keepdims=True)
    centred = values_in - centre_mean
    inv_scale = lax.rsqrt(jnp.mean(centred * centred, axis=-1, keepdims=True) + NORM_EPS)
    unit_rows = centred * inv_scale
    return (unit_rows * gain_vec, unit_rows, inv_scale)


def norm_backward(gradient, unit_rows, inv_scale, gain_vec):
    scaled = gradient * gain_vec
    inner_sum = (
        scaled
        - jnp.mean(scaled, axis=-1, keepdims=True)
        - unit_rows * jnp.mean(scaled * unit_rows, axis=-1, keepdims=True)
    )
    return (inner_sum * inv_scale, jnp.sum(gradient * unit_rows, axis=0))


def attend_kernel(q_ref, k0, k1, v0, v1, o_ref, p_ref, li_ref, vext, *, scale):
    half = k0.shape[0]

    @pl.when(pl.program_id(1) == 0)
    def _():
        ones = jnp.ones((half, 128), BF)
        vext[0:half, 0:128] = v0[...]
        vext[half:, 0:128] = v1[...]
        vext[0:half, 128:256] = ones
        vext[half:, 128:256] = ones

    low = lax.broadcasted_iota(jnp.int32, q_ref.shape, 1) < 64
    q = q_ref[...]
    outs, sums = [], []
    factor = scale * math.log2(math.e)
    for h in range(2):
        picked = jnp.where(low if h == 0 else jnp.logical_not(low), q, jnp.zeros_like(q))
        s0 = mm(picked, k0[...], NT)
        s1 = mm(picked, k1[...], NT)
        peak = factor * jnp.maximum(
            jnp.max(s0, axis=1, keepdims=True), jnp.max(s1, axis=1, keepdims=True)
        )
        p_ref[h, :, 0:half] = jnp.exp2(s0 * factor - peak).astype(BF)
        p_ref[h, :, half:] = jnp.exp2(s1 * factor - peak).astype(BF)
        both = mm(p_ref[h], vext[...])
        outs.append(both[:, 0:128])
        sums.append(both[:, 128:256])
    inv = 1.0 / jnp.where(low, sums[0], sums[1])
    o_ref[...] = (jnp.where(low, outs[0], outs[1]) * inv).astype(BF)
    li_ref[...] = inv


def attend(qkv, kv_other, block):
    rows = qkv.shape[0]
    width = qkv.shape[1] // 3
    pairs = width // 128
    tile = pl.BlockSpec((block, 128), lambda h, i: (i, h))
    return pl.pallas_call(
        functools.partial(attend_kernel, scale=1.0 / math.sqrt(width // HEADS)),
        grid=(pairs, rows // block),
        in_specs=[
            tile,
            pl.BlockSpec((rows, 128), lambda h, i: (0, pairs + h)),
            pl.BlockSpec((rows, 128), lambda h, i: (0, h)),
            pl.BlockSpec((rows, 128), lambda h, i: (0, 2 * pairs + h)),
            pl.BlockSpec((rows, 128), lambda h, i: (0, pairs + h)),
        ],
        out_specs=[tile, pl.BlockSpec((2, block, 2 * rows), lambda h, i: (h, i, 0)), tile],
        out_shape=[
            jax.ShapeDtypeStruct((rows, width), BF),
            jax.ShapeDtypeStruct((HEADS, rows, 2 * rows), BF),
            jax.ShapeDtypeStruct((rows, width), F32),
        ],
        scratch_shapes=[pltpu.VMEM((2 * rows, 256), BF)],
        compiler_params=pltpu.CompilerParams(vmem_limit_bytes=VMEM_BYTES),
        cost_estimate=estimate(8 * 12 * rows * rows * 256, HEADS * rows * rows * 4, HEADS * rows * rows * 2),
        name="attend",
    )(qkv, qkv, kv_other, qkv, kv_other)


def attend_back_kernel(
    q_ref, k0, k1, v0, v1, o_ref, g_ref, li_ref, p_ref,
    dq_ref, own_ref, far_ref, vext, kacc, vacc, *, scale, steps,
):
    i = pl.program_id(1)
    half = k0.shape[0]
    lane = lax.broadcasted_iota(jnp.int32, q_ref.shape, 1)
    low = lane < 64

    @pl.when(i == 0)
    def _():
        ones = jnp.where(lax.broadcasted_iota(jnp.int32, (half, 128), 1) < 2, 1.0, 0.0).astype(BF)
        vext[0:half, 0:128] = v0[...]
        vext[half:, 0:128] = v1[...]
        vext[0:half, 128:256] = ones
        vext[half:, 128:256] = ones

    g = g_ref[...].astype(F32) * li_ref[...]
    gb = g.astype(BF)
    go = g * o_ref[...].astype(F32)
    qt = q_ref[...].T
    gt = gb.T
    dqs = []
    for h in range(2):
        mine = low if h == 0 else jnp.logical_not(low)
        delta = -jnp.sum(jnp.where(mine, go, 0.0), axis=1, keepdims=True)
        high = delta.astype(BF).astype(F32)
        extra = jnp.where(lane == 0, high, jnp.where(lane == 1, delta - high, 0.0)).astype(BF)
        gext = jnp.concatenate([jnp.where(mine, gb, jnp.zeros_like(gb)), extra], axis=1)
        p = p_ref[h]
        ds = (p.astype(F32) * mm(gext, vext[...], NT)).astype(BF)
        dqs.append(mm(ds[:, 0:half], k0[...]) + mm(ds[:, half:], k1[...]))
        rows = slice(64 * h, 64 * h + 64)
        dk = mm(qt[rows], ds)
        dv = mm(gt[rows], p)

        @pl.when(i == 0)
        def _():
            kacc[rows] = dk
            vacc[rows] = dv

        @pl.when(i > 0)
        def _():
            kacc[rows] += dk
            vacc[rows] += dv

    dq_ref[...] = (jnp.where(low, dqs[0], dqs[1]) * scale).astype(BF)

    @pl.when(i == steps - 1)
    def _():
        own_ref[0] = kacc[:, 0:half].T * scale
        own_ref[1] = vacc[:, 0:half].T
        far_ref[0] = (kacc[:, half:].T * scale).astype(BF)
        far_ref[1] = vacc[:, half:].T.astype(BF)


def attend_back(qkv, kv_other, mixed, grad, inv_sum, probs, block, first, count):
    rows = qkv.shape[0]
    width = qkv.shape[1] // 3
    pairs = width // 128
    steps = rows // block
    tile = pl.BlockSpec((block, 128), lambda h, i: (i, first + h))
    both = pl.BlockSpec((2, rows, 128), lambda h, i: (0, 0, h))
    return pl.pallas_call(
        functools.partial(attend_back_kernel, scale=1.0 / math.sqrt(width // HEADS), steps=steps),
        grid=(count, steps),
        in_specs=[
            tile,
            pl.BlockSpec((rows, 128), lambda h, i: (0, pairs + first + h)),
            pl.BlockSpec((rows, 128), lambda h, i: (0, first + h)),
            pl.BlockSpec((rows, 128), lambda h, i: (0, 2 * pairs + first + h)),
            pl.BlockSpec((rows, 128), lambda h, i: (0, pairs + first + h)),
            tile,
            tile,
            tile,
            pl.BlockSpec((2, block, 2 * rows), lambda h, i: (first + h, i, 0)),
        ],
        out_specs=[pl.BlockSpec((block, 128), lambda h, i: (i, h)), both, both],
        out_shape=[
            jax.ShapeDtypeStruct((rows, 128 * count), BF),
            jax.ShapeDtypeStruct((2, rows, 128 * count), F32),
            jax.ShapeDtypeStruct((2, rows, 128 * count), BF),
        ],
        scratch_shapes=[
            pltpu.VMEM((2 * rows, 256), BF),
            pltpu.VMEM((128, 2 * rows), F32),
            pltpu.VMEM((128, 2 * rows), F32),
        ],
        compiler_params=pltpu.CompilerParams(vmem_limit_bytes=VMEM_BYTES),
        cost_estimate=estimate(16 * 2 * count * rows * rows * 256, 2 * count * rows * rows * 4, 0),
        name="attend_back",
    )(qkv, qkv, kv_other, qkv, kv_other, mixed, grad, inv_sum, probs)


def grad_qkv_kernel(normed, *refs, count, with_out):
    grad_ref, dqkv_ref = refs[-2:]
    cols = dqkv_ref.shape[1]
    wide = cols // 3
    at = 0
    for n in range(count):
        dq, own, far = refs[n], refs[count + n], refs[2 * count + n]
        size = dq.shape[1]
        dqkv_ref[:, at : at + size] = dq[...]
        for m in range(2):
            start = (m + 1) * wide + at
            dqkv_ref[:, start : start + size] = (own[m] + far[m].astype(F32)).astype(BF)
        at += size
    grad_ref[:, 0:cols] = mm(normed[...].T, dqkv_ref[...]).astype(BF)
    if with_out:
        mixed, branch, small = refs[3 * count : 3 * count + 3]
        width = branch.shape[1]
        grad_ref[:, cols : cols + width] = mm(mixed[...].T, branch[...]).astype(BF)
        value = small[...]
        high = value.astype(BF).astype(F32)
        rest = jnp.zeros((SMALL - 2 * value.shape[0], value.shape[1]), F32)
        grad_ref[:, cols + width :] = jnp.concatenate([high, value - high, rest], axis=0).T.astype(BF)


def grad_qkv(normed, dqs, owns, fars, more=()):
    rows, width = normed.shape
    cols = 3 * sum(dq.shape[1] for dq in dqs)
    out_cols = cols + (more[1].shape[1] + SMALL if more else 0)
    return pl.pallas_call(
        functools.partial(grad_qkv_kernel, count=len(dqs), with_out=bool(more)),
        out_shape=[
            jax.ShapeDtypeStruct((width, out_cols), BF),
            jax.ShapeDtypeStruct((rows, cols), BF),
        ],
        compiler_params=pltpu.CompilerParams(vmem_limit_bytes=VMEM_BYTES),
        cost_estimate=estimate(2 * rows * width * out_cols, 8 * rows * out_cols),
        name="grad_qkv",
    )(normed, *dqs, *owns, *fars, *more)


GELU_A = math.sqrt(2.0 / math.pi)
GELU_B = 0.044715


def gelu_both(v):
    square = v * v
    t = jnp.tanh(v * (GELU_A + GELU_A * GELU_B * square))
    half = 0.5 + 0.5 * t
    slope = half + (0.5 * v) * (1.0 - t * t) * (GELU_A + 3 * GELU_A * GELU_B * square)
    return v * half, slope


def expert_kernel(
    which, x_in, dy_in, up_ref, down_ref, out_ref, back_ref, grad_ref,
    x, xt, dp, dpt, gate, out_acc, dx_acc, act, dhid, *, steps, pieces,
):
    f = pl.program_id(0)
    peers, cap = dy_in.shape[0], dy_in.shape[1]

    @pl.when(f == 0)
    def _():
        sent = [x_in[r, cap : cap + EXTRA, 0:cap].astype(F32) for r in range(peers)]
        gates = jnp.concatenate([g[0:1] + g[1:2] + g[2:3] for g in sent], axis=0).T
        for r in range(peers):
            at = slice(r * cap, (r + 1) * cap)
            x[at] = x_in[r, 0:cap, :]
            g = gates[:, r : r + 1]
            gate[at] = g
            dp[at] = (dy_in[r].astype(F32) * g).astype(BF)
        xt[...] = x[...].T
        dpt[...] = dp[...].T

    up = up_ref[0]
    down = down_ref[0]
    value, slope = gelu_both(mm(x[...], up))
    act[...] = value.astype(BF)
    dhid[...] = (mm(dp[...], down, NT) * slope).astype(BF)

    @pl.when(f == 0)
    def _():
        out_acc[...] = mm(act[...], down)
        dx_acc[...] = mm(dhid[...], up, NT)

    @pl.when(f > 0)
    def _():
        out_acc[...] += mm(act[...], down)
        dx_acc[...] += mm(dhid[...], up, NT)

    gup = mm(xt[...], dhid[...]).astype(BF)
    gdown = mm(dpt[...], act[...]).astype(BF)
    wide = gup.shape[1] // pieces
    for s in range(pieces):
        grad_ref[s, 0, 0] = gup[:, s * wide : (s + 1) * wide]
        grad_ref[s, 0, 1] = gdown[:, s * wide : (s + 1) * wide]

    @pl.when(f == steps - 1)
    def _():
        sums = []
        for r in range(peers):
            at = slice(r * cap, (r + 1) * cap)
            produced = out_acc[at].astype(BF).astype(F32)
            back_ref[r, 0:cap, :] = dx_acc[at].astype(BF)
            out_ref[r] = (produced * gate[at]).astype(BF)
            sums.append(jnp.sum(produced * dy_in[r].astype(F32), axis=1, keepdims=True))
        sums = jnp.concatenate(sums, axis=1).T
        for r in range(peers):
            put_extra(back_ref, r, cap, sums[r : r + 1])


def put_extra(ref, r, cap, row):
    width = ref.shape[2]
    high, mid, low = three_parts(row)
    line = lax.broadcasted_iota(jnp.int32, (EXTRA, cap), 0)
    full = jnp.where(
        line == 0, high.astype(F32), jnp.where(line == 1, mid.astype(F32), jnp.where(line == 2, low.astype(F32), 0.0))
    )
    ref[r, cap:, :] = jnp.concatenate([full, jnp.zeros((EXTRA, width - cap), F32)], axis=1).astype(BF)


def run_expert(which, part, x, dy, w_up, w_down, n_ctx, n_dp, chunk=768):
    peers, cap, width = x.shape[0], x.shape[1] - EXTRA, x.shape[2]
    mine = jax.ShapeDtypeStruct((peers, cap, width), BF)
    rows = peers * cap
    hidden = w_up.shape[-1]
    steps = hidden // chunk
    wide = hidden // (n_ctx * n_dp)
    pieces = chunk // wide
    per = n_dp // pieces
    full = lambda shape: pl.BlockSpec(shape, lambda f, j: (0,) * len(shape))
    return pl.pallas_call(
        functools.partial(expert_kernel, steps=steps, pieces=pieces),
        grid_spec=pltpu.PrefetchScalarGridSpec(
            num_scalar_prefetch=1,
            grid=(steps,),
            in_specs=[
                full(x.shape),
                pl.BlockSpec(mine.shape, lambda f, j: (0, part, 0)),
                pl.BlockSpec((1, width, chunk), lambda f, j: (j[0], 0, f)),
                pl.BlockSpec((1, chunk, width), lambda f, j: (j[0], f, 0)),
            ],
            out_specs=[
                full(mine.shape),
                full(x.shape),
                pl.BlockSpec((pieces, 1, 2, width, wide), lambda f, j: (f % per, f // per, 0, 0, 0)),
            ],
            scratch_shapes=[
                pltpu.VMEM((rows, width), BF),
                pltpu.VMEM((width, rows), BF),
                pltpu.VMEM((rows, width), BF),
                pltpu.VMEM((width, rows), BF),
                pltpu.VMEM((rows, 1), F32),
                pltpu.VMEM((rows, width), F32),
                pltpu.VMEM((rows, width), F32),
                pltpu.VMEM((rows, chunk), BF),
                pltpu.VMEM((rows, chunk), BF),
            ],
        ),
        out_shape=[
            mine,
            jax.ShapeDtypeStruct(x.shape, BF),
            jax.ShapeDtypeStruct((n_dp, n_ctx, 2, width, wide), BF),
        ],
        compiler_params=pltpu.CompilerParams(vmem_limit_bytes=VMEM_BYTES),
        cost_estimate=estimate(12 * rows * width * hidden, 8 * width * hidden, rows * hidden),
        name="expert",
    )(which, x, dy, w_up, w_down)


def seats(expert_ids, seat_order, expert_count, capacity, place_of):
    token_count = expert_ids.shape[0]
    places = jnp.arange(token_count, dtype=jnp.int32)
    earlier = (seat_order[:, None] < seat_order[None, :]) | (
        seat_order[:, None] == seat_order[None, :]
    ) & (places[:, None] < places[None, :])
    earlier = earlier.astype(BF)
    lane_ids = jnp.arange(expert_count, dtype=jnp.int32)
    first_hot = expert_ids[:, 0:1] == lane_ids[None, :]
    second_hot = expert_ids[:, 1:2] == lane_ids[None, :]
    both_hot = jnp.concatenate([first_hot, second_hot], axis=1).astype(BF)
    ahead = jnp.einsum("st,se->te", earlier, both_hot, preferred_element_type=F32)
    ahead_first = ahead[:, :expert_count]
    ahead_second = ahead[:, expert_count:] + jnp.sum(first_hot.astype(F32), axis=0)[None, :]
    rank_first = jnp.sum(jnp.where(first_hot, ahead_first, 0.0), axis=-1)
    rank_second = jnp.sum(jnp.where(second_hot, ahead_second, 0.0), axis=-1)

    def slot(picked, rank):
        at = rank.astype(jnp.int32)
        return jnp.where(at < capacity, place_of(picked) * capacity + at, -1)

    return (
        slot(expert_ids[:, 0], rank_first),
        slot(expert_ids[:, 1], rank_second),
        first_hot,
        second_hot,
    )


def three_parts(v):
    high = v.astype(BF)
    rest = v - high.astype(F32)
    mid = rest.astype(BF)
    return high, mid, (rest - mid.astype(F32)).astype(BF)


def seat_rows_kernel(t1, t2, *refs, parts):
    *gate_refs, rows_ref, out_ref = refs
    peers = out_ref.shape[0]
    cap = (out_ref.shape[1] - (EXTRA if gate_refs else 0)) // len(parts)
    tokens = t1.shape[1]

    def hot_of(t, block):
        ids = lax.broadcasted_iota(jnp.int32, (cap, tokens), 0) + block * cap
        return ids == t[...]

    if gate_refs:
        left1 = jnp.concatenate(three_parts(gate_refs[0][...]), axis=0)
        left2 = jnp.concatenate(three_parts(gate_refs[1][...]), axis=0)
    for r in range(peers):
        for n, part in enumerate(parts):
            first = hot_of(t1, part * peers + r)
            second = hot_of(t2, part * peers + r)
            hot = jnp.where(first | second, 1.0, 0.0).astype(BF)
            out_ref[r, n * cap : (n + 1) * cap, :] = mm(hot, rows_ref[...]).astype(BF)
            if gate_refs:
                got = mm(left1, jnp.where(first, 1.0, 0.0).astype(BF), NT) + mm(
                    left2, jnp.where(second, 1.0, 0.0).astype(BF), NT
                )
                put_extra(out_ref, r, cap, jnp.sum(got, axis=0, keepdims=True))


def seat_rows(t1, t2, rows, gates, parts, peers, cap):
    tokens, width = rows.shape
    per_peer = len(parts) * cap + (EXTRA if gates else 0)
    return pl.pallas_call(
        functools.partial(seat_rows_kernel, parts=parts),
        out_shape=jax.ShapeDtypeStruct((peers, per_peer, width), BF),
        compiler_params=pltpu.CompilerParams(vmem_limit_bytes=VMEM_BYTES),
        cost_estimate=estimate(2 * peers * per_peer * tokens * width, 4 * tokens * width),
        name="seat_rows",
    )(t1[None], t2[None], *[g[None] for g in gates], rows)


def rows_back(t1, t2, back, extra):
    tokens = t1.shape[0]
    total, place = None, 0
    firsts = jnp.zeros((tokens, 1), F32)
    seconds = firsts
    for ref in back:
        cap = ref.shape[1] - extra
        group = max(1, 512 // cap)
        for b in range(0, ref.shape[0], group):
            ids = lax.broadcasted_iota(jnp.int32, (tokens, group * cap), 1) + place
            place += group * cap
            first = ids == t1
            second = ids == t2
            hot = jnp.where(first | second, 1.0, 0.0).astype(BF)
            add = mm(hot, jnp.concatenate([ref[b + n, 0:cap, :] for n in range(group)], axis=0))
            total = add if total is None else total + add
            if extra:
                sent = [ref[b + n, cap:, 0:cap].astype(F32) for n in range(group)]
                dg = jnp.concatenate([g[0:1] + g[1:2] + g[2:3] for g in sent], axis=1)
                firsts += jnp.sum(jnp.where(first, dg, 0.0), axis=1, keepdims=True)
                seconds += jnp.sum(jnp.where(second, dg, 0.0), axis=1, keepdims=True)
    return total, firsts, seconds


def unseat_kernel(t1, t2, base, *refs):
    out_ref = refs[-1]
    total, _, _ = rows_back(t1[...], t2[...], refs[:-1], 0)
    out_ref[...] = (base[...] + total).astype(BF)


def unseat(t1, t2, base, parts, block=256):
    tokens, width = base.shape
    col = pl.BlockSpec((block, 1), lambda i: (i, 0))
    rows = pl.BlockSpec((block, width), lambda i: (i, 0))
    return pl.pallas_call(
        unseat_kernel,
        grid=(tokens // block,),
        in_specs=[col, col, rows] + [pl.BlockSpec(part.shape, lambda i: (0, 0, 0)) for part in parts],
        out_specs=rows,
        out_shape=jax.ShapeDtypeStruct((tokens, width), BF),
        compiler_params=pltpu.CompilerParams(vmem_limit_bytes=VMEM_BYTES),
        cost_estimate=estimate(4 * tokens * tokens * width, 8 * tokens * width),
        name="unseat",
    )(t1[:, None], t2[:, None], base, *parts)


def route_back_kernel(
    t1, t2, ids, probs, dy, middle, gain, w_router, w_out, *refs,
):
    dmiddle_ref, dbranch_ref, dmixed_ref, small_ref = refs[-4:]
    total, dg1, dg2 = rows_back(t1[...], t2[...], refs[:-4], EXTRA)
    p = probs[...]
    experts = p.shape[1]
    lane = lax.broadcasted_iota(jnp.int32, p.shape, 1)
    d_gates = jnp.where(lane == ids[:, 0:1], dg1, 0.0) + jnp.where(lane == ids[:, 1:2], dg2, 0.0)
    d_logits = p * (d_gates - jnp.sum(p * d_gates, axis=1, keepdims=True))
    d_routed = total
    for piece in three_parts(d_logits):
        d_routed = d_routed + mm(piece, w_router[...], NT)
    v = middle[...]
    centred = v - jnp.mean(v, axis=1, keepdims=True)
    inv = lax.rsqrt(jnp.mean(centred * centred, axis=1, keepdims=True) + NORM_EPS)
    unit = centred * inv
    routed = (unit * gain[...]).astype(BF)
    scaled = d_routed * gain[...]
    d_norm = inv * (
        scaled
        - jnp.mean(scaled, axis=1, keepdims=True)
        - unit * jnp.mean(scaled * unit, axis=1, keepdims=True)
    )
    d_middle = dy[...].astype(F32) + d_norm
    d_branch = d_middle.astype(BF)
    dmiddle_ref[...] = d_middle
    dbranch_ref[...] = d_branch
    dmixed_ref[...] = mm(d_branch, w_out[...], NT).astype(BF)
    to_router = 0.0
    for piece in three_parts(d_logits.T):
        to_router = to_router + mm(piece, routed)
    to_gain = jnp.sum(d_routed * unit, axis=0, keepdims=True)

    @pl.when(pl.program_id(0) == 0)
    def _():
        small_ref[...] = jnp.zeros_like(small_ref)

    small_ref[0:experts, :] += to_router
    small_ref[experts : experts + 1, :] += to_gain


def route_back(t1, t2, ids, probs, dy, middle, gain, w_router, w_out, parts, block=256):
    tokens, width = dy.shape
    experts = probs.shape[1]
    line = lambda cols: pl.BlockSpec((block, cols), lambda i: (i, 0))
    full = lambda a: pl.BlockSpec(a.shape, lambda i: (0,) * a.ndim)
    gain = gain[None]
    return pl.pallas_call(
        route_back_kernel,
        grid=(tokens // block,),
        in_specs=[
            line(1), line(1), line(2), line(experts), line(width), line(width),
            full(gain), full(w_router), full(w_out),
        ]
        + [full(part) for part in parts],
        out_specs=[
            line(width), line(width), line(width),
            pl.BlockSpec((experts + 8, width), lambda i: (0, 0)),
        ],
        out_shape=[
            jax.ShapeDtypeStruct((tokens, width), F32),
            jax.ShapeDtypeStruct((tokens, width), BF),
            jax.ShapeDtypeStruct((tokens, width), BF),
            jax.ShapeDtypeStruct((experts + 8, width), F32),
        ],
        compiler_params=pltpu.CompilerParams(vmem_limit_bytes=VMEM_BYTES),
        cost_estimate=estimate(6 * tokens * tokens * width, 20 * tokens * width),
        name="route_back",
    )(t1[:, None], t2[:, None], ids, probs, dy, middle, gain, w_router, w_out, *parts)


def swap(value):
    n = lax.axis_size("ctx")
    return lax.ppermute(value, "ctx", [(i, (i + 1) % n) for i in range(n)])


def exchange(value, axes):
    return lax.all_to_all(value, axes, 0, 0, tiled=True)


def shift(value, axis, by):
    n = lax.axis_size(axis)
    return lax.ppermute(value, axis, [(i, (i + by) % n) for i in range(n)])


def scatter_sum(x, axis):
    n = lax.axis_size(axis)
    me = lax.axis_index(axis)
    got = [
        shift(lax.dynamic_index_in_dim(x, lax.rem(me + s, n), 0, keepdims=False), axis, s)
        for s in range(1, n)
    ]
    total = lax.dynamic_index_in_dim(x, me, 0, keepdims=False).astype(F32)
    for piece in got:
        total = total + piece.astype(F32)
    return total.astype(BF)


def gather_back(x, axis):
    n = lax.axis_size(axis)
    return jnp.stack([x] + [shift(x, axis, s) for s in range(1, n)])


def sum_everywhere(value):
    part = value
    for axis in ("ctx", "dp", "expert"):
        n = lax.axis_size(axis)
        part = scatter_sum(part.reshape(n, part.shape[0] // n, value.shape[1]), axis)
    full = gather_back(gather_back(part, "expert"), "dp")
    return full, swap(full)


def assemble_kernel(at, w_ref, *refs, groups, spans):
    ins, outs = refs[: 2 * groups], refs[2 * groups :]
    here, me = at[0], at[2]
    core = pl.program_id(0)
    owners, rows = ins[0].shape[1], ins[0].shape[2]
    for z in range(owners):
        back = lax.rem(me + owners - z, owners)
        for mine, other, span in zip(ins[:groups], ins[groups:], spans):
            piece = jnp.where(core == here, mine[0, back].astype(F32), other[0, back].astype(F32))
            for src, which, dst, size in span:
                outs[which][z * rows : (z + 1) * rows, dst : dst + size] = piece[:, src : src + size]
    outs[-1][...] = jnp.sum(outs[0][...] * w_ref[...].astype(F32), axis=1, keepdims=True)


def assemble(sums, spans, widths, w_qkv):
    n_dp, owners, rows, _ = sums[0][0].shape
    n_ctx = lax.axis_size("ctx")
    block = owners * rows
    height = n_ctx * n_dp * block
    at = jnp.stack([lax.axis_index(axis) for axis in ("ctx", "dp", "expert")]).astype(jnp.int32)
    back = lambda c, d, at: ((at[1] + n_dp - d) % n_dp, 0, 0, 0)
    line = lambda cols: pl.BlockSpec((block, cols), lambda c, d, at: (c * n_dp + d, 0))
    arrays = [full for full, _ in sums] + [other for _, other in sums]
    widths = [*widths, 1]
    return pl.pallas_call(
        functools.partial(assemble_kernel, groups=len(sums), spans=spans),
        grid_spec=pltpu.PrefetchScalarGridSpec(
            num_scalar_prefetch=1,
            grid=(n_ctx, n_dp),
            in_specs=[line(w_qkv.shape[1])] + [pl.BlockSpec((1,) + full.shape[1:], back) for full in arrays],
            out_specs=[line(cols) for cols in widths],
        ),
        out_shape=[jax.ShapeDtypeStruct((height, cols), F32) for cols in widths],
        compiler_params=pltpu.CompilerParams(vmem_limit_bytes=VMEM_BYTES),
        cost_estimate=estimate(height * 2304, 12 * height * 2304),
        name="assemble",
    )(at, w_qkv, *arrays)


def spread_kernel(at, *refs, parts):
    mine, other = refs[:parts], refs[parts : 2 * parts]
    up_ref, down_ref = refs[2 * parts :]
    j = pl.program_id(0)
    for part in range(parts):
        for src, kept in ((mine, True), (other, False)):

            @pl.when((j % parts == part) & ((j // parts == at[0]) == kept))
            def _():
                value = src[part][0] if kept else src[part]
                up_ref[0] = value[0].astype(F32)
                down_ref[0] = value[1].astype(F32).T


def spread(summed):
    parts = len(summed)
    n_ctx, _, width, cols = summed[0].shape
    here = lax.axis_index("ctx")
    other = [swap(lax.dynamic_index_in_dim(s, 1 - here, 0, keepdims=False)) for s in summed]
    mine = pl.BlockSpec((1, 2, width, cols), lambda j, at: (at[0], 0, 0, 0))
    return pl.pallas_call(
        functools.partial(spread_kernel, parts=parts),
        grid_spec=pltpu.PrefetchScalarGridSpec(
            num_scalar_prefetch=1,
            grid=(n_ctx * parts,),
            in_specs=[mine] * parts + [pl.BlockSpec((2, width, cols), lambda j, at: (0, 0, 0))] * parts,
            out_specs=[
                pl.BlockSpec((1, width, cols), lambda j, at: (j, 0, 0)),
                pl.BlockSpec((1, cols, width), lambda j, at: (j, 0, 0)),
            ],
        ),
        out_shape=[
            jax.ShapeDtypeStruct((n_ctx * parts, width, cols), F32),
            jax.ShapeDtypeStruct((n_ctx * parts, cols, width), F32),
        ],
        compiler_params=pltpu.CompilerParams(vmem_limit_bytes=VMEM_BYTES),
        cost_estimate=estimate(width * cols, 24 * parts * n_ctx * width * cols),
        name="spread",
    )(here.astype(jnp.int32)[None], *summed, *other)


def after(value, *others):
    return lax.optimization_barrier((value, others))[0]


def body(
    tokens,
    cotangent,
    router_noise,
    expert_ids,
    seat_order,
    gain_attn,
    w_qkv,
    w_out,
    gain_moe,
    w_router,
    w_up,
    w_down,
):
    image_count, half_len, width = tokens.shape
    rows = image_count * half_len
    expert_count = router_noise.shape[-1]
    n_owner = lax.axis_size("expert")
    n_ctx = lax.axis_size("ctx")
    n_dp = lax.axis_size("dp")
    here = lax.axis_index("ctx")
    per_device = w_up.shape[0] // n_ctx
    capacity = (2 * rows + expert_count - 1) // expert_count
    peers = n_owner * n_ctx
    to_owner = ("expert", "ctx")

    def place_of(e):
        return (e % per_device) * peers + e // per_device

    t1, t2, first_hot, second_hot = seats(
        expert_ids.reshape(rows, 2), seat_order.reshape(rows), expert_count, capacity, place_of
    )
    dy_b = cotangent.reshape(rows, width)
    every = tuple(range(per_device))
    dy_slots = seat_rows(t1, t2, dy_b, (), every, peers, capacity)
    dy_got = exchange(dy_slots, to_owner)

    tokens_f = after(tokens, dy_slots).reshape(rows, width).astype(F32)
    normed_a, unit_a, inv_a = norm_forward(tokens_f, gain_attn)
    normed_ab = normed_a.astype(BF)
    qkv_b = mm(normed_ab, w_qkv).astype(BF)
    kv_other = swap(qkv_b[:, width:])
    mixed_b, probs, inv_sum = attend(qkv_b, kv_other, 512)

    middle = tokens_f + mm(mixed_b, w_out)
    normed_m, _, _ = norm_forward(middle, gain_moe)
    routed_b = normed_m.astype(BF)
    logits = mm(routed_b, w_router) + router_noise.reshape(rows, expert_count)
    gate_probs = jax.nn.softmax(logits, axis=-1)
    gate_first = jnp.sum(jnp.where(first_hot, gate_probs, 0.0), axis=-1)
    gate_second = jnp.sum(jnp.where(second_hot, gate_probs, 0.0), axis=-1)

    gates = (gate_first, gate_second)
    sent = [seat_rows(t1, t2, routed_b, gates, (part,), peers, capacity) for part in every]
    sent[0], dy_got = lax.optimization_barrier((sent[0], dy_got))
    x_next = exchange(sent[0], to_owner)
    out_parts, dx_back, summed = [], [], []
    for part in every:
        which = (here * per_device + part).astype(jnp.int32)[None]
        x = x_next
        if part + 1 < per_device:
            x, following = lax.optimization_barrier((x, sent[part + 1]))
            x_next = exchange(following, to_owner)
        out, dx, grads = run_expert(which, part, x, dy_got, w_up, w_down, n_ctx, n_dp)
        out_parts.append(out)
        if part + 1 < per_device:
            dx, x_next, grads = lax.optimization_barrier((dx, x_next, grads))
        if dx_back:
            dx, dx_back[-1], grads = lax.optimization_barrier((dx, dx_back[-1], grads))
        dx_back.append(exchange(dx, to_owner))
        summed.append(
            lax.psum_scatter(
                grads.reshape(-1, grads.shape[-1]), "dp", scatter_dimension=0, tiled=True
            ).reshape(grads.shape[1:])
        )
    out_parts, dx_back = lax.optimization_barrier((out_parts, dx_back))

    d_middle, d_branch_b, d_mixed_b, small = route_back(
        t1, t2, expert_ids.reshape(rows, 2), gate_probs, dy_b, middle, gain_moe, w_router, w_out, dx_back
    )

    pairs = width // 128
    cut = pairs - pairs // 3
    groups = [(0, cut), (cut, pairs - cut)]
    d_normed_a = 0.0
    qkv_sums, spans, returned = [], [], []
    for n, (first, count) in enumerate(groups):
        returned.append(exchange(out_parts[n], to_owner) if n < per_device else None)
        dq, own, far = attend_back(
            qkv_b, kv_other, mixed_b, d_mixed_b, inv_sum, probs, 512, first, count
        )
        if n == 0:
            far, own, returned[0], d_mixed_b = lax.optimization_barrier(
                (far, own, returned[0], d_mixed_b)
            )
            out_parts[1:] = after(out_parts[1:], returned[0])
        if n == 1:
            far, returned, summed = lax.optimization_barrier((far, returned, summed))
        more = (mixed_b, d_branch_b, small) if n == 0 else ()
        grad, d_qkv = grad_qkv(normed_ab, [dq], [own], [swap(far)], more)
        qkv_sums.append(sum_everywhere(grad))
        start, wide = 128 * first, 128 * count
        spans.append([(m * wide, 0, m * width + start, wide) for m in range(3)])
        if n == 0:
            spans[0] += [(3 * wide, 1, 0, width), (3 * wide + width, 2, 0, SMALL)]
        columns = [w_qkv[:, m * width + start : m * width + start + wide] for m in range(3)]
        d_normed_a = d_normed_a + mm(d_qkv, jnp.concatenate(columns, axis=1), NT)
    returned += [exchange(part, to_owner) for part in out_parts[len(groups) :]]
    d_tokens_norm, _ = norm_backward(d_normed_a, unit_a, inv_a, gain_attn)
    d_tokens = d_middle + d_tokens_norm

    result = unseat(t1, t2, middle, returned)
    grad_up, grad_down = spread(summed)

    grad_w_qkv, grad_w_out, small_sum, gain_sum = assemble(
        qkv_sums, spans, (3 * width, width, SMALL), w_qkv
    )
    n_small = small.shape[0]
    small_sum = small_sum[:, :n_small] + small_sum[:, n_small : 2 * n_small]
    return (
        result.reshape(image_count, half_len, width),
        d_tokens.reshape(image_count, half_len, width),
        gain_sum[:, 0] / gain_attn,
        grad_w_qkv,
        grad_w_out,
        small_sum[:, expert_count],
        small_sum[:, :expert_count],
        grad_up,
        grad_down,
    )


def solution(mesh):
    placed = (
        P(("expert", "dp"), "ctx", None),
        P(("expert", "dp"), "ctx", None),
        P(("expert", "dp"), "ctx", None),
        P(("expert", "dp"), "ctx", None),
        P(("expert", "dp"), "ctx"),
        P(),
        P(),
        P(),
        P(),
        P(),
        P("expert", None, None),
        P("expert", None, None),
    )
    return jax.shard_map(
        body,
        mesh=mesh,
        in_specs=placed,
        out_specs=(
            P(("expert", "dp"), "ctx", None),
            P(("expert", "dp"), "ctx", None),
            P(),
            P(),
            P(),
            P(),
            P(),
            P("expert", None, ("ctx", "dp")),
            P("expert", ("ctx", "dp"), None),
        ),
        check_vma=False,
    )
```

```python
import functools
import math

import jax
import jax.numpy as jnp
from jax import lax
from jax.experimental import pallas as pl
from jax.experimental.pallas import tpu as pltpu
from jax.sharding import PartitionSpec as P

HEADS = 12
NORM_EPS = 1e-06
BF = jnp.bfloat16
F32 = jnp.float32
NN = (((1,), (0,)), ((), ()))
NT = (((1,), (1,)), ((), ()))
VMEM_BYTES = 60 << 20
EXTRA = 8
SMALL = 128
SAFE = 40.0


def estimate(flops, moved, slow=0):
    return pl.CostEstimate(flops=flops // 4, bytes_accessed=moved // 4, transcendentals=slow // 4)


def mm(left, right, dims=NN):
    return lax.dot_general(left, right, dims, preferred_element_type=F32)


def norm_forward(values_in, gain_vec):
    centre_mean = jnp.mean(values_in, axis=-1, keepdims=True)
    centred = values_in - centre_mean
    inv_scale = lax.rsqrt(jnp.mean(centred * centred, axis=-1, keepdims=True) + NORM_EPS)
    unit_rows = centred * inv_scale
    return (unit_rows * gain_vec, unit_rows, inv_scale)


def norm_backward(gradient, unit_rows, inv_scale, gain_vec):
    scaled = gradient * gain_vec
    inner_sum = (
        scaled
        - jnp.mean(scaled, axis=-1, keepdims=True)
        - unit_rows * jnp.mean(scaled * unit_rows, axis=-1, keepdims=True)
    )
    return (inner_sum * inv_scale, jnp.sum(gradient * unit_rows, axis=0))


def attend_kernel(q_ref, k0, k1, v0, v1, o_ref, p_ref, li_ref, vext, ksize, *, scale):
    half = k0.shape[0]

    def largest(v):
        return jnp.max(jnp.sum(v * v, axis=1, keepdims=True))

    @pl.when(pl.program_id(1) == 0)
    def _():
        ones = jnp.ones((half, 128), BF)
        vext[0:half, 0:128] = v0[...]
        vext[half:, 0:128] = v1[...]
        vext[0:half, 128:256] = ones
        vext[half:, 128:256] = ones
        ksize[0] = jnp.maximum(largest(k0[...].astype(F32)), largest(k1[...].astype(F32)))

    low = lax.broadcasted_iota(jnp.int32, q_ref.shape, 1) < 64
    q = q_ref[...]
    factor = scale * math.log2(math.e)
    small = largest(q.astype(F32)) * ksize[0] * (factor * factor) < SAFE * SAFE

    def run(shifted):
        outs, sums = [], []
        for h in range(2):
            picked = jnp.where(low if h == 0 else jnp.logical_not(low), q, jnp.zeros_like(q))
            s0 = mm(picked, k0[...], NT) * factor
            s1 = mm(picked, k1[...], NT) * factor
            if shifted:
                peak = jnp.maximum(
                    jnp.max(s0, axis=1, keepdims=True), jnp.max(s1, axis=1, keepdims=True)
                )
                s0 = s0 - peak
                s1 = s1 - peak
            p_ref[h, :, 0:half] = jnp.exp2(s0).astype(BF)
            p_ref[h, :, half:] = jnp.exp2(s1).astype(BF)
            both = mm(p_ref[h], vext[...])
            outs.append(both[:, 0:128])
            sums.append(both[:, 128:256])
        inv = 1.0 / jnp.where(low, sums[0], sums[1])
        o_ref[...] = (jnp.where(low, outs[0], outs[1]) * inv).astype(BF)
        li_ref[...] = inv

    pl.when(small)(lambda: run(False))
    pl.when(jnp.logical_not(small))(lambda: run(True))


def attend(qkv, kv_other, block):
    rows = qkv.shape[0]
    width = qkv.shape[1] // 3
    pairs = width // 128
    tile = pl.BlockSpec((block, 128), lambda h, i: (i, h))
    return pl.pallas_call(
        functools.partial(attend_kernel, scale=1.0 / math.sqrt(width // HEADS)),
        grid=(pairs, rows // block),
        in_specs=[
            tile,
            pl.BlockSpec((rows, 128), lambda h, i: (0, pairs + h)),
            pl.BlockSpec((rows, 128), lambda h, i: (0, h)),
            pl.BlockSpec((rows, 128), lambda h, i: (0, 2 * pairs + h)),
            pl.BlockSpec((rows, 128), lambda h, i: (0, pairs + h)),
        ],
        out_specs=[tile, pl.BlockSpec((2, block, 2 * rows), lambda h, i: (h, i, 0)), tile],
        out_shape=[
            jax.ShapeDtypeStruct((rows, width), BF),
            jax.ShapeDtypeStruct((HEADS, rows, 2 * rows), BF),
            jax.ShapeDtypeStruct((rows, width), F32),
        ],
        scratch_shapes=[pltpu.VMEM((2 * rows, 256), BF), pltpu.SMEM((1,), F32)],
        compiler_params=pltpu.CompilerParams(vmem_limit_bytes=VMEM_BYTES),
        cost_estimate=estimate(rows * width, rows * width),
        name="attend",
    )(qkv, qkv, kv_other, qkv, kv_other)


def attend_back_kernel(
    q_ref, k0, k1, v0, v1, o_ref, g_ref, li_ref, p_ref,
    dq_ref, own_ref, far_ref, vext, kacc, vacc, *, scale, steps,
):
    i = pl.program_id(1)
    half = k0.shape[0]
    lane = lax.broadcasted_iota(jnp.int32, q_ref.shape, 1)
    low = lane < 64

    @pl.when(i == 0)
    def _():
        ones = jnp.where(lax.broadcasted_iota(jnp.int32, (half, 128), 1) < 2, 1.0, 0.0).astype(BF)
        vext[0:half, 0:128] = v0[...]
        vext[half:, 0:128] = v1[...]
        vext[0:half, 128:256] = ones
        vext[half:, 128:256] = ones

    g = g_ref[...].astype(F32) * li_ref[...]
    gb = g.astype(BF)
    go = g * o_ref[...].astype(F32)
    qt = q_ref[...].T
    gt = gb.T
    dqs = []
    for h in range(2):
        mine = low if h == 0 else jnp.logical_not(low)
        delta = -jnp.sum(jnp.where(mine, go, 0.0), axis=1, keepdims=True)
        high = delta.astype(BF).astype(F32)
        extra = jnp.where(lane == 0, high, jnp.where(lane == 1, delta - high, 0.0)).astype(BF)
        gext = jnp.concatenate([jnp.where(mine, gb, jnp.zeros_like(gb)), extra], axis=1)
        p = p_ref[h]
        ds = (p.astype(F32) * mm(gext, vext[...], NT)).astype(BF)
        dqs.append(mm(ds[:, 0:half], k0[...]) + mm(ds[:, half:], k1[...]))
        rows = slice(64 * h, 64 * h + 64)
        dk = mm(qt[rows], ds)
        dv = mm(gt[rows], p)

        @pl.when(i == 0)
        def _():
            kacc[rows] = dk
            vacc[rows] = dv

        @pl.when(i > 0)
        def _():
            kacc[rows] += dk
            vacc[rows] += dv

    dq_ref[...] = (jnp.where(low, dqs[0], dqs[1]) * scale).astype(BF)

    @pl.when(i == steps - 1)
    def _():
        own_ref[0] = kacc[:, 0:half].T * scale
        own_ref[1] = vacc[:, 0:half].T
        far_ref[0] = (kacc[:, half:].T * scale).astype(BF)
        far_ref[1] = vacc[:, half:].T.astype(BF)


def attend_back(qkv, kv_other, mixed, grad, inv_sum, probs, block, first, count):
    rows = qkv.shape[0]
    width = qkv.shape[1] // 3
    pairs = width // 128
    steps = rows // block
    tile = pl.BlockSpec((block, 128), lambda h, i: (i, first + h))
    both = pl.BlockSpec((2, rows, 128), lambda h, i: (0, 0, h))
    return pl.pallas_call(
        functools.partial(attend_back_kernel, scale=1.0 / math.sqrt(width // HEADS), steps=steps),
        grid=(count, steps),
        in_specs=[
            tile,
            pl.BlockSpec((rows, 128), lambda h, i: (0, pairs + first + h)),
            pl.BlockSpec((rows, 128), lambda h, i: (0, first + h)),
            pl.BlockSpec((rows, 128), lambda h, i: (0, 2 * pairs + first + h)),
            pl.BlockSpec((rows, 128), lambda h, i: (0, pairs + first + h)),
            tile,
            tile,
            tile,
            pl.BlockSpec((2, block, 2 * rows), lambda h, i: (first + h, i, 0)),
        ],
        out_specs=[pl.BlockSpec((block, 128), lambda h, i: (i, h)), both, both],
        out_shape=[
            jax.ShapeDtypeStruct((rows, 128 * count), BF),
            jax.ShapeDtypeStruct((2, rows, 128 * count), F32),
            jax.ShapeDtypeStruct((2, rows, 128 * count), BF),
        ],
        scratch_shapes=[
            pltpu.VMEM((2 * rows, 256), BF),
            pltpu.VMEM((128, 2 * rows), F32),
            pltpu.VMEM((128, 2 * rows), F32),
        ],
        compiler_params=pltpu.CompilerParams(vmem_limit_bytes=VMEM_BYTES),
        cost_estimate=estimate(rows * width, rows * width),
        name="attend_back",
    )(qkv, qkv, kv_other, qkv, kv_other, mixed, grad, inv_sum, probs)


def grad_qkv_kernel(core, normed, *refs, count, with_out):
    if count:
        grad_ref, dqkv_ref = refs[-2:]
        cols = dqkv_ref.shape[1]
        wide = cols // 3
        at = 0
        for n in range(count):
            dq, own, far = refs[n], refs[count + n], refs[2 * count + n]
            size = dq.shape[1]
            dqkv_ref[:, at : at + size] = dq[...]
            for m in range(2):
                start = (m + 1) * wide + at
                dqkv_ref[:, start : start + size] = (own[m] + far[m].astype(F32)).astype(BF)
            at += size
        more = refs[3 * count :]
    else:
        dqkv_ref, grad_ref = refs[0], refs[-1]
        cols = dqkv_ref.shape[1]
        more = refs[1:]
    grad_ref[:, 0:cols] = mm(normed[...].T, dqkv_ref[...]).astype(BF)
    if with_out:
        mixed, branch, small = more[:3]
        width = branch.shape[1]
        grad_ref[:, cols : cols + width] = mm(mixed[...].T, branch[...]).astype(BF)
        value = small[...]
        high = value.astype(BF).astype(F32)
        rest = jnp.zeros((SMALL - 2 * value.shape[0], value.shape[1]), F32)
        grad_ref[:, cols + width :] = jnp.concatenate([high, value - high, rest], axis=0).T.astype(BF)


def grad_qkv_half(core, normed, sides, count, more):
    rows, width = normed.shape
    half = width // 2
    cols = sum(side.shape[-1] for side in sides[:count]) * 3 if count else sides[0].shape[1]
    out_cols = cols + (more[1].shape[1] + SMALL if more else 0)
    full = lambda a: pl.BlockSpec(a.shape, lambda i, core: (0,) * a.ndim)
    part = lambda a: pl.BlockSpec((a.shape[0], half), lambda i, core: (0, core[0]))
    out_specs = [pl.BlockSpec((half, out_cols), lambda i, core: (0, 0))]
    out_shape = [jax.ShapeDtypeStruct((half, out_cols), BF)]
    if count:
        out_specs.append(pl.BlockSpec((rows, cols), lambda i, core: (0, 0)))
        out_shape.append(jax.ShapeDtypeStruct((rows, cols), BF))
    return pl.pallas_call(
        functools.partial(grad_qkv_kernel, count=count, with_out=bool(more)),
        grid_spec=pltpu.PrefetchScalarGridSpec(
            num_scalar_prefetch=1,
            grid=(1,),
            in_specs=[part(normed)]
            + [full(side) for side in sides]
            + ([part(more[0]), full(more[1]), part(more[2])] if more else []),
            out_specs=out_specs,
        ),
        out_shape=out_shape,
        compiler_params=pltpu.CompilerParams(vmem_limit_bytes=VMEM_BYTES),
        cost_estimate=estimate(rows * width, rows * width),
        name="grad_qkv",
    )(core.astype(jnp.int32)[None], normed, *sides, *more)


def grad_qkv(normed, dqs, owns, fars, more=()):
    here = lax.axis_index("ctx")
    give, d_qkv = grad_qkv_half(1 - here, normed, (*dqs, *owns, *fars), len(dqs), more)
    other = swap(give)
    (keep,) = grad_qkv_half(here, normed, (d_qkv,), 0, more)
    return [keep, other], d_qkv


GELU_A = math.sqrt(2.0 / math.pi)
GELU_B = 0.044715


def gelu_both(v):
    square = v * v
    t = jnp.tanh(v * (GELU_A + GELU_A * GELU_B * square))
    half = 0.5 + 0.5 * t
    slope = half + (0.5 * v) * (1.0 - t * t) * (GELU_A + 3 * GELU_A * GELU_B * square)
    return v * half, slope


def put_extra(ref, r, row):
    width = ref.shape[2]
    cap = row.shape[1]
    line = lax.broadcasted_iota(jnp.int32, (EXTRA, cap), 0)
    full = jnp.zeros((EXTRA, cap), F32)
    for n, piece in enumerate(three_parts(row)):
        full = jnp.where(line == n, piece.astype(F32), full)
    full = jnp.concatenate([full, jnp.zeros((EXTRA, width - cap), F32)], axis=1)
    ref[r, ref.shape[1] - EXTRA :, :] = full.astype(BF)


def get_extra(ref, r, lanes):
    sent = ref[r, ref.shape[1] - EXTRA :, lanes].astype(F32)
    return sent[0:1] + sent[1:2] + sent[2:3]


def expert_kernel(which, x_in, gate_in, dy_in, *refs, part, parts, steps, first):
    last = part == parts - 1
    if not first:
        refs = refs[1:]
    dg_in = ()
    if last:
        dg_in, refs = refs[: parts - 1], refs[parts - 1 :]
    up_ref, down_ref, out_ref, dx_ref, act_ref, dhid_ref, dp_ref, *refs = refs
    if not last:
        dg_out, refs = refs[0], refs[1:]
    x, gate, out_acc, dx_acc = refs
    f = pl.program_id(0)
    peers, cap = dy_in.shape[0], dy_in.shape[1]

    @pl.when(f == 0)
    def _():
        lanes = slice(part * cap, (part + 1) * cap)
        gates = jnp.concatenate([get_extra(gate_in, r, lanes) for r in range(peers)], axis=0).T
        for r in range(peers):
            at = slice(r * cap, (r + 1) * cap)
            x[at] = x_in[r, 0:cap, :]
            g = gates[:, r : r + 1]
            gate[at] = g
            dp_ref[at] = (dy_in[r].astype(F32) * g).astype(BF)

    up = up_ref[0]
    down = down_ref[0]
    value, slope = gelu_both(mm(x[...], up))
    act_ref[...] = value.astype(BF)
    dhid_ref[...] = (mm(dp_ref[...], down, NT) * slope).astype(BF)

    @pl.when(f == 0)
    def _():
        dx_acc[...] = mm(dhid_ref[...], up, NT)
        out_acc[...] = mm(act_ref[...], down)

    @pl.when(f > 0)
    def _():
        dx_acc[...] += mm(dhid_ref[...], up, NT)
        out_acc[...] += mm(act_ref[...], down)

    @pl.when(f == steps - 1)
    def _():
        sums = []
        for r in range(peers):
            at = slice(r * cap, (r + 1) * cap)
            produced = out_acc[at].astype(BF).astype(F32)
            dx_ref[r, 0:cap, :] = dx_acc[at].astype(BF)
            out_ref[r] = (produced * gate[at]).astype(BF)
            sums.append(jnp.sum(produced * dy_in[r].astype(F32), axis=1, keepdims=True))
        sums = jnp.concatenate(sums, axis=1).T
        if last:
            full = jnp.concatenate([ref[...] for ref in dg_in] + [sums], axis=1)
            for r in range(peers):
                put_extra(dx_ref, r, full[r : r + 1])
        else:
            dg_out[...] = sums


def run_expert(which, part, parts, x, first_x, dy, outs, dgates, w_up, w_down, chunk=768):
    peers, width = x.shape[0], x.shape[2]
    cap = dy.shape[1] // parts
    rows = peers * cap
    hidden = w_up.shape[-1]
    last = part == parts - 1
    full = lambda shape: pl.BlockSpec(shape, lambda f, j: (0,) * len(shape))
    wide = pl.BlockSpec((rows, chunk), lambda f, j: (0, f))
    dx_shape = (peers, cap + (EXTRA if last else 0), width)
    extra_at = (first_x.shape[1] - EXTRA) // EXTRA
    out_specs = [
        pl.BlockSpec((peers, cap, width), lambda f, j: (0, part, 0)),
        full(dx_shape), wide, wide, full((rows, width)),
    ]
    out_shape = [
        jax.ShapeDtypeStruct(dy.shape, BF),
        jax.ShapeDtypeStruct(dx_shape, BF),
        jax.ShapeDtypeStruct((rows, hidden), BF),
        jax.ShapeDtypeStruct((rows, hidden), BF),
        jax.ShapeDtypeStruct((rows, width), BF),
    ]
    if not last:
        out_specs.append(full((peers, cap)))
        out_shape.append(jax.ShapeDtypeStruct((peers, cap), F32))
        dgates = []
    return pl.pallas_call(
        functools.partial(
            expert_kernel, part=part, parts=parts, steps=hidden // chunk, first=outs is None
        ),
        grid_spec=pltpu.PrefetchScalarGridSpec(
            num_scalar_prefetch=1,
            grid=(hidden // chunk,),
            in_specs=[
                full(x.shape),
                pl.BlockSpec((peers, EXTRA, width), lambda f, j: (0, extra_at, 0)),
                pl.BlockSpec((peers, cap, width), lambda f, j: (0, part, 0)),
                *[pl.BlockSpec(memory_space=pl.ANY)] * (outs is not None),
                *[full(d.shape) for d in dgates],
                pl.BlockSpec((1, width, chunk), lambda f, j: (j[0], 0, f)),
                pl.BlockSpec((1, chunk, width), lambda f, j: (j[0], f, 0)),
            ],
            out_specs=out_specs,
            scratch_shapes=[
                pltpu.VMEM((rows, width), BF),
                pltpu.VMEM((rows, 1), F32),
                pltpu.VMEM((rows, width), F32),
                pltpu.VMEM((rows, width), F32),
            ],
        ),
        out_shape=out_shape,
        compiler_params=pltpu.CompilerParams(vmem_limit_bytes=VMEM_BYTES),
        cost_estimate=estimate(8 * rows * width * hidden, 4 * width * hidden, rows * hidden),
        input_output_aliases={} if outs is None else {4: 0},
        name="expert",
    )(which, x, first_x, dy, *([] if outs is None else [outs]), *dgates, w_up, w_down)


def weights_kernel(at, *refs, count, pieces, turned):
    acts, dhids, refs = refs[:count], refs[count : 2 * count], refs[2 * count :]
    if turned:
        xt, dpt, out_ref = refs
    else:
        xs, dps, (out_ref, xt, dpt) = refs[:count], refs[count : 2 * count], refs[2 * count :]

        @pl.when(pl.program_id(0) == 0)
        def _():
            place = 0
            for x, dp in zip(xs, dps):
                rows = dp.shape[0]
                cap = rows // x.shape[0]
                held = jnp.concatenate([x[r, 0:cap, :] for r in range(x.shape[0])], axis=0)
                xt[:, place : place + rows] = held.T
                dpt[:, place : place + rows] = dp[...].T
                place += rows

    def product(left, rights):
        total, place = None, 0
        for right in rights:
            rows = right.shape[0]
            add = mm(left[:, place : place + rows], right[...])
            total = add if total is None else total + add
            place += rows
        return total.astype(BF)

    gup = product(xt, dhids)
    gdown = product(dpt, acts)
    wide = gup.shape[1] // pieces
    for s in range(pieces):
        out_ref[s, 0] = gup[:, s * wide : (s + 1) * wide]
        out_ref[s, 1] = gdown[:, s * wide : (s + 1) * wide]


def weight_grads(core, acts, dhids, sides, turned, n_ctx, n_dp, chunk=768):
    width, hidden = (sides[0].shape[0] if turned else sides[0].shape[2]), acts[0].shape[1]
    rows = sum(a.shape[0] for a in acts)
    half = hidden // n_ctx
    steps = half // chunk
    wide = half // n_dp
    pieces = chunk // wide
    full = lambda shape: pl.BlockSpec(shape, lambda f, at: (0,) * len(shape))
    out_specs = [pl.BlockSpec((pieces, 2, width, wide), lambda f, at: (f, 0, 0, 0))]
    out_shape = [jax.ShapeDtypeStruct((n_dp, 2, width, wide), BF)]
    if not turned:
        out_specs += [full((width, rows))] * 2
        out_shape += [jax.ShapeDtypeStruct((width, rows), BF)] * 2
    made = pl.pallas_call(
        functools.partial(weights_kernel, count=len(acts), pieces=pieces, turned=turned),
        grid_spec=pltpu.PrefetchScalarGridSpec(
            num_scalar_prefetch=1,
            grid=(steps,),
            in_specs=[
                pl.BlockSpec((a.shape[0], chunk), lambda f, at: (0, at[0] * steps + f))
                for a in (*acts, *dhids)
            ]
            + [full(a.shape) for a in sides],
            out_specs=out_specs,
        ),
        out_shape=out_shape,
        compiler_params=pltpu.CompilerParams(vmem_limit_bytes=VMEM_BYTES),
        cost_estimate=estimate(rows * width, rows * width),
        name="weight_grads",
    )(core.astype(jnp.int32)[None], *acts, *dhids, *sides)
    return made[0], made[1:]


def both_weight_grads(group, here, n_ctx, n_dp):
    xs, dps, acts, dhids = zip(*group)
    give, sides = weight_grads(1 - here, acts, dhids, (*xs, *dps), False, n_ctx, n_dp)
    keep, _ = weight_grads(here, acts, dhids, sides, True, n_ctx, n_dp)
    return give, keep


def seats(expert_ids, seat_order, expert_count, capacity, slot_of):
    token_count = expert_ids.shape[0]
    places = jnp.arange(token_count, dtype=jnp.int32)
    earlier = (seat_order[:, None] < seat_order[None, :]) | (
        seat_order[:, None] == seat_order[None, :]
    ) & (places[:, None] < places[None, :])
    earlier = earlier.astype(BF)
    lane_ids = jnp.arange(expert_count, dtype=jnp.int32)
    first_hot = expert_ids[:, 0:1] == lane_ids[None, :]
    second_hot = expert_ids[:, 1:2] == lane_ids[None, :]
    both_hot = jnp.concatenate([first_hot, second_hot], axis=1).astype(BF)
    ahead = jnp.einsum("st,se->te", earlier, both_hot, preferred_element_type=F32)
    ahead_first = ahead[:, :expert_count]
    ahead_second = ahead[:, expert_count:] + jnp.sum(first_hot.astype(F32), axis=0)[None, :]
    rank_first = jnp.sum(jnp.where(first_hot, ahead_first, 0.0), axis=-1)
    rank_second = jnp.sum(jnp.where(second_hot, ahead_second, 0.0), axis=-1)

    def slot(picked, rank):
        at = rank.astype(jnp.int32)
        return jnp.where(at < capacity, slot_of(picked, at), -1)

    return (
        slot(expert_ids[:, 0], rank_first),
        slot(expert_ids[:, 1], rank_second),
        first_hot,
        second_hot,
    )


def three_parts(v):
    high = v.astype(BF)
    rest = v - high.astype(F32)
    mid = rest.astype(BF)
    return high, mid, (rest - mid.astype(F32)).astype(BF)


def seat_rows_kernel(t1, t2, *refs, chosen, parts, cap):
    *gate_refs, rows_ref, out_ref = refs
    peers = out_ref.shape[0]
    tokens = t1.shape[1]
    group = min(peers, max(1, 256 // cap))

    def hot_of(t, part, r):
        ids = lax.broadcasted_iota(jnp.int32, (group * cap, tokens), 0) + (part * peers + r) * cap
        return ids == t[...]

    for n, part in enumerate(chosen):
        for r in range(0, peers, group):
            hot = hot_of(t1, part, r) | hot_of(t2, part, r)
            got = mm(jnp.where(hot, 1.0, 0.0).astype(BF), rows_ref[...]).astype(BF)
            for m in range(group):
                out_ref[r + m, n * cap : (n + 1) * cap, :] = got[m * cap : (m + 1) * cap]
    if gate_refs:
        lefts = [jnp.concatenate(three_parts(g[...]), axis=0) for g in gate_refs]
        for r in range(0, peers, group):
            got = []
            for part in range(parts):
                both = sum(
                    mm(left, jnp.where(hot_of(t, part, r), 1.0, 0.0).astype(BF), NT)
                    for left, t in zip(lefts, (t1, t2))
                )
                got.append(jnp.sum(both, axis=0, keepdims=True))
            for m in range(group):
                put_extra(
                    out_ref, r + m, jnp.concatenate([g[:, m * cap : (m + 1) * cap] for g in got], axis=1)
                )


def seat_rows(t1, t2, rows, gates, chosen, parts, peers, cap):
    tokens, width = rows.shape
    per_peer = len(chosen) * cap + (EXTRA if gates else 0)
    return pl.pallas_call(
        functools.partial(seat_rows_kernel, chosen=chosen, parts=parts, cap=cap),
        out_shape=jax.ShapeDtypeStruct((peers, per_peer, width), BF),
        compiler_params=pltpu.CompilerParams(vmem_limit_bytes=VMEM_BYTES),
        cost_estimate=estimate(2 * peers * per_peer * tokens * width, 4 * tokens * width),
        name="seat_rows",
    )(t1[None], t2[None], *[g[None] for g in gates], rows)


def rows_back(t1, t2, back, extra, split=1):
    tokens = t1.shape[0]
    total, place = None, 0
    firsts = jnp.zeros((tokens, 1), F32)
    seconds = firsts
    peers = back[0].shape[0]
    parts = [(ref, 0, back[0].shape[1]) for ref in back]
    if split > 1:
        cap = back[0].shape[1] // split
        parts = [(back[0], n * cap, cap) for n in range(split)]
    for part, (ref, start, cap) in enumerate(parts):
        group = min(peers, max(1, 512 // cap))
        for b in range(0, peers, group):
            ids = lax.broadcasted_iota(jnp.int32, (tokens, group * cap), 1) + place
            place += group * cap
            first = ids == t1
            second = ids == t2
            hot = jnp.where(first | second, 1.0, 0.0).astype(BF)
            add = mm(hot, jnp.concatenate([ref[b + n, start : start + cap, :] for n in range(group)], axis=0))
            total = add if total is None else total + add
            if extra:
                lanes = slice(part * cap, (part + 1) * cap)
                dg = jnp.concatenate([get_extra(back[-1], b + n, lanes) for n in range(group)], axis=1)
                firsts += jnp.sum(jnp.where(first, dg, 0.0), axis=1, keepdims=True)
                seconds += jnp.sum(jnp.where(second, dg, 0.0), axis=1, keepdims=True)
    return total, firsts, seconds


def unseat_kernel(t1, t2, base, back, out_ref, *, split):
    total, _, _ = rows_back(t1[...], t2[...], [back], False, split)
    out_ref[...] = (base[...] + total).astype(BF)


def unseat(t1, t2, base, back, split, block=256):
    tokens, width = base.shape
    col = pl.BlockSpec((block, 1), lambda i: (i, 0))
    rows = pl.BlockSpec((block, width), lambda i: (i, 0))
    return pl.pallas_call(
        functools.partial(unseat_kernel, split=split),
        grid=(tokens // block,),
        in_specs=[col, col, rows, pl.BlockSpec(back.shape, lambda i: (0, 0, 0))],
        out_specs=rows,
        out_shape=jax.ShapeDtypeStruct((tokens, width), BF),
        compiler_params=pltpu.CompilerParams(vmem_limit_bytes=VMEM_BYTES),
        cost_estimate=estimate(tokens * width, tokens * width),
        name="unseat",
    )(t1[:, None], t2[:, None], base, back)


def route_back_kernel(
    t1, t2, ids, probs, dy, middle, gain, w_router, w_out, *refs,
):
    dmiddle_ref, dbranch_ref, dmixed_ref, small_ref = refs[-4:]
    total, dg1, dg2 = rows_back(t1[...], t2[...], refs[:-4], True)
    p = probs[...]
    experts = p.shape[1]
    lane = lax.broadcasted_iota(jnp.int32, p.shape, 1)
    d_gates = jnp.where(lane == ids[:, 0:1], dg1, 0.0) + jnp.where(lane == ids[:, 1:2], dg2, 0.0)
    d_logits = p * (d_gates - jnp.sum(p * d_gates, axis=1, keepdims=True))
    d_routed = total
    for piece in three_parts(d_logits):
        d_routed = d_routed + mm(piece, w_router[...], NT)
    v = middle[...]
    centred = v - jnp.mean(v, axis=1, keepdims=True)
    inv = lax.rsqrt(jnp.mean(centred * centred, axis=1, keepdims=True) + NORM_EPS)
    unit = centred * inv
    routed = (unit * gain[...]).astype(BF)
    scaled = d_routed * gain[...]
    d_norm = inv * (
        scaled
        - jnp.mean(scaled, axis=1, keepdims=True)
        - unit * jnp.mean(scaled * unit, axis=1, keepdims=True)
    )
    d_middle = dy[...].astype(F32) + d_norm
    d_branch = d_middle.astype(BF)
    dmiddle_ref[...] = d_middle
    dbranch_ref[...] = d_branch
    dmixed_ref[...] = mm(d_branch, w_out[...], NT).astype(BF)
    to_router = 0.0
    for piece in three_parts(d_logits.T):
        to_router = to_router + mm(piece, routed)
    to_gain = jnp.sum(d_routed * unit, axis=0, keepdims=True)

    @pl.when(pl.program_id(0) == 0)
    def _():
        small_ref[...] = jnp.zeros_like(small_ref)

    small_ref[0:experts, :] += to_router
    small_ref[experts : experts + 1, :] += to_gain


def route_back(t1, t2, ids, probs, dy, middle, gain, w_router, w_out, parts, block=256):
    tokens, width = dy.shape
    experts = probs.shape[1]
    line = lambda cols: pl.BlockSpec((block, cols), lambda i: (i, 0))
    full = lambda a: pl.BlockSpec(a.shape, lambda i: (0,) * a.ndim)
    gain = gain[None]
    return pl.pallas_call(
        route_back_kernel,
        grid=(tokens // block,),
        in_specs=[
            line(1), line(1), line(2), line(experts), line(width), line(width),
            full(gain), full(w_router), full(w_out),
        ]
        + [full(part) for part in parts],
        out_specs=[
            line(width), line(width), line(width),
            pl.BlockSpec((experts + 8, width), lambda i: (0, 0)),
        ],
        out_shape=[
            jax.ShapeDtypeStruct((tokens, width), F32),
            jax.ShapeDtypeStruct((tokens, width), BF),
            jax.ShapeDtypeStruct((tokens, width), BF),
            jax.ShapeDtypeStruct((experts + 8, width), F32),
        ],
        compiler_params=pltpu.CompilerParams(vmem_limit_bytes=VMEM_BYTES),
        cost_estimate=estimate(tokens * width, tokens * width),
        name="route_back",
    )(t1[:, None], t2[:, None], ids, probs, dy, middle, gain, w_router, w_out, *parts)


def swap(value):
    n = lax.axis_size("ctx")
    return lax.ppermute(value, "ctx", [(i, (i + 1) % n) for i in range(n)])


def exchange(value, axes):
    return lax.all_to_all(value, axes, 0, 0, tiled=True)


def shift(value, axis, by):
    n = lax.axis_size(axis)
    return lax.ppermute(value, axis, [(i, (i + by) % n) for i in range(n)])


def scatter_begin(value, axis):
    n = lax.axis_size(axis)
    me = lax.axis_index(axis)
    x = value.reshape(n, value.shape[0] // n, value.shape[1])
    pick = lambda at: lax.dynamic_index_in_dim(x, at, 0, keepdims=False)
    return [pick(me)] + [shift(pick(lax.rem(me + s, n)), axis, s) for s in range(1, n)]


def add_up(pieces):
    total = pieces[0].astype(F32)
    for piece in pieces[1:]:
        total = total + piece.astype(F32)
    return total.astype(BF)


def gather_back(x, axis):
    n = lax.axis_size(axis)
    return [x] + [shift(x, axis, s) for s in range(1, n)]


def assemble_kernel(at, w_ref, *refs, groups, spans):
    ins, outs = refs[: 2 * groups], refs[2 * groups :]
    me = at[2]
    owners, rows = ins[0].shape[1], ins[0].shape[2]

    def write(held):
        for z in range(owners):
            back = lax.rem(me + owners - z, owners)
            for ref, span in zip(held, spans):
                piece = ref[0, back].astype(F32)
                for src, which, dst, size in span:
                    outs[which][z * rows : (z + 1) * rows, dst : dst + size] = piece[:, src : src + size]

    is_mine = pl.program_id(0) == at[0]
    pl.when(is_mine)(lambda: write(ins[:groups]))
    pl.when(jnp.logical_not(is_mine))(lambda: write(ins[groups:]))
    outs[-1][...] = jnp.sum(outs[0][...] * w_ref[...].astype(F32), axis=1, keepdims=True)


def assemble(sums, spans, widths, w_qkv):
    n_dp, owners, rows, _ = sums[0][0].shape
    n_ctx = lax.axis_size("ctx")
    block = owners * rows
    height = n_ctx * n_dp * block
    at = jnp.stack([lax.axis_index(axis) for axis in ("ctx", "dp", "expert")]).astype(jnp.int32)

    def back(mine):
        def place(c, d, at):
            edge = jnp.where(c == 0, 0, n_dp - 1)
            return ((at[1] + n_dp - jnp.where((c == at[0]) == mine, d, edge)) % n_dp, 0, 0, 0)

        return place

    line = lambda cols: pl.BlockSpec((block, cols), lambda c, d, at: (c * n_dp + d, 0))
    widths = [*widths, 1]
    return pl.pallas_call(
        functools.partial(assemble_kernel, groups=len(sums), spans=spans),
        grid_spec=pltpu.PrefetchScalarGridSpec(
            num_scalar_prefetch=1,
            grid=(n_ctx, n_dp),
            in_specs=[line(w_qkv.shape[1])]
            + [pl.BlockSpec((1,) + mine.shape[1:], back(True)) for mine, _ in sums]
            + [pl.BlockSpec((1,) + mine.shape[1:], back(False)) for mine, _ in sums],
            out_specs=[line(cols) for cols in widths],
        ),
        out_shape=[jax.ShapeDtypeStruct((height, cols), F32) for cols in widths],
        compiler_params=pltpu.CompilerParams(vmem_limit_bytes=VMEM_BYTES),
        cost_estimate=estimate(height * 2304, 12 * height * 2304),
        name="assemble",
    )(at, w_qkv, *[mine for mine, _ in sums], *[other for _, other in sums])


def spread_kernel(at, *refs):
    *ins, up_ref, down_ref = refs
    j = pl.program_id(0)
    for s, src in enumerate(ins):

        @pl.when(lax.rem(at[0] + len(ins) - s, len(ins)) == j)
        def _():
            up_ref[0] = src[0].astype(F32)
            down_ref[0] = src[1].astype(F32).T


def spread(pieces, place):
    count = len(pieces)
    _, width, cols = pieces[0].shape
    return pl.pallas_call(
        spread_kernel,
        grid_spec=pltpu.PrefetchScalarGridSpec(
            num_scalar_prefetch=1,
            grid=(count,),
            in_specs=[pl.BlockSpec((2, width, cols), lambda j, at: (0, 0, 0))] * count,
            out_specs=[
                pl.BlockSpec((1, width, cols), lambda j, at: (j, 0, 0)),
                pl.BlockSpec((1, cols, width), lambda j, at: (j, 0, 0)),
            ],
        ),
        out_shape=[
            jax.ShapeDtypeStruct((count, width, cols), F32),
            jax.ShapeDtypeStruct((count, cols, width), F32),
        ],
        compiler_params=pltpu.CompilerParams(vmem_limit_bytes=VMEM_BYTES),
        cost_estimate=estimate(width * cols, 12 * count * width * cols),
        name="spread",
    )(place.astype(jnp.int32)[None], *pieces)


def after(value, *others):
    return lax.optimization_barrier((value, others))[0]


def body(
    tokens,
    cotangent,
    router_noise,
    expert_ids,
    seat_order,
    gain_attn,
    w_qkv,
    w_out,
    gain_moe,
    w_router,
    w_up,
    w_down,
):
    image_count, half_len, width = tokens.shape
    rows = image_count * half_len
    expert_count = router_noise.shape[-1]
    n_owner = lax.axis_size("expert")
    n_ctx = lax.axis_size("ctx")
    n_dp = lax.axis_size("dp")
    here = lax.axis_index("ctx")
    my_dp = lax.axis_index("dp")
    held = w_up.shape[0]
    capacity = (2 * rows + expert_count - 1) // expert_count
    one_each = held == n_dp
    if one_each:
        parts, peers, axes = 2, n_owner * n_dp, ("expert", "dp")
        cap = capacity // parts
        slot_of = lambda e, at: (at // cap * peers + e) * cap + at % cap
        which = [my_dp] * parts
    else:
        parts, peers, axes = held // n_ctx, n_owner * n_ctx, ("expert", "ctx")
        cap = capacity
        slot_of = lambda e, at: ((e % parts) * peers + e // parts) * cap + at
        which = [here * parts + part for part in range(parts)]

    t1, t2, first_hot, second_hot = seats(
        expert_ids.reshape(rows, 2), seat_order.reshape(rows), expert_count, capacity, slot_of
    )
    dy_b = cotangent.reshape(rows, width)
    every = tuple(range(parts))
    dy_slots = seat_rows(t1, t2, dy_b, (), every, parts, peers, cap)
    dy_got = exchange(dy_slots, axes)

    tokens_f = after(tokens, dy_slots).reshape(rows, width).astype(F32)
    normed_a, unit_a, inv_a = norm_forward(tokens_f, gain_attn)
    normed_ab = normed_a.astype(BF)
    qkv_b = mm(normed_ab, w_qkv).astype(BF)
    kv_other = swap(qkv_b[:, width:])
    mixed_b, probs, inv_sum = attend(qkv_b, kv_other, rows)

    middle = tokens_f + mm(mixed_b, w_out)
    normed_m, _, _ = norm_forward(middle, gain_moe)
    routed_b = normed_m.astype(BF)
    logits = mm(routed_b, w_router) + router_noise.reshape(rows, expert_count)
    gate_probs = jax.nn.softmax(logits, axis=-1)
    gate_first = jnp.sum(jnp.where(first_hot, gate_probs, 0.0), axis=-1)
    gate_second = jnp.sum(jnp.where(second_hot, gate_probs, 0.0), axis=-1)

    sent = [
        seat_rows(
            t1, t2, routed_b, () if part else (gate_first, gate_second), (part,), parts, peers, cap
        )
        for part in every
    ]
    sent[0], dy_got = lax.optimization_barrier((sent[0], dy_got))
    x_got = [exchange(sent[0], axes)]
    outs, dx_back, dgates, kept = None, [], [], []
    for part in every:
        last = part == parts - 1
        x = x_got[part]
        if not last:
            x, following = lax.optimization_barrier((x, sent[part + 1]))
            x_got.append(exchange(following, axes))
        outs, dx, act, dhid, dp, *dg = run_expert(
            which[part].astype(jnp.int32)[None], part, parts, x, x_got[0], dy_got, outs, dgates, w_up, w_down
        )
        dgates += dg
        if not last:
            dx, x_got[-1] = lax.optimization_barrier((dx, x_got[-1]))
        if dx_back:
            dx, dx_back[-1], act = lax.optimization_barrier((dx, dx_back[-1], act))
        dx_back.append(exchange(dx, axes))
        kept.append((x_got[part], dp, act, dhid))
    if one_each:
        give, keep = both_weight_grads(kept, here, n_ctx, n_dp)
        dx_back, give, keep = lax.optimization_barrier((dx_back, give, keep))
        other = swap(give)
    else:
        mine, far = [], []
        for group in kept:
            give, keep = (
                lax.psum_scatter(
                    g.reshape(-1, g.shape[-1]), "dp", scatter_dimension=0, tiled=True
                ).reshape(g.shape[1:])
                for g in both_weight_grads([group], here, n_ctx, n_dp)
            )
            mine.append(keep)
            far.append(swap(give))
        pieces = [
            jnp.where(here == n // parts, mine[n % parts], far[n % parts]) for n in reversed(range(held))
        ]
    outs, dx_back = lax.optimization_barrier((outs, dx_back))
    returned = exchange(outs, axes)
    if one_each:
        blocks = []
        for n in range(n_dp):
            pick = lambda v: lax.dynamic_index_in_dim(v, lax.rem(my_dp + n, n_dp), 0, keepdims=False)
            blocks.append(add_up([pick(keep), pick(other)]))
        dx_back, blocks = lax.optimization_barrier((dx_back, blocks))
        pieces = [block if n == 0 else shift(block, "dp", n) for n, block in enumerate(blocks)]

    d_middle, d_branch_b, d_mixed_b, small = route_back(
        t1, t2, expert_ids.reshape(rows, 2), gate_probs, dy_b, middle, gain_moe, w_router, w_out, dx_back
    )

    pairs = width // 128
    calls = [(first, pairs // 3) for first in range(0, pairs, pairs // 3)]

    def call(n, grad):
        return attend_back(qkv_b, kv_other, mixed_b, grad, inv_sum, probs, rows, *calls[n])

    dq0, own0, far0 = call(0, d_mixed_b)
    dq1, own1, far1 = call(1, after(d_mixed_b, dq0))
    fars = [swap(far0), swap(far1)]
    result = unseat(t1, t2, after(middle, dq1), returned, parts)
    fars, pieces, result = lax.optimization_barrier((fars, pieces, result))
    grad_a, d_qkv_a = grad_qkv(
        normed_ab, [dq0, dq1], [own0, own1], fars, (mixed_b, d_branch_b, small)
    )
    sum_a = add_up(grad_a)
    d_mixed_b, sum_a = lax.optimization_barrier((d_mixed_b, sum_a))
    got_a = scatter_begin(sum_a, "dp")
    dq2, own2, far2 = call(2, d_mixed_b)
    got_a, dq2, own2, far2 = lax.optimization_barrier((got_a, dq2, own2, far2))
    got_a = scatter_begin(add_up(got_a), "expert")
    far2 = swap(far2)
    got_b, d_qkv_b = grad_qkv(normed_ab, [dq2], [own2], [far2])
    got_a, got_b[0] = lax.optimization_barrier((got_a, got_b[0]))
    got_a = gather_back(add_up(got_a), "expert")
    got_b = scatter_begin(add_up(got_b), "dp")
    got_a, got_b[0] = lax.optimization_barrier((got_a, got_b[0]))
    got_a = gather_back(jnp.stack(got_a), "dp")
    got_b, got_a[0] = lax.optimization_barrier((got_b, got_a[0]))
    got_b = scatter_begin(add_up(got_b), "expert")
    grad_up, grad_down = spread(after(pieces, got_a[0]), my_dp if one_each else jnp.int32(held - 1))
    got_b, grad_up = lax.optimization_barrier((got_b, grad_up))
    got_b = gather_back(add_up(got_b), "expert")
    got_b = gather_back(jnp.stack(got_b), "dp")
    got_a, got_b[0] = lax.optimization_barrier((got_a, got_b[0]))
    all_a = jnp.stack(got_a)
    all_a = (all_a, swap(all_a))

    d_normed_a = 0.0
    for first, d_qkv in ((0, d_qkv_a), (calls[2][0], after(d_qkv_b, all_a[0]))):
        start, wide = 128 * first, d_qkv.shape[1] // 3
        columns = [w_qkv[:, m * width + start : m * width + start + wide] for m in range(3)]
        d_normed_a = d_normed_a + mm(d_qkv, jnp.concatenate(columns, axis=1), NT)
    d_tokens_norm, _ = norm_backward(d_normed_a, unit_a, inv_a, gain_attn)
    d_tokens = d_middle + d_tokens_norm
    d_tokens, got_b = lax.optimization_barrier((d_tokens, got_b))

    all_b = jnp.stack(got_b)
    all_b = (all_b, swap(all_b))
    cols_a, cols_b, start_b = d_qkv_a.shape[1], d_qkv_b.shape[1], 128 * calls[2][0]
    spans = [
        [(m * cols_a // 3, 0, m * width, cols_a // 3) for m in range(3)]
        + [(cols_a, 1, 0, width), (cols_a + width, 2, 0, SMALL)],
        [(m * cols_b // 3, 0, m * width + start_b, cols_b // 3) for m in range(3)],
    ]
    grad_w_qkv, grad_w_out, small_sum, gain_sum = assemble(
        [all_a, all_b], spans, (3 * width, width, SMALL), w_qkv
    )
    n_small = small.shape[0]
    small_sum = small_sum[:, :n_small] + small_sum[:, n_small : 2 * n_small]
    return (
        result.reshape(image_count, half_len, width),
        d_tokens.reshape(image_count, half_len, width),
        gain_sum[:, 0] / gain_attn,
        grad_w_qkv,
        grad_w_out,
        small_sum[:, expert_count],
        small_sum[:, :expert_count],
        grad_up,
        grad_down,
    )


def solution(mesh):
    placed = (
        P(("expert", "dp"), "ctx", None),
        P(("expert", "dp"), "ctx", None),
        P(("expert", "dp"), "ctx", None),
        P(("expert", "dp"), "ctx", None),
        P(("expert", "dp"), "ctx"),
        P(),
        P(),
        P(),
        P(),
        P(),
        P("expert", None, None),
        P("expert", None, None),
    )
    return jax.shard_map(
        body,
        mesh=mesh,
        in_specs=placed,
        out_specs=(
            P(("expert", "dp"), "ctx", None),
            P(("expert", "dp"), "ctx", None),
            P(),
            P(),
            P(),
            P(),
            P(),
            P("expert", None, ("ctx", "dp")),
            P("expert", ("ctx", "dp"), None),
        ),
        check_vma=False,
    )
```

```python
import functools
import math

import jax
import jax.numpy as jnp
from jax import lax
from jax.experimental import pallas as pl
from jax.experimental.pallas import tpu as pltpu
from jax.sharding import PartitionSpec as P

HEADS = 12
NORM_EPS = 1e-06
BF = jnp.bfloat16
F32 = jnp.float32
NN = (((1,), (0,)), ((), ()))
NT = (((1,), (1,)), ((), ()))
VMEM_BYTES = 60 << 20
EXTRA = 8
SMALL = 128
SAFE = 40.0


def estimate(flops, moved, slow=0):
    return pl.CostEstimate(flops=flops // 4, bytes_accessed=moved // 4, transcendentals=slow // 4)


def mm(left, right, dims=NN):
    return lax.dot_general(left, right, dims, preferred_element_type=F32)


def norm_forward(values_in, gain_vec):
    centre_mean = jnp.mean(values_in, axis=-1, keepdims=True)
    centred = values_in - centre_mean
    inv_scale = lax.rsqrt(jnp.mean(centred * centred, axis=-1, keepdims=True) + NORM_EPS)
    unit_rows = centred * inv_scale
    return (unit_rows * gain_vec, unit_rows, inv_scale)


def norm_backward(gradient, unit_rows, inv_scale, gain_vec):
    scaled = gradient * gain_vec
    inner_sum = (
        scaled
        - jnp.mean(scaled, axis=-1, keepdims=True)
        - unit_rows * jnp.mean(scaled * unit_rows, axis=-1, keepdims=True)
    )
    return (inner_sum * inv_scale, jnp.sum(gradient * unit_rows, axis=0))


def project_kernel(x_ref, gain, w_ref, normed_ref, q_ref, kv_ref):
    width = x_ref.shape[1]
    normed = norm_forward(x_ref[...].astype(F32), gain[...])[0].astype(BF)
    normed_ref[...] = normed
    out = mm(normed, w_ref[...]).astype(BF)
    q_ref[...] = out[:, 0:width]
    kv_ref[...] = out[:, width:]


def project(x, gain, w_qkv, block=256):
    rows, width = x.shape
    line = lambda cols: pl.BlockSpec((block, cols), lambda i: (i, 0))
    return pl.pallas_call(
        project_kernel,
        grid=(rows // block,),
        in_specs=[
            line(width),
            pl.BlockSpec((1, width), lambda i: (0, 0)),
            pl.BlockSpec(w_qkv.shape, lambda i: (0, 0)),
        ],
        out_specs=[line(width), line(width), line(2 * width)],
        out_shape=[jax.ShapeDtypeStruct((rows, n * width), BF) for n in (1, 1, 2)],
        compiler_params=pltpu.CompilerParams(vmem_limit_bytes=VMEM_BYTES),
        cost_estimate=estimate(6 * rows * width * width, 20 * rows * width),
        name="project",
    )(x, gain[None], w_qkv)


def attend_kernel(q_ref, k0, k1, v0, v1, o_ref, p_ref, li_ref, vext, ksize, *, scale):
    half = k0.shape[0]

    def largest(v):
        same = lax.broadcasted_iota(jnp.int32, (128, 128), 0) // 64 == (
            lax.broadcasted_iota(jnp.int32, (128, 128), 1) // 64
        )
        squares = (v.astype(F32) * v.astype(F32)).astype(BF)
        return 1.01 * jnp.max(mm(squares, same.astype(BF)), axis=0, keepdims=True)

    @pl.when(pl.program_id(1) == 0)
    def _():
        ones = jnp.ones((half, 128), BF)
        vext[0:half, 0:128] = v0[...]
        vext[half:, 0:128] = v1[...]
        vext[0:half, 128:256] = ones
        vext[half:, 128:256] = ones
        ksize[...] = jnp.maximum(largest(k0[...]), largest(k1[...]))

    low = lax.broadcasted_iota(jnp.int32, q_ref.shape, 1) < 64
    q = q_ref[...]
    factor = scale * math.log2(math.e)
    small = jnp.max(largest(q) * ksize[...]) * (factor * factor) < SAFE * SAFE

    def run(shifted):
        outs, sums = [], []
        for h in range(2):
            picked = jnp.where(low if h == 0 else jnp.logical_not(low), q, jnp.zeros_like(q))
            s0 = mm(picked, k0[...], NT) * factor
            s1 = mm(picked, k1[...], NT) * factor
            if shifted:
                peak = jnp.maximum(
                    jnp.max(s0, axis=1, keepdims=True), jnp.max(s1, axis=1, keepdims=True)
                )
                s0 = s0 - peak
                s1 = s1 - peak
            p_ref[h, :, 0:half] = jnp.exp2(s0).astype(BF)
            p_ref[h, :, half:] = jnp.exp2(s1).astype(BF)
            both = mm(p_ref[h], vext[...])
            outs.append(both[:, 0:128])
            sums.append(both[:, 128:256])
        inv = 1.0 / jnp.where(low, sums[0], sums[1])
        o_ref[...] = (jnp.where(low, outs[0], outs[1]) * inv).astype(BF)
        li_ref[...] = inv

    pl.when(small)(lambda: run(False))
    pl.when(jnp.logical_not(small))(lambda: run(True))


def attend(q, kv, kv_other, block):
    rows, width = q.shape
    pairs = width // 128
    tile = pl.BlockSpec((block, 128), lambda h, i: (i, h))
    return pl.pallas_call(
        functools.partial(attend_kernel, scale=1.0 / math.sqrt(width // HEADS)),
        grid=(pairs, rows // block),
        in_specs=[
            tile,
            pl.BlockSpec((rows, 128), lambda h, i: (0, h)),
            pl.BlockSpec((rows, 128), lambda h, i: (0, h)),
            pl.BlockSpec((rows, 128), lambda h, i: (0, pairs + h)),
            pl.BlockSpec((rows, 128), lambda h, i: (0, pairs + h)),
        ],
        out_specs=[tile, pl.BlockSpec((2, block, 2 * rows), lambda h, i: (h, i, 0)), tile],
        out_shape=[
            jax.ShapeDtypeStruct((rows, width), BF),
            jax.ShapeDtypeStruct((HEADS, rows, 2 * rows), BF),
            jax.ShapeDtypeStruct((rows, width), F32),
        ],
        scratch_shapes=[pltpu.VMEM((2 * rows, 256), BF), pltpu.VMEM((1, 128), F32)],
        compiler_params=pltpu.CompilerParams(vmem_limit_bytes=VMEM_BYTES),
        cost_estimate=estimate(rows * width, rows * width),
        name="attend",
    )(q, kv, kv_other, kv, kv_other)


def attend_back_kernel(
    q_ref, k0, k1, v0, v1, o_ref, g_ref, li_ref, p_ref,
    dq_ref, own_ref, far_ref, vext, kacc, vacc, *, scale, steps,
):
    i = pl.program_id(1)
    half = k0.shape[0]
    lane = lax.broadcasted_iota(jnp.int32, q_ref.shape, 1)
    low = lane < 64

    @pl.when(i == 0)
    def _():
        ones = jnp.where(lax.broadcasted_iota(jnp.int32, (half, 128), 1) < 2, 1.0, 0.0).astype(BF)
        vext[0:half, 0:128] = v0[...]
        vext[half:, 0:128] = v1[...]
        vext[0:half, 128:256] = ones
        vext[half:, 128:256] = ones

    g = g_ref[...].astype(F32) * li_ref[...]
    gb = g.astype(BF)
    go = g * o_ref[...].astype(F32)
    qt = q_ref[...].T
    gt = gb.T
    dqs = []
    for h in range(2):
        mine = low if h == 0 else jnp.logical_not(low)
        delta = -jnp.sum(jnp.where(mine, go, 0.0), axis=1, keepdims=True)
        high = delta.astype(BF).astype(F32)
        extra = jnp.where(lane == 0, high, jnp.where(lane == 1, delta - high, 0.0)).astype(BF)
        gext = jnp.concatenate([jnp.where(mine, gb, jnp.zeros_like(gb)), extra], axis=1)
        p = p_ref[h]
        ds = (p.astype(F32) * mm(gext, vext[...], NT)).astype(BF)
        dqs.append(mm(ds[:, 0:half], k0[...]) + mm(ds[:, half:], k1[...]))
        rows = slice(64 * h, 64 * h + 64)
        dk = mm(qt[rows], ds)
        dv = mm(gt[rows], p)

        @pl.when(i == 0)
        def _():
            kacc[rows] = dk
            vacc[rows] = dv

        @pl.when(i > 0)
        def _():
            kacc[rows] += dk
            vacc[rows] += dv

    dq_ref[...] = (jnp.where(low, dqs[0], dqs[1]) * scale).astype(BF)

    @pl.when(i == steps - 1)
    def _():
        own_ref[0] = kacc[:, 0:half].T * scale
        own_ref[1] = vacc[:, 0:half].T
        far_ref[0] = (kacc[:, half:].T * scale).astype(BF)
        far_ref[1] = vacc[:, half:].T.astype(BF)


def attend_back(q, kv, kv_other, mixed, grad, inv_sum, probs, block, first, count):
    rows, width = q.shape
    pairs = width // 128
    steps = rows // block
    tile = pl.BlockSpec((block, 128), lambda h, i: (i, first + h))
    both = pl.BlockSpec((2, rows, 128), lambda h, i: (0, 0, h))
    return pl.pallas_call(
        functools.partial(attend_back_kernel, scale=1.0 / math.sqrt(width // HEADS), steps=steps),
        grid=(count, steps),
        in_specs=[
            tile,
            pl.BlockSpec((rows, 128), lambda h, i: (0, first + h)),
            pl.BlockSpec((rows, 128), lambda h, i: (0, first + h)),
            pl.BlockSpec((rows, 128), lambda h, i: (0, pairs + first + h)),
            pl.BlockSpec((rows, 128), lambda h, i: (0, pairs + first + h)),
            tile,
            tile,
            tile,
            pl.BlockSpec((2, block, 2 * rows), lambda h, i: (first + h, i, 0)),
        ],
        out_specs=[pl.BlockSpec((block, 128), lambda h, i: (i, h)), both, both],
        out_shape=[
            jax.ShapeDtypeStruct((rows, 128 * count), BF),
            jax.ShapeDtypeStruct((2, rows, 128 * count), F32),
            jax.ShapeDtypeStruct((2, rows, 128 * count), BF),
        ],
        scratch_shapes=[
            pltpu.VMEM((2 * rows, 256), BF),
            pltpu.VMEM((128, 2 * rows), F32),
            pltpu.VMEM((128, 2 * rows), F32),
        ],
        compiler_params=pltpu.CompilerParams(vmem_limit_bytes=VMEM_BYTES),
        cost_estimate=estimate(rows * width, rows * width),
        name="attend_back",
    )(q, kv, kv_other, kv, kv_other, mixed, grad, inv_sum, probs)


def grad_qkv_kernel(core, normed, *refs, count, with_out):
    if count:
        grad_ref, dqkv_ref = refs[-2:]
        cols = dqkv_ref.shape[1]
        wide = cols // 3
        at = 0
        for n in range(count):
            dq, own, far = refs[n], refs[count + n], refs[2 * count + n]
            size = dq.shape[1]
            dqkv_ref[:, at : at + size] = dq[...]
            for m in range(2):
                start = (m + 1) * wide + at
                dqkv_ref[:, start : start + size] = (own[m] + far[m].astype(F32)).astype(BF)
            at += size
        more = refs[3 * count :]
    else:
        dqkv_ref, grad_ref = refs[0], refs[-1]
        cols = dqkv_ref.shape[1]
        more = refs[1:]
    grad_ref[:, 0:cols] = mm(normed[...].T, dqkv_ref[...]).astype(BF)
    if with_out:
        mixed, branch, small = more[:3]
        width = branch.shape[1]
        grad_ref[:, cols : cols + width] = mm(mixed[...].T, branch[...]).astype(BF)
        value = small[...]
        high = value.astype(BF).astype(F32)
        rest = jnp.zeros((SMALL - 2 * value.shape[0], value.shape[1]), F32)
        grad_ref[:, cols + width :] = jnp.concatenate([high, value - high, rest], axis=0).T.astype(BF)


def grad_qkv_part(core, normed, sides, count, more, half):
    rows, width = normed.shape
    cols = sum(side.shape[-1] for side in sides[:count]) * 3 if count else sides[0].shape[1]
    out_cols = cols + (more[1].shape[1] + SMALL if more else 0)
    full = lambda a: pl.BlockSpec(a.shape, lambda i, core: (0,) * a.ndim)
    part = lambda a: pl.BlockSpec((a.shape[0], half), lambda i, core: (0, core[0]))
    out_specs = [pl.BlockSpec((half, out_cols), lambda i, core: (0, 0))]
    out_shape = [jax.ShapeDtypeStruct((half, out_cols), BF)]
    if count:
        out_specs.append(pl.BlockSpec((rows, cols), lambda i, core: (0, 0)))
        out_shape.append(jax.ShapeDtypeStruct((rows, cols), BF))
    return pl.pallas_call(
        functools.partial(grad_qkv_kernel, count=count, with_out=bool(more)),
        grid_spec=pltpu.PrefetchScalarGridSpec(
            num_scalar_prefetch=1,
            grid=(1,),
            in_specs=[part(normed)]
            + [full(side) for side in sides]
            + ([part(more[0]), full(more[1]), part(more[2])] if more else []),
            out_specs=out_specs,
        ),
        out_shape=out_shape,
        compiler_params=pltpu.CompilerParams(vmem_limit_bytes=VMEM_BYTES),
        cost_estimate=estimate(rows * width, rows * width),
        name="grad_qkv",
    )(core.astype(jnp.int32)[None], normed, *sides, *more)


def grad_qkv(normed, dqs, owns, fars, more=()):
    return grad_qkv_part(jnp.int32(0), normed, (*dqs, *owns, *fars), len(dqs), more, normed.shape[1])


def grad_qkv_halves(normed, dqs, owns, fars):
    here = lax.axis_index("ctx")
    half = normed.shape[1] // 2
    give, d_qkv = grad_qkv_part(1 - here, normed, (*dqs, *owns, *fars), len(dqs), (), half)
    other = swap(give)
    (keep,) = grad_qkv_part(here, normed, (d_qkv,), 0, (), half)
    return [keep, other], d_qkv


GELU_A = math.sqrt(2.0 / math.pi)
GELU_B = 0.044715


def gelu_both(v):
    square = v * v
    t = jnp.tanh(v * (GELU_A + GELU_A * GELU_B * square))
    half = 0.5 + 0.5 * t
    slope = half + (0.5 * v) * (1.0 - t * t) * (GELU_A + 3 * GELU_A * GELU_B * square)
    return v * half, slope


def put_extra(ref, r, row):
    width = ref.shape[2]
    cap = row.shape[1]
    line = lax.broadcasted_iota(jnp.int32, (EXTRA, cap), 0)
    full = jnp.zeros((EXTRA, cap), F32)
    for n, piece in enumerate(three_parts(row)):
        full = jnp.where(line == n, piece.astype(F32), full)
    full = jnp.concatenate([full, jnp.zeros((EXTRA, width - cap), F32)], axis=1)
    ref[r, ref.shape[1] - EXTRA :, :] = full.astype(BF)


def get_extra(ref, r, lanes):
    sent = ref[r, ref.shape[1] - EXTRA :, lanes].astype(F32)
    return sent[0:1] + sent[1:2] + sent[2:3]


def expert_kernel(which, x_in, gate_in, dy_in, *refs, part, parts, steps, first):
    last = part == parts - 1
    if not first:
        refs = refs[1:]
    dg_in = ()
    if last:
        dg_in, refs = refs[: parts - 1], refs[parts - 1 :]
    up_ref, down_ref, out_ref, dx_ref, act_ref, dhid_ref, dp_ref, *refs = refs
    if not last:
        dg_out, refs = refs[0], refs[1:]
    x, gate, out_acc, dx_acc = refs
    f = pl.program_id(0)
    peers, cap = dy_in.shape[0], dy_in.shape[1]

    @pl.when(f == 0)
    def _():
        lanes = slice(part * cap, (part + 1) * cap)
        gates = jnp.concatenate([get_extra(gate_in, r, lanes) for r in range(peers)], axis=0).T
        for r in range(peers):
            at = slice(r * cap, (r + 1) * cap)
            x[at] = x_in[r, 0:cap, :]
            g = gates[:, r : r + 1]
            gate[at] = g
            dp_ref[at] = (dy_in[r].astype(F32) * g).astype(BF)

    up = up_ref[0]
    down = down_ref[0]
    value, slope = gelu_both(mm(x[...], up))
    act_ref[...] = value.astype(BF)
    dhid_ref[...] = (mm(dp_ref[...], down, NT) * slope).astype(BF)

    @pl.when(f == 0)
    def _():
        dx_acc[...] = mm(dhid_ref[...], up, NT)
        out_acc[...] = mm(act_ref[...], down)

    @pl.when(f > 0)
    def _():
        dx_acc[...] += mm(dhid_ref[...], up, NT)
        out_acc[...] += mm(act_ref[...], down)

    @pl.when(f == steps - 1)
    def _():
        sums = []
        for r in range(peers):
            at = slice(r * cap, (r + 1) * cap)
            produced = out_acc[at].astype(BF).astype(F32)
            dx_ref[r, 0:cap, :] = dx_acc[at].astype(BF)
            out_ref[r] = (produced * gate[at]).astype(BF)
            sums.append(jnp.sum(produced * dy_in[r].astype(F32), axis=1, keepdims=True))
        sums = jnp.concatenate(sums, axis=1).T
        if last:
            full = jnp.concatenate([ref[...] for ref in dg_in] + [sums], axis=1)
            for r in range(peers):
                put_extra(dx_ref, r, full[r : r + 1])
        else:
            dg_out[...] = sums


def run_expert(which, part, parts, x, first_x, dy, outs, dgates, w_up, w_down, chunk=768):
    peers, width = x.shape[0], x.shape[2]
    cap = dy.shape[1] // parts
    rows = peers * cap
    hidden = w_up.shape[-1]
    last = part == parts - 1
    full = lambda shape: pl.BlockSpec(shape, lambda f, j: (0,) * len(shape))
    wide = pl.BlockSpec((rows, chunk), lambda f, j: (0, f))
    dx_shape = (peers, cap + (EXTRA if last else 0), width)
    extra_at = (first_x.shape[1] - EXTRA) // EXTRA
    out_specs = [
        pl.BlockSpec((peers, cap, width), lambda f, j: (0, part, 0)),
        full(dx_shape), wide, wide, full((rows, width)),
    ]
    out_shape = [
        jax.ShapeDtypeStruct(dy.shape, BF),
        jax.ShapeDtypeStruct(dx_shape, BF),
        jax.ShapeDtypeStruct((rows, hidden), BF),
        jax.ShapeDtypeStruct((rows, hidden), BF),
        jax.ShapeDtypeStruct((rows, width), BF),
    ]
    if not last:
        out_specs.append(full((peers, cap)))
        out_shape.append(jax.ShapeDtypeStruct((peers, cap), F32))
        dgates = []
    return pl.pallas_call(
        functools.partial(
            expert_kernel, part=part, parts=parts, steps=hidden // chunk, first=outs is None
        ),
        grid_spec=pltpu.PrefetchScalarGridSpec(
            num_scalar_prefetch=1,
            grid=(hidden // chunk,),
            in_specs=[
                full(x.shape),
                pl.BlockSpec((peers, EXTRA, width), lambda f, j: (0, extra_at, 0)),
                pl.BlockSpec((peers, cap, width), lambda f, j: (0, part, 0)),
                *[pl.BlockSpec(memory_space=pl.ANY)] * (outs is not None),
                *[full(d.shape) for d in dgates],
                pl.BlockSpec((1, width, chunk), lambda f, j: (j[0], 0, f)),
                pl.BlockSpec((1, chunk, width), lambda f, j: (j[0], f, 0)),
            ],
            out_specs=out_specs,
            scratch_shapes=[
                pltpu.VMEM((rows, width), BF),
                pltpu.VMEM((rows, 1), F32),
                pltpu.VMEM((rows, width), F32),
                pltpu.VMEM((rows, width), F32),
            ],
        ),
        out_shape=out_shape,
        compiler_params=pltpu.CompilerParams(vmem_limit_bytes=VMEM_BYTES),
        cost_estimate=estimate(8 * rows * width * hidden, 4 * width * hidden, rows * hidden),
        input_output_aliases={} if outs is None else {4: 0},
        name="expert",
    )(which, x, first_x, dy, *([] if outs is None else [outs]), *dgates, w_up, w_down)


def weights_kernel(at, *refs, count, pieces, turned):
    acts, dhids, refs = refs[:count], refs[count : 2 * count], refs[2 * count :]
    if turned:
        xt, dpt, out_ref = refs
    else:
        xs, dps, (out_ref, xt, dpt) = refs[:count], refs[count : 2 * count], refs[2 * count :]

        @pl.when(pl.program_id(0) == 0)
        def _():
            place = 0
            for x, dp in zip(xs, dps):
                rows = dp.shape[0]
                cap = rows // x.shape[0]
                held = jnp.concatenate([x[r, 0:cap, :] for r in range(x.shape[0])], axis=0)
                xt[:, place : place + rows] = held.T
                dpt[:, place : place + rows] = dp[...].T
                place += rows

    def product(left, rights):
        total, place = None, 0
        for right in rights:
            rows = right.shape[0]
            add = mm(left[:, place : place + rows], right[...])
            total = add if total is None else total + add
            place += rows
        return total.astype(BF)

    gup = product(xt, dhids)
    gdown = product(dpt, acts)
    wide = gup.shape[1] // pieces
    for s in range(pieces):
        out_ref[s, 0] = gup[:, s * wide : (s + 1) * wide]
        out_ref[s, 1] = gdown[:, s * wide : (s + 1) * wide]


def weight_grads(core, acts, dhids, sides, turned, n_ctx, n_dp, chunk=768):
    width, hidden = (sides[0].shape[0] if turned else sides[0].shape[2]), acts[0].shape[1]
    rows = sum(a.shape[0] for a in acts)
    half = hidden // n_ctx
    steps = half // chunk
    wide = half // n_dp
    pieces = chunk // wide
    full = lambda shape: pl.BlockSpec(shape, lambda f, at: (0,) * len(shape))
    out_specs = [pl.BlockSpec((pieces, 2, width, wide), lambda f, at: (f, 0, 0, 0))]
    out_shape = [jax.ShapeDtypeStruct((n_dp, 2, width, wide), BF)]
    if not turned:
        out_specs += [full((width, rows))] * 2
        out_shape += [jax.ShapeDtypeStruct((width, rows), BF)] * 2
    made = pl.pallas_call(
        functools.partial(weights_kernel, count=len(acts), pieces=pieces, turned=turned),
        grid_spec=pltpu.PrefetchScalarGridSpec(
            num_scalar_prefetch=1,
            grid=(steps,),
            in_specs=[
                pl.BlockSpec((a.shape[0], chunk), lambda f, at: (0, at[0] * steps + f))
                for a in (*acts, *dhids)
            ]
            + [full(a.shape) for a in sides],
            out_specs=out_specs,
        ),
        out_shape=out_shape,
        compiler_params=pltpu.CompilerParams(vmem_limit_bytes=VMEM_BYTES),
        cost_estimate=estimate(rows * width, rows * width),
        name="weight_grads",
    )(core.astype(jnp.int32)[None], *acts, *dhids, *sides)
    return made[0], made[1:]


def both_weight_grads(group, here, n_ctx, n_dp):
    xs, dps, acts, dhids = zip(*group)
    give, sides = weight_grads(1 - here, acts, dhids, (*xs, *dps), False, n_ctx, n_dp)
    keep, _ = weight_grads(here, acts, dhids, sides, True, n_ctx, n_dp)
    return give, keep


def seats(expert_ids, seat_order, expert_count, capacity, slot_of):
    token_count = expert_ids.shape[0]
    places = jnp.arange(token_count, dtype=jnp.int32)
    earlier = (seat_order[:, None] < seat_order[None, :]) | (
        seat_order[:, None] == seat_order[None, :]
    ) & (places[:, None] < places[None, :])
    earlier = earlier.astype(BF)
    lane_ids = jnp.arange(expert_count, dtype=jnp.int32)
    first_hot = expert_ids[:, 0:1] == lane_ids[None, :]
    second_hot = expert_ids[:, 1:2] == lane_ids[None, :]
    both_hot = jnp.concatenate([first_hot, second_hot], axis=1).astype(BF)
    ahead = jnp.einsum("st,se->te", earlier, both_hot, preferred_element_type=F32)
    ahead_first = ahead[:, :expert_count]
    ahead_second = ahead[:, expert_count:] + jnp.sum(first_hot.astype(F32), axis=0)[None, :]
    rank_first = jnp.sum(jnp.where(first_hot, ahead_first, 0.0), axis=-1)
    rank_second = jnp.sum(jnp.where(second_hot, ahead_second, 0.0), axis=-1)

    def slot(picked, rank):
        at = rank.astype(jnp.int32)
        return jnp.where(at < capacity, slot_of(picked, at), -1)

    return (
        slot(expert_ids[:, 0], rank_first),
        slot(expert_ids[:, 1], rank_second),
        first_hot,
        second_hot,
    )


def three_parts(v):
    high = v.astype(BF)
    rest = v - high.astype(F32)
    mid = rest.astype(BF)
    return high, mid, (rest - mid.astype(F32)).astype(BF)


def seat_rows_kernel(t1, t2, *refs, chosen, parts, cap):
    *gate_refs, rows_ref, out_ref = refs
    peers = out_ref.shape[0]
    tokens = t1.shape[1]
    group = min(peers, max(1, 256 // cap))

    def hot_of(t, part, r):
        ids = lax.broadcasted_iota(jnp.int32, (group * cap, tokens), 0) + (part * peers + r) * cap
        return ids == t[...]

    for n, part in enumerate(chosen):
        for r in range(0, peers, group):
            hot = hot_of(t1, part, r) | hot_of(t2, part, r)
            got = mm(jnp.where(hot, 1.0, 0.0).astype(BF), rows_ref[...]).astype(BF)
            for m in range(group):
                out_ref[r + m, n * cap : (n + 1) * cap, :] = got[m * cap : (m + 1) * cap]
    if gate_refs:
        lefts = [jnp.concatenate(three_parts(g[...]), axis=0) for g in gate_refs]
        for r in range(0, peers, group):
            got = []
            for part in range(parts):
                both = sum(
                    mm(left, jnp.where(hot_of(t, part, r), 1.0, 0.0).astype(BF), NT)
                    for left, t in zip(lefts, (t1, t2))
                )
                got.append(jnp.sum(both, axis=0, keepdims=True))
            for m in range(group):
                put_extra(
                    out_ref, r + m, jnp.concatenate([g[:, m * cap : (m + 1) * cap] for g in got], axis=1)
                )


def seat_rows(t1, t2, rows, gates, chosen, parts, peers, cap):
    tokens, width = rows.shape
    per_peer = len(chosen) * cap + (EXTRA if gates else 0)
    return pl.pallas_call(
        functools.partial(seat_rows_kernel, chosen=chosen, parts=parts, cap=cap),
        out_shape=jax.ShapeDtypeStruct((peers, per_peer, width), BF),
        compiler_params=pltpu.CompilerParams(vmem_limit_bytes=VMEM_BYTES),
        cost_estimate=estimate(2 * peers * per_peer * tokens * width, 4 * tokens * width),
        name="seat_rows",
    )(t1[None], t2[None], *[g[None] for g in gates], rows)


def rows_back(t1, t2, back, extra, split=1):
    tokens = t1.shape[0]
    total, place = None, 0
    firsts = jnp.zeros((tokens, 1), F32)
    seconds = firsts
    peers = back[0].shape[0]
    parts = [(ref, 0, back[0].shape[1]) for ref in back]
    if split > 1:
        cap = back[0].shape[1] // split
        parts = [(back[0], n * cap, cap) for n in range(split)]
    for part, (ref, start, cap) in enumerate(parts):
        group = min(peers, max(1, 512 // cap))
        for b in range(0, peers, group):
            ids = lax.broadcasted_iota(jnp.int32, (tokens, group * cap), 1) + place
            place += group * cap
            first = ids == t1
            second = ids == t2
            hot = jnp.where(first | second, 1.0, 0.0).astype(BF)
            add = mm(hot, jnp.concatenate([ref[b + n, start : start + cap, :] for n in range(group)], axis=0))
            total = add if total is None else total + add
            if extra:
                lanes = slice(part * cap, (part + 1) * cap)
                dg = jnp.concatenate([get_extra(back[-1], b + n, lanes) for n in range(group)], axis=1)
                firsts += jnp.sum(jnp.where(first, dg, 0.0), axis=1, keepdims=True)
                seconds += jnp.sum(jnp.where(second, dg, 0.0), axis=1, keepdims=True)
    return total, firsts, seconds


def unseat_kernel(t1, t2, base, back, out_ref, *, split, sub):
    for r in range(0, t1.shape[0], sub):
        at = slice(r, r + sub)
        total, _, _ = rows_back(t1[at], t2[at], [back], False, split)
        out_ref[at] = (base[at] + total).astype(BF)


def unseat(t1, t2, base, back, split, block=512, sub=512):
    tokens, width = base.shape
    col = pl.BlockSpec((block, 1), lambda i: (i, 0))
    rows = pl.BlockSpec((block, width), lambda i: (i, 0))
    return pl.pallas_call(
        functools.partial(unseat_kernel, split=split, sub=sub),
        grid=(tokens // block,),
        in_specs=[col, col, rows, pl.BlockSpec(back.shape, lambda i: (0, 0, 0))],
        out_specs=rows,
        out_shape=jax.ShapeDtypeStruct((tokens, width), BF),
        compiler_params=pltpu.CompilerParams(vmem_limit_bytes=VMEM_BYTES),
        cost_estimate=estimate(tokens * width, tokens * width),
        name="unseat",
    )(t1, t2, base, back)


def route_back_kernel(
    t1, t2, ids, probs, dy, middle, gain, w_router, w_out, *refs, sub
):
    dmiddle_ref, dbranch_ref, dmixed_ref, small_ref = refs[-4:]
    experts = probs.shape[1]
    to_router, to_gain = 0.0, 0.0
    for r in range(0, t1.shape[0], sub):
        at = slice(r, r + sub)
        d_routed, dg1, dg2 = rows_back(t1[at], t2[at], refs[:-4], True)
        p = probs[at]
        lane = lax.broadcasted_iota(jnp.int32, p.shape, 1)
        d_gates = jnp.where(lane == ids[at, 0:1], dg1, 0.0) + jnp.where(lane == ids[at, 1:2], dg2, 0.0)
        d_logits = p * (d_gates - jnp.sum(p * d_gates, axis=1, keepdims=True))
        for piece in three_parts(d_logits):
            d_routed = d_routed + mm(piece, w_router[...], NT)
        normed, unit, inv = norm_forward(middle[at], gain[...])
        routed = normed.astype(BF)
        scaled = d_routed * gain[...]
        d_norm = inv * (
            scaled
            - jnp.mean(scaled, axis=1, keepdims=True)
            - unit * jnp.mean(scaled * unit, axis=1, keepdims=True)
        )
        d_middle = dy[at].astype(F32) + d_norm
        d_branch = d_middle.astype(BF)
        dmiddle_ref[at] = d_middle
        dbranch_ref[at] = d_branch
        dmixed_ref[at] = mm(d_branch, w_out[...], NT).astype(BF)
        for piece in three_parts(d_logits.T):
            to_router = to_router + mm(piece, routed)
        to_gain = to_gain + jnp.sum(d_routed * unit, axis=0, keepdims=True)

    @pl.when(pl.program_id(0) == 0)
    def _():
        small_ref[...] = jnp.zeros_like(small_ref)

    small_ref[0:experts, :] += to_router
    small_ref[experts : experts + 1, :] += to_gain


def route_back(t1, t2, ids, probs, dy, middle, gain, w_router, w_out, parts, block=512, sub=256):
    tokens, width = dy.shape
    experts = probs.shape[1]
    line = lambda cols: pl.BlockSpec((block, cols), lambda i: (i, 0))
    full = lambda a: pl.BlockSpec(a.shape, lambda i: (0,) * a.ndim)
    gain = gain[None]
    return pl.pallas_call(
        functools.partial(route_back_kernel, sub=sub),
        grid=(tokens // block,),
        in_specs=[
            line(1), line(1), line(2), line(experts), line(width), line(width),
            full(gain), full(w_router), full(w_out),
        ]
        + [full(part) for part in parts],
        out_specs=[
            line(width), line(width), line(width),
            pl.BlockSpec((experts + 8, width), lambda i: (0, 0)),
        ],
        out_shape=[
            jax.ShapeDtypeStruct((tokens, width), F32),
            jax.ShapeDtypeStruct((tokens, width), BF),
            jax.ShapeDtypeStruct((tokens, width), BF),
            jax.ShapeDtypeStruct((experts + 8, width), F32),
        ],
        compiler_params=pltpu.CompilerParams(vmem_limit_bytes=VMEM_BYTES),
        cost_estimate=estimate(tokens * width, tokens * width),
        name="route_back",
    )(t1, t2, ids, probs, dy, middle, gain, w_router, w_out, *parts)


def swap(value):
    n = lax.axis_size("ctx")
    return lax.ppermute(value, "ctx", [(i, (i + 1) % n) for i in range(n)])


def exchange(value, axes):
    return lax.all_to_all(value, axes, 0, 0, tiled=True)


def shift(value, axis, by):
    n = lax.axis_size(axis)
    return lax.ppermute(value, axis, [(i, (i + by) % n) for i in range(n)])


def scatter_begin(value, axis):
    n = lax.axis_size(axis)
    me = lax.axis_index(axis)
    x = value.reshape(n, value.shape[0] // n, value.shape[1])
    pick = lambda at: lax.dynamic_index_in_dim(x, at, 0, keepdims=False)
    return [pick(me)] + [shift(pick(lax.rem(me + s, n)), axis, s) for s in range(1, n)]


def add_up(pieces):
    total = pieces[0].astype(F32)
    for piece in pieces[1:]:
        total = total + piece.astype(F32)
    return total.astype(BF)


def gather_back(x, axis):
    n = lax.axis_size(axis)
    return [x] + [shift(x, axis, s) for s in range(1, n)]


def assemble_kernel(at, w_ref, *refs, groups, spans):
    ins, outs = refs[: 2 * groups], refs[2 * groups :]
    me = at[2]
    owners, rows = ins[0].shape[1], ins[0].shape[2]

    def write(held):
        for z in range(owners):
            back = lax.rem(me + owners - z, owners)
            for ref, span in zip(held, spans):
                piece = ref[0, back].astype(F32)
                for src, which, dst, size in span:
                    outs[which][z * rows : (z + 1) * rows, dst : dst + size] = piece[:, src : src + size]

    is_mine = pl.program_id(0) == at[0]
    pl.when(is_mine)(lambda: write(ins[:groups]))
    pl.when(jnp.logical_not(is_mine))(lambda: write(ins[groups:]))
    outs[-1][...] = jnp.sum(outs[0][...] * w_ref[...].astype(F32), axis=1, keepdims=True)


def assemble(sums, spans, widths, w_qkv):
    n_dp, owners, rows, _ = sums[0][0].shape
    n_ctx = lax.axis_size("ctx")
    block = owners * rows
    height = n_ctx * n_dp * block
    at = jnp.stack([lax.axis_index(axis) for axis in ("ctx", "dp", "expert")]).astype(jnp.int32)

    def back(mine):
        def place(c, d, at):
            edge = jnp.where(c == 0, 0, n_dp - 1)
            return ((at[1] + n_dp - jnp.where((c == at[0]) == mine, d, edge)) % n_dp, 0, 0, 0)

        return place

    line = lambda cols: pl.BlockSpec((block, cols), lambda c, d, at: (c * n_dp + d, 0))
    widths = [*widths, 1]
    return pl.pallas_call(
        functools.partial(assemble_kernel, groups=len(sums), spans=spans),
        grid_spec=pltpu.PrefetchScalarGridSpec(
            num_scalar_prefetch=1,
            grid=(n_ctx, n_dp),
            in_specs=[line(w_qkv.shape[1])]
            + [pl.BlockSpec((1,) + mine.shape[1:], back(True)) for mine, _ in sums]
            + [pl.BlockSpec((1,) + mine.shape[1:], back(False)) for mine, _ in sums],
            out_specs=[line(cols) for cols in widths],
        ),
        out_shape=[jax.ShapeDtypeStruct((height, cols), F32) for cols in widths],
        compiler_params=pltpu.CompilerParams(vmem_limit_bytes=VMEM_BYTES),
        cost_estimate=estimate(height * 2304, 12 * height * 2304),
        name="assemble",
    )(at, w_qkv, *[mine for mine, _ in sums], *[other for _, other in sums])


def spread_kernel(at, *refs):
    *ins, up_ref, down_ref = refs
    j = pl.program_id(0)
    for s, src in enumerate(ins):

        @pl.when(lax.rem(at[0] + len(ins) - s, len(ins)) == j)
        def _():
            up_ref[0] = src[0].astype(F32)
            down_ref[0] = src[1].astype(F32).T


def spread(pieces, place):
    count = len(pieces)
    _, width, cols = pieces[0].shape
    return pl.pallas_call(
        spread_kernel,
        grid_spec=pltpu.PrefetchScalarGridSpec(
            num_scalar_prefetch=1,
            grid=(count,),
            in_specs=[pl.BlockSpec((2, width, cols), lambda j, at: (0, 0, 0))] * count,
            out_specs=[
                pl.BlockSpec((1, width, cols), lambda j, at: (j, 0, 0)),
                pl.BlockSpec((1, cols, width), lambda j, at: (j, 0, 0)),
            ],
        ),
        out_shape=[
            jax.ShapeDtypeStruct((count, width, cols), F32),
            jax.ShapeDtypeStruct((count, cols, width), F32),
        ],
        compiler_params=pltpu.CompilerParams(vmem_limit_bytes=VMEM_BYTES),
        cost_estimate=estimate(width * cols, 12 * count * width * cols),
        name="spread",
    )(place.astype(jnp.int32)[None], *pieces)


def after(value, *others):
    return lax.optimization_barrier((value, others))[0]


def body(
    tokens,
    cotangent,
    router_noise,
    expert_ids,
    seat_order,
    gain_attn,
    w_qkv,
    w_out,
    gain_moe,
    w_router,
    w_up,
    w_down,
):
    image_count, half_len, width = tokens.shape
    rows = image_count * half_len
    expert_count = router_noise.shape[-1]
    n_owner = lax.axis_size("expert")
    n_ctx = lax.axis_size("ctx")
    n_dp = lax.axis_size("dp")
    here = lax.axis_index("ctx")
    my_dp = lax.axis_index("dp")
    held = w_up.shape[0]
    capacity = (2 * rows + expert_count - 1) // expert_count
    one_each = held == n_dp
    if one_each:
        parts, peers, axes = 2, n_owner * n_dp, ("expert", "dp")
        cap = capacity // parts
        slot_of = lambda e, at: (at // cap * peers + e) * cap + at % cap
        which = [my_dp] * parts
    else:
        parts, peers, axes = held // n_ctx, n_owner * n_ctx, ("expert", "ctx")
        cap = capacity
        slot_of = lambda e, at: ((e % parts) * peers + e // parts) * cap + at
        which = [here * parts + part for part in range(parts)]

    t1, t2, first_hot, second_hot = seats(
        expert_ids.reshape(rows, 2), seat_order.reshape(rows), expert_count, capacity, slot_of
    )
    dy_b = cotangent.reshape(rows, width)
    every = tuple(range(parts))
    dy_slots = seat_rows(t1, t2, dy_b, (), every, parts, peers, cap)
    dy_got = exchange(dy_slots, axes)

    tokens_b = after(tokens, dy_slots).reshape(rows, width)
    normed_ab, q_b, kv_b = project(tokens_b, gain_attn, w_qkv)
    kv_other = swap(kv_b)
    mixed_b, probs, inv_sum = attend(q_b, kv_b, kv_other, rows)

    middle = tokens_b.astype(F32) + mm(mixed_b, w_out)
    normed_m, _, _ = norm_forward(middle, gain_moe)
    routed_b = normed_m.astype(BF)
    logits = mm(routed_b, w_router) + router_noise.reshape(rows, expert_count)
    gate_probs = jax.nn.softmax(logits, axis=-1)
    gate_first = jnp.sum(jnp.where(first_hot, gate_probs, 0.0), axis=-1)
    gate_second = jnp.sum(jnp.where(second_hot, gate_probs, 0.0), axis=-1)

    sent = [
        seat_rows(
            t1, t2, routed_b, () if part else (gate_first, gate_second), (part,), parts, peers, cap
        )
        for part in every
    ]
    sent[0], dy_got = lax.optimization_barrier((sent[0], dy_got))
    x_got = [exchange(sent[0], axes)]
    outs, dx_back, dgates, kept = None, [], [], []
    t1c, t2c = t1[:, None], t2[:, None]
    for part in every:
        last = part == parts - 1
        x = x_got[part]
        if not last:
            x, following, t1c, t2c = lax.optimization_barrier((x, sent[part + 1], t1c, t2c))
            x_got.append(exchange(following, axes))
        outs, dx, act, dhid, dp, *dg = run_expert(
            which[part].astype(jnp.int32)[None], part, parts, x, x_got[0], dy_got, outs, dgates, w_up, w_down
        )
        dgates += dg
        if not last:
            dx, x_got[-1] = lax.optimization_barrier((dx, x_got[-1]))
        if dx_back:
            dx, dx_back[-1], act = lax.optimization_barrier((dx, dx_back[-1], act))
        dx_back.append(exchange(dx, axes))
        kept.append((x_got[part], dp, act, dhid))
    if one_each:
        give, keep = both_weight_grads(kept, here, n_ctx, n_dp)
        dx_back, give, keep = lax.optimization_barrier((dx_back, give, keep))
        other = swap(give)
    else:
        mine, far = [], []
        for group in kept:
            give, keep = (
                lax.psum_scatter(
                    g.reshape(-1, g.shape[-1]), "dp", scatter_dimension=0, tiled=True
                ).reshape(g.shape[1:])
                for g in both_weight_grads([group], here, n_ctx, n_dp)
            )
            mine.append(keep)
            far.append(swap(give))
        pieces = [
            jnp.where(here == n // parts, mine[n % parts], far[n % parts]) for n in reversed(range(held))
        ]
    outs, dx_back = lax.optimization_barrier((outs, dx_back))
    returned = exchange(outs, axes)
    if one_each:
        blocks = []
        for n in range(n_dp):
            pick = lambda v: lax.dynamic_index_in_dim(v, lax.rem(my_dp + n, n_dp), 0, keepdims=False)
            blocks.append(add_up([pick(keep), pick(other)]))
        dx_back, blocks = lax.optimization_barrier((dx_back, blocks))
        pieces = [block if n == 0 else shift(block, "dp", n) for n, block in enumerate(blocks)]

    d_middle, d_branch_b, d_mixed_b, small = route_back(
        t1c, t2c, expert_ids.reshape(rows, 2), gate_probs, dy_b, middle, gain_moe, w_router, w_out, dx_back
    )

    pairs = width // 128
    calls = [(first, pairs // 3) for first in range(0, pairs, pairs // 3)]

    def call(n, grad):
        return attend_back(q_b, kv_b, kv_other, mixed_b, grad, inv_sum, probs, rows, *calls[n])

    dq0, own0, far0 = call(0, d_mixed_b)
    dq1, own1, far1 = call(1, after(d_mixed_b, dq0))
    fars = [swap(far0), swap(far1)]
    result = unseat(t1c, t2c, after(middle, dq1), returned, parts)
    fars, result = lax.optimization_barrier((fars, result))
    grad_a, d_qkv_a = grad_qkv(
        normed_ab, [dq0, dq1], [own0, own1], fars, (mixed_b, d_branch_b, small)
    )
    grad_a, pieces = lax.optimization_barrier((grad_a, pieces))
    sum_a = add_up(scatter_begin(grad_a, "ctx"))
    d_mixed_b, sum_a = lax.optimization_barrier((d_mixed_b, sum_a))
    got_a = scatter_begin(sum_a, "dp")
    dq2, own2, far2 = call(2, d_mixed_b)
    got_a, dq2, own2, far2 = lax.optimization_barrier((got_a, dq2, own2, far2))
    got_a = scatter_begin(add_up(got_a), "expert")
    far2 = swap(far2)
    got_b, d_qkv_b = grad_qkv_halves(normed_ab, [dq2], [own2], [far2])
    got_a, got_b[0] = lax.optimization_barrier((got_a, got_b[0]))
    got_a = gather_back(add_up(got_a), "expert")
    got_b = scatter_begin(add_up(got_b), "dp")
    got_a, got_b[0] = lax.optimization_barrier((got_a, got_b[0]))
    got_a = gather_back(jnp.stack(got_a), "dp")
    got_b, got_a[0] = lax.optimization_barrier((got_b, got_a[0]))
    got_b = scatter_begin(add_up(got_b), "expert")
    grad_up, grad_down = spread(after(pieces, got_a[0]), my_dp if one_each else jnp.int32(held - 1))
    got_b, grad_up = lax.optimization_barrier((got_b, grad_up))
    got_b = gather_back(add_up(got_b), "expert")
    got_b = gather_back(jnp.stack(got_b), "dp")
    got_a, got_b[0] = lax.optimization_barrier((got_a, got_b[0]))
    all_a = jnp.stack(got_a)
    all_a = (all_a, swap(all_a))

    d_normed_a = 0.0
    for first, d_qkv in ((0, d_qkv_a), (calls[2][0], after(d_qkv_b, all_a[0]))):
        start, wide = 128 * first, d_qkv.shape[1] // 3
        columns = [w_qkv[:, m * width + start : m * width + start + wide] for m in range(3)]
        d_normed_a = d_normed_a + mm(d_qkv, jnp.concatenate(columns, axis=1), NT)
    _, unit_a, inv_a = norm_forward(tokens_b.astype(F32), gain_attn)
    d_tokens = d_middle + norm_backward(d_normed_a, unit_a, inv_a, gain_attn)[0]
    d_tokens, got_b = lax.optimization_barrier((d_tokens, got_b))

    all_b = jnp.stack(got_b)
    all_b = (all_b, swap(all_b))
    cols_a, cols_b, start_b = d_qkv_a.shape[1], d_qkv_b.shape[1], 128 * calls[2][0]
    spans = [
        [(m * cols_a // 3, 0, m * width, cols_a // 3) for m in range(3)]
        + [(cols_a, 1, 0, width), (cols_a + width, 2, 0, SMALL)],
        [(m * cols_b // 3, 0, m * width + start_b, cols_b // 3) for m in range(3)],
    ]
    grad_w_qkv, grad_w_out, small_sum, gain_sum = assemble(
        [all_a, all_b], spans, (3 * width, width, SMALL), w_qkv
    )
    n_small = small.shape[0]
    small_sum = small_sum[:, :n_small] + small_sum[:, n_small : 2 * n_small]
    return (
        result.reshape(image_count, half_len, width),
        d_tokens.reshape(image_count, half_len, width),
        gain_sum[:, 0] / gain_attn,
        grad_w_qkv,
        grad_w_out,
        small_sum[:, expert_count],
        small_sum[:, :expert_count],
        grad_up,
        grad_down,
    )


def solution(mesh):
    placed = (
        P(("expert", "dp"), "ctx", None),
        P(("expert", "dp"), "ctx", None),
        P(("expert", "dp"), "ctx", None),
        P(("expert", "dp"), "ctx", None),
        P(("expert", "dp"), "ctx"),
        P(),
        P(),
        P(),
        P(),
        P(),
        P("expert", None, None),
        P("expert", None, None),
    )
    return jax.shard_map(
        body,
        mesh=mesh,
        in_specs=placed,
        out_specs=(
            P(("expert", "dp"), "ctx", None),
            P(("expert", "dp"), "ctx", None),
            P(),
            P(),
            P(),
            P(),
            P(),
            P("expert", None, ("ctx", "dp")),
            P("expert", ("ctx", "dp"), None),
        ),
        check_vma=False,
    )
```

```python
import functools
import math

import jax
import jax.numpy as jnp
from jax import lax
from jax.experimental import pallas as pl
from jax.experimental.pallas import tpu as pltpu
from jax.sharding import PartitionSpec as P

HEADS = 12
NORM_EPS = 1e-06
BF = jnp.bfloat16
F32 = jnp.float32
NN = (((1,), (0,)), ((), ()))
NT = (((1,), (1,)), ((), ()))
VMEM_BYTES = 60 << 20
EXTRA = 8
SMALL = 128
SAFE = 40.0


def estimate(flops, moved, slow=0):
    return pl.CostEstimate(flops=flops // 4, bytes_accessed=moved // 4, transcendentals=slow // 4)


def mm(left, right, dims=NN):
    return lax.dot_general(left, right, dims, preferred_element_type=F32)


def norm_forward(values_in, gain_vec):
    centre_mean = jnp.mean(values_in, axis=-1, keepdims=True)
    centred = values_in - centre_mean
    inv_scale = lax.rsqrt(jnp.mean(centred * centred, axis=-1, keepdims=True) + NORM_EPS)
    unit_rows = centred * inv_scale
    return (unit_rows * gain_vec, unit_rows, inv_scale)


def norm_backward(gradient, unit_rows, inv_scale, gain_vec):
    scaled = gradient * gain_vec
    inner_sum = (
        scaled
        - jnp.mean(scaled, axis=-1, keepdims=True)
        - unit_rows * jnp.mean(scaled * unit_rows, axis=-1, keepdims=True)
    )
    return (inner_sum * inv_scale, jnp.sum(gradient * unit_rows, axis=0))


def project_kernel(x_ref, gain, w_ref, normed_ref, q_ref, kv_ref):
    width = x_ref.shape[1]
    normed = norm_forward(x_ref[...].astype(F32), gain[...])[0].astype(BF)
    normed_ref[...] = normed
    out = mm(normed, w_ref[...]).astype(BF)
    q_ref[...] = out[:, 0:width]
    kv_ref[...] = out[:, width:]


def project(x, gain, w_qkv, block=256):
    rows, width = x.shape
    line = lambda cols: pl.BlockSpec((block, cols), lambda i: (i, 0))
    return pl.pallas_call(
        project_kernel,
        grid=(rows // block,),
        in_specs=[
            line(width),
            pl.BlockSpec((1, width), lambda i: (0, 0)),
            pl.BlockSpec(w_qkv.shape, lambda i: (0, 0)),
        ],
        out_specs=[line(width), line(width), line(2 * width)],
        out_shape=[jax.ShapeDtypeStruct((rows, n * width), BF) for n in (1, 1, 2)],
        compiler_params=pltpu.CompilerParams(vmem_limit_bytes=VMEM_BYTES),
        cost_estimate=estimate(6 * rows * width * width, 20 * rows * width),
        name="project",
    )(x, gain[None], w_qkv)


def attend_kernel(q_ref, k0, k1, v0, v1, o_ref, p_ref, li_ref, vext, ksize, *, scale):
    half = k0.shape[0]

    def largest(v):
        same = lax.broadcasted_iota(jnp.int32, (128, 128), 0) // 64 == (
            lax.broadcasted_iota(jnp.int32, (128, 128), 1) // 64
        )
        squares = (v.astype(F32) * v.astype(F32)).astype(BF)
        return 1.01 * jnp.max(mm(squares, same.astype(BF)), axis=0, keepdims=True)

    @pl.when(pl.program_id(1) == 0)
    def _():
        ones = jnp.ones((half, 128), BF)
        vext[0:half, 0:128] = v0[...]
        vext[half:, 0:128] = v1[...]
        vext[0:half, 128:256] = ones
        vext[half:, 128:256] = ones
        ksize[...] = jnp.maximum(largest(k0[...]), largest(k1[...]))

    low = lax.broadcasted_iota(jnp.int32, q_ref.shape, 1) < 64
    q = q_ref[...]
    factor = scale * math.log2(math.e)
    small = jnp.max(largest(q) * ksize[...]) * (factor * factor) < SAFE * SAFE

    def run(shifted):
        outs, sums = [], []
        for h in range(2):
            picked = jnp.where(low if h == 0 else jnp.logical_not(low), q, jnp.zeros_like(q))
            s0 = mm(picked, k0[...], NT) * factor
            s1 = mm(picked, k1[...], NT) * factor
            if shifted:
                peak = jnp.maximum(
                    jnp.max(s0, axis=1, keepdims=True), jnp.max(s1, axis=1, keepdims=True)
                )
                s0 = s0 - peak
                s1 = s1 - peak
            p_ref[h, :, 0:half] = jnp.exp2(s0).astype(BF)
            p_ref[h, :, half:] = jnp.exp2(s1).astype(BF)
            both = mm(p_ref[h], vext[...])
            outs.append(both[:, 0:128])
            sums.append(both[:, 128:256])
        inv = 1.0 / jnp.where(low, sums[0], sums[1])
        o_ref[...] = (jnp.where(low, outs[0], outs[1]) * inv).astype(BF)
        li_ref[...] = inv

    pl.when(small)(lambda: run(False))
    pl.when(jnp.logical_not(small))(lambda: run(True))


def attend(q, kv, kv_other, block):
    rows, width = q.shape
    pairs = width // 128
    tile = pl.BlockSpec((block, 128), lambda h, i: (i, h))
    return pl.pallas_call(
        functools.partial(attend_kernel, scale=1.0 / math.sqrt(width // HEADS)),
        grid=(pairs, rows // block),
        in_specs=[
            tile,
            pl.BlockSpec((rows, 128), lambda h, i: (0, h)),
            pl.BlockSpec((rows, 128), lambda h, i: (0, h)),
            pl.BlockSpec((rows, 128), lambda h, i: (0, pairs + h)),
            pl.BlockSpec((rows, 128), lambda h, i: (0, pairs + h)),
        ],
        out_specs=[tile, pl.BlockSpec((2, block, 2 * rows), lambda h, i: (h, i, 0)), tile],
        out_shape=[
            jax.ShapeDtypeStruct((rows, width), BF),
            jax.ShapeDtypeStruct((HEADS, rows, 2 * rows), BF),
            jax.ShapeDtypeStruct((rows, width), F32),
        ],
        scratch_shapes=[pltpu.VMEM((2 * rows, 256), BF), pltpu.VMEM((1, 128), F32)],
        compiler_params=pltpu.CompilerParams(vmem_limit_bytes=VMEM_BYTES),
        cost_estimate=estimate(rows * width, rows * width),
        name="attend",
    )(q, kv, kv_other, kv, kv_other)


def attend_back_kernel(
    q_ref, k0, k1, v0, v1, o_ref, g_ref, li_ref, p_ref,
    dq_ref, own_ref, far_ref, vext, kacc, vacc, *, scale, steps,
):
    i = pl.program_id(1)
    half = k0.shape[0]
    lane = lax.broadcasted_iota(jnp.int32, q_ref.shape, 1)
    low = lane < 64

    @pl.when(i == 0)
    def _():
        ones = jnp.where(lax.broadcasted_iota(jnp.int32, (half, 128), 1) < 2, 1.0, 0.0).astype(BF)
        vext[0:half, 0:128] = v0[...]
        vext[half:, 0:128] = v1[...]
        vext[0:half, 128:256] = ones
        vext[half:, 128:256] = ones

    g = g_ref[...].astype(F32) * li_ref[...]
    gb = g.astype(BF)
    go = g * o_ref[...].astype(F32)
    qt = q_ref[...].T
    gt = gb.T
    dqs = []
    for h in range(2):
        mine = low if h == 0 else jnp.logical_not(low)
        delta = -jnp.sum(jnp.where(mine, go, 0.0), axis=1, keepdims=True)
        high = delta.astype(BF).astype(F32)
        extra = jnp.where(lane == 0, high, jnp.where(lane == 1, delta - high, 0.0)).astype(BF)
        gext = jnp.concatenate([jnp.where(mine, gb, jnp.zeros_like(gb)), extra], axis=1)
        p = p_ref[h]
        ds = (p.astype(F32) * mm(gext, vext[...], NT)).astype(BF)
        dqs.append(mm(ds[:, 0:half], k0[...]) + mm(ds[:, half:], k1[...]))
        rows = slice(64 * h, 64 * h + 64)
        dk = mm(qt[rows], ds)
        dv = mm(gt[rows], p)

        @pl.when(i == 0)
        def _():
            kacc[rows] = dk
            vacc[rows] = dv

        @pl.when(i > 0)
        def _():
            kacc[rows] += dk
            vacc[rows] += dv

    dq_ref[...] = (jnp.where(low, dqs[0], dqs[1]) * scale).astype(BF)

    @pl.when(i == steps - 1)
    def _():
        own_ref[0] = (kacc[:, 0:half].T * scale).astype(BF)
        own_ref[1] = vacc[:, 0:half].T.astype(BF)
        far_ref[0] = (kacc[:, half:].T * scale).astype(BF)
        far_ref[1] = vacc[:, half:].T.astype(BF)


def attend_back(q, kv, kv_other, mixed, grad, inv_sum, probs, block, first, count):
    rows, width = q.shape
    pairs = width // 128
    steps = rows // block
    tile = pl.BlockSpec((block, 128), lambda h, i: (i, first + h))
    both = pl.BlockSpec((2, rows, 128), lambda h, i: (0, 0, h))
    return pl.pallas_call(
        functools.partial(attend_back_kernel, scale=1.0 / math.sqrt(width // HEADS), steps=steps),
        grid=(count, steps),
        in_specs=[
            tile,
            pl.BlockSpec((rows, 128), lambda h, i: (0, first + h)),
            pl.BlockSpec((rows, 128), lambda h, i: (0, first + h)),
            pl.BlockSpec((rows, 128), lambda h, i: (0, pairs + first + h)),
            pl.BlockSpec((rows, 128), lambda h, i: (0, pairs + first + h)),
            tile,
            tile,
            tile,
            pl.BlockSpec((2, block, 2 * rows), lambda h, i: (first + h, i, 0)),
        ],
        out_specs=[pl.BlockSpec((block, 128), lambda h, i: (i, h)), both, both],
        out_shape=[
            jax.ShapeDtypeStruct((rows, 128 * count), BF),
            jax.ShapeDtypeStruct((2, rows, 128 * count), BF),
            jax.ShapeDtypeStruct((2, rows, 128 * count), BF),
        ],
        scratch_shapes=[
            pltpu.VMEM((2 * rows, 256), BF),
            pltpu.VMEM((128, 2 * rows), F32),
            pltpu.VMEM((128, 2 * rows), F32),
        ],
        compiler_params=pltpu.CompilerParams(vmem_limit_bytes=VMEM_BYTES),
        cost_estimate=estimate(rows * width, rows * width),
        name="attend_back",
    )(q, kv, kv_other, kv, kv_other, mixed, grad, inv_sum, probs)


def grad_qkv_kernel(core, normed, *refs, count, with_out):
    if count:
        grad_ref, dqkv_ref = refs[-2:]
        cols = dqkv_ref.shape[1]
        wide = cols // 3
        at = 0
        for n in range(count):
            dq, own, far = refs[n], refs[count + n], refs[2 * count + n]
            size = dq.shape[1]
            dqkv_ref[:, at : at + size] = dq[...]
            for m in range(2):
                start = (m + 1) * wide + at
                dqkv_ref[:, start : start + size] = (own[m].astype(F32) + far[m].astype(F32)).astype(BF)
            at += size
        more = refs[3 * count :]
    else:
        dqkv_ref, grad_ref = refs[0], refs[-1]
        cols = dqkv_ref.shape[1]
        more = refs[1:]
    grad_ref[:, 0:cols] = mm(normed[...].T, dqkv_ref[...]).astype(BF)
    if with_out:
        mixed, branch, small = more[:3]
        width = branch.shape[1]
        grad_ref[:, cols : cols + width] = mm(mixed[...].T, branch[...]).astype(BF)
        value = small[...]
        high = value.astype(BF).astype(F32)
        rest = jnp.zeros((SMALL - 2 * value.shape[0], value.shape[1]), F32)
        grad_ref[:, cols + width :] = jnp.concatenate([high, value - high, rest], axis=0).T.astype(BF)


def grad_qkv_part(core, normed, sides, count, more, half):
    rows, width = normed.shape
    cols = sum(side.shape[-1] for side in sides[:count]) * 3 if count else sides[0].shape[1]
    out_cols = cols + (more[1].shape[1] + SMALL if more else 0)
    full = lambda a: pl.BlockSpec(a.shape, lambda i, core: (0,) * a.ndim)
    part = lambda a: pl.BlockSpec((a.shape[0], half), lambda i, core: (0, core[0]))
    out_specs = [pl.BlockSpec((half, out_cols), lambda i, core: (0, 0))]
    out_shape = [jax.ShapeDtypeStruct((half, out_cols), BF)]
    if count:
        out_specs.append(pl.BlockSpec((rows, cols), lambda i, core: (0, 0)))
        out_shape.append(jax.ShapeDtypeStruct((rows, cols), BF))
    return pl.pallas_call(
        functools.partial(grad_qkv_kernel, count=count, with_out=bool(more)),
        grid_spec=pltpu.PrefetchScalarGridSpec(
            num_scalar_prefetch=1,
            grid=(1,),
            in_specs=[part(normed)]
            + [full(side) for side in sides]
            + ([part(more[0]), full(more[1]), part(more[2])] if more else []),
            out_specs=out_specs,
        ),
        out_shape=out_shape,
        compiler_params=pltpu.CompilerParams(vmem_limit_bytes=VMEM_BYTES),
        cost_estimate=estimate(rows * width, rows * width),
        name="grad_qkv",
    )(core.astype(jnp.int32)[None], normed, *sides, *more)


def grad_qkv(normed, dqs, owns, fars, more=()):
    return grad_qkv_part(jnp.int32(0), normed, (*dqs, *owns, *fars), len(dqs), more, normed.shape[1])


def grad_qkv_halves(normed, dqs, owns, fars):
    here = lax.axis_index("ctx")
    half = normed.shape[1] // 2
    give, d_qkv = grad_qkv_part(1 - here, normed, (*dqs, *owns, *fars), len(dqs), (), half)
    other = swap(give)
    (keep,) = grad_qkv_part(here, normed, (d_qkv,), 0, (), half)
    return [keep, other], d_qkv


GELU_A = math.sqrt(2.0 / math.pi)
GELU_B = 0.044715


def gelu_both(v):
    square = v * v
    t = jnp.tanh(v * (GELU_A + GELU_A * GELU_B * square))
    half = 0.5 + 0.5 * t
    slope = half + (0.5 * v) * (1.0 - t * t) * (GELU_A + 3 * GELU_A * GELU_B * square)
    return v * half, slope


def put_extra(ref, r, row):
    width = ref.shape[2]
    cap = row.shape[1]
    line = lax.broadcasted_iota(jnp.int32, (EXTRA, cap), 0)
    full = jnp.zeros((EXTRA, cap), F32)
    for n, piece in enumerate(three_parts(row)):
        full = jnp.where(line == n, piece.astype(F32), full)
    full = jnp.concatenate([full, jnp.zeros((EXTRA, width - cap), F32)], axis=1)
    ref[r, ref.shape[1] - EXTRA :, :] = full.astype(BF)


def get_extra(ref, r, lanes):
    sent = ref[r, ref.shape[1] - EXTRA :, lanes].astype(F32)
    return sent[0:1] + sent[1:2] + sent[2:3]


def expert_kernel(which, x_in, gate_in, dy_in, *refs, part, parts, steps, first):
    last = part == parts - 1
    if not first:
        refs = refs[1:]
    dg_in = ()
    if last:
        dg_in, refs = refs[: parts - 1], refs[parts - 1 :]
    up_ref, down_ref, out_ref, dx_ref, act_ref, dhid_ref, dp_ref, *refs = refs
    if not last:
        dg_out, refs = refs[0], refs[1:]
    x, gate, out_acc, dx_acc = refs
    f = pl.program_id(0)
    peers, cap = dy_in.shape[0], dy_in.shape[1]

    @pl.when(f == 0)
    def _():
        lanes = slice(part * cap, (part + 1) * cap)
        gates = jnp.concatenate([get_extra(gate_in, r, lanes) for r in range(peers)], axis=0).T
        for r in range(peers):
            at = slice(r * cap, (r + 1) * cap)
            x[at] = x_in[r, 0:cap, :]
            g = gates[:, r : r + 1]
            gate[at] = g
            dp_ref[at] = (dy_in[r].astype(F32) * g).astype(BF)

    up = up_ref[0]
    down = down_ref[0]
    value, slope = gelu_both(mm(x[...], up))
    act_ref[...] = value.astype(BF)
    dhid_ref[...] = (mm(dp_ref[...], down, NT) * slope).astype(BF)

    @pl.when(f == 0)
    def _():
        dx_acc[...] = mm(dhid_ref[...], up, NT)
        out_acc[...] = mm(act_ref[...], down)

    @pl.when(f > 0)
    def _():
        dx_acc[...] += mm(dhid_ref[...], up, NT)
        out_acc[...] += mm(act_ref[...], down)

    @pl.when(f == steps - 1)
    def _():
        sums = []
        for r in range(peers):
            at = slice(r * cap, (r + 1) * cap)
            produced = out_acc[at].astype(BF).astype(F32)
            dx_ref[r, 0:cap, :] = dx_acc[at].astype(BF)
            out_ref[r] = (produced * gate[at]).astype(BF)
            sums.append(jnp.sum(produced * dy_in[r].astype(F32), axis=1, keepdims=True))
        sums = jnp.concatenate(sums, axis=1).T
        if last:
            full = jnp.concatenate([ref[...] for ref in dg_in] + [sums], axis=1)
            for r in range(peers):
                put_extra(dx_ref, r, full[r : r + 1])
        else:
            dg_out[...] = sums


def run_expert(which, part, parts, x, first_x, dy, outs, dgates, w_up, w_down, chunk=768):
    peers, width = x.shape[0], x.shape[2]
    cap = dy.shape[1] // parts
    rows = peers * cap
    hidden = w_up.shape[-1]
    last = part == parts - 1
    full = lambda shape: pl.BlockSpec(shape, lambda f, j: (0,) * len(shape))
    wide = pl.BlockSpec((rows, chunk), lambda f, j: (0, f))
    dx_shape = (peers, cap + (EXTRA if last else 0), width)
    extra_at = (first_x.shape[1] - EXTRA) // EXTRA
    out_specs = [
        pl.BlockSpec((peers, cap, width), lambda f, j: (0, part, 0)),
        full(dx_shape), wide, wide, full((rows, width)),
    ]
    out_shape = [
        jax.ShapeDtypeStruct(dy.shape, BF),
        jax.ShapeDtypeStruct(dx_shape, BF),
        jax.ShapeDtypeStruct((rows, hidden), BF),
        jax.ShapeDtypeStruct((rows, hidden), BF),
        jax.ShapeDtypeStruct((rows, width), BF),
    ]
    if not last:
        out_specs.append(full((peers, cap)))
        out_shape.append(jax.ShapeDtypeStruct((peers, cap), F32))
        dgates = []
    return pl.pallas_call(
        functools.partial(
            expert_kernel, part=part, parts=parts, steps=hidden // chunk, first=outs is None
        ),
        grid_spec=pltpu.PrefetchScalarGridSpec(
            num_scalar_prefetch=1,
            grid=(hidden // chunk,),
            in_specs=[
                full(x.shape),
                pl.BlockSpec((peers, EXTRA, width), lambda f, j: (0, extra_at, 0)),
                pl.BlockSpec((peers, cap, width), lambda f, j: (0, part, 0)),
                *[pl.BlockSpec(memory_space=pl.ANY)] * (outs is not None),
                *[full(d.shape) for d in dgates],
                pl.BlockSpec((1, width, chunk), lambda f, j: (j[0], 0, f)),
                pl.BlockSpec((1, chunk, width), lambda f, j: (j[0], f, 0)),
            ],
            out_specs=out_specs,
            scratch_shapes=[
                pltpu.VMEM((rows, width), BF),
                pltpu.VMEM((rows, 1), F32),
                pltpu.VMEM((rows, width), F32),
                pltpu.VMEM((rows, width), F32),
            ],
        ),
        out_shape=out_shape,
        compiler_params=pltpu.CompilerParams(vmem_limit_bytes=VMEM_BYTES),
        cost_estimate=estimate(8 * rows * width * hidden, 4 * width * hidden, rows * hidden),
        input_output_aliases={} if outs is None else {4: 0},
        name="expert",
    )(which, x, first_x, dy, *([] if outs is None else [outs]), *dgates, w_up, w_down)


def weights_kernel(at, *refs, count, pieces, turned):
    acts, dhids, refs = refs[:count], refs[count : 2 * count], refs[2 * count :]
    if turned:
        xt, dpt, out_ref = refs
    else:
        xs, dps, (out_ref, xt, dpt) = refs[:count], refs[count : 2 * count], refs[2 * count :]

        @pl.when(pl.program_id(0) == 0)
        def _():
            place = 0
            for x, dp in zip(xs, dps):
                rows = dp.shape[0]
                cap = rows // x.shape[0]
                held = jnp.concatenate([x[r, 0:cap, :] for r in range(x.shape[0])], axis=0)
                xt[:, place : place + rows] = held.T
                dpt[:, place : place + rows] = dp[...].T
                place += rows

    def product(left, rights):
        total, place = None, 0
        for right in rights:
            rows = right.shape[0]
            add = mm(left[:, place : place + rows], right[...])
            total = add if total is None else total + add
            place += rows
        return total.astype(BF)

    gup = product(xt, dhids)
    gdown = product(dpt, acts)
    wide = gup.shape[1] // pieces
    for s in range(pieces):
        out_ref[s, 0] = gup[:, s * wide : (s + 1) * wide]
        out_ref[s, 1] = gdown[:, s * wide : (s + 1) * wide]


def weight_grads(core, acts, dhids, sides, turned, n_ctx, n_dp, chunk=768):
    width, hidden = (sides[0].shape[0] if turned else sides[0].shape[2]), acts[0].shape[1]
    rows = sum(a.shape[0] for a in acts)
    half = hidden // n_ctx
    steps = half // chunk
    wide = half // n_dp
    pieces = chunk // wide
    full = lambda shape: pl.BlockSpec(shape, lambda f, at: (0,) * len(shape))
    out_specs = [pl.BlockSpec((pieces, 2, width, wide), lambda f, at: (f, 0, 0, 0))]
    out_shape = [jax.ShapeDtypeStruct((n_dp, 2, width, wide), BF)]
    if not turned:
        out_specs += [full((width, rows))] * 2
        out_shape += [jax.ShapeDtypeStruct((width, rows), BF)] * 2
    made = pl.pallas_call(
        functools.partial(weights_kernel, count=len(acts), pieces=pieces, turned=turned),
        grid_spec=pltpu.PrefetchScalarGridSpec(
            num_scalar_prefetch=1,
            grid=(steps,),
            in_specs=[
                pl.BlockSpec((a.shape[0], chunk), lambda f, at: (0, at[0] * steps + f))
                for a in (*acts, *dhids)
            ]
            + [full(a.shape) for a in sides],
            out_specs=out_specs,
        ),
        out_shape=out_shape,
        compiler_params=pltpu.CompilerParams(vmem_limit_bytes=VMEM_BYTES),
        cost_estimate=estimate(rows * width, rows * width),
        name="weight_grads",
    )(core.astype(jnp.int32)[None], *acts, *dhids, *sides)
    return made[0], made[1:]


def both_weight_grads(group, here, n_ctx, n_dp):
    xs, dps, acts, dhids = zip(*group)
    give, sides = weight_grads(1 - here, acts, dhids, (*xs, *dps), False, n_ctx, n_dp)
    keep, _ = weight_grads(here, acts, dhids, sides, True, n_ctx, n_dp)
    return give, keep


def seats(expert_ids, seat_order, expert_count, capacity, slot_of):
    token_count = expert_ids.shape[0]
    places = jnp.arange(token_count, dtype=jnp.int32)
    earlier = (seat_order[:, None] < seat_order[None, :]) | (
        seat_order[:, None] == seat_order[None, :]
    ) & (places[:, None] < places[None, :])
    earlier = earlier.astype(BF)
    lane_ids = jnp.arange(expert_count, dtype=jnp.int32)
    first_hot = expert_ids[:, 0:1] == lane_ids[None, :]
    second_hot = expert_ids[:, 1:2] == lane_ids[None, :]
    both_hot = jnp.concatenate([first_hot, second_hot], axis=1).astype(BF)
    ahead = jnp.einsum("st,se->te", earlier, both_hot, preferred_element_type=F32)
    ahead_first = ahead[:, :expert_count]
    ahead_second = ahead[:, expert_count:] + jnp.sum(first_hot.astype(F32), axis=0)[None, :]
    rank_first = jnp.sum(jnp.where(first_hot, ahead_first, 0.0), axis=-1)
    rank_second = jnp.sum(jnp.where(second_hot, ahead_second, 0.0), axis=-1)

    def slot(picked, rank):
        at = rank.astype(jnp.int32)
        return jnp.where(at < capacity, slot_of(picked, at), -1)

    return (
        slot(expert_ids[:, 0], rank_first),
        slot(expert_ids[:, 1], rank_second),
        first_hot,
        second_hot,
    )


def three_parts(v):
    high = v.astype(BF)
    rest = v - high.astype(F32)
    mid = rest.astype(BF)
    return high, mid, (rest - mid.astype(F32)).astype(BF)


def seat_rows_kernel(t1, t2, *refs, chosen, parts, cap):
    *gate_refs, rows_ref, out_ref = refs
    peers = out_ref.shape[0]
    tokens = t1.shape[1]
    group = min(peers, max(1, 256 // cap))

    def hot_of(t, part, r):
        ids = lax.broadcasted_iota(jnp.int32, (group * cap, tokens), 0) + (part * peers + r) * cap
        return ids == t[...]

    for n, part in enumerate(chosen):
        for r in range(0, peers, group):
            hot = hot_of(t1, part, r) | hot_of(t2, part, r)
            got = mm(jnp.where(hot, 1.0, 0.0).astype(BF), rows_ref[...]).astype(BF)
            for m in range(group):
                out_ref[r + m, n * cap : (n + 1) * cap, :] = got[m * cap : (m + 1) * cap]
    if gate_refs:
        lefts = [jnp.concatenate(three_parts(g[...]), axis=0) for g in gate_refs]
        for r in range(0, peers, group):
            got = []
            for part in range(parts):
                both = sum(
                    mm(left, jnp.where(hot_of(t, part, r), 1.0, 0.0).astype(BF), NT)
                    for left, t in zip(lefts, (t1, t2))
                )
                got.append(jnp.sum(both, axis=0, keepdims=True))
            for m in range(group):
                put_extra(
                    out_ref, r + m, jnp.concatenate([g[:, m * cap : (m + 1) * cap] for g in got], axis=1)
                )


def seat_rows(t1, t2, rows, gates, chosen, parts, peers, cap):
    tokens, width = rows.shape
    per_peer = len(chosen) * cap + (EXTRA if gates else 0)
    return pl.pallas_call(
        functools.partial(seat_rows_kernel, chosen=chosen, parts=parts, cap=cap),
        out_shape=jax.ShapeDtypeStruct((peers, per_peer, width), BF),
        compiler_params=pltpu.CompilerParams(vmem_limit_bytes=VMEM_BYTES),
        cost_estimate=estimate(2 * peers * per_peer * tokens * width, 4 * tokens * width),
        name="seat_rows",
    )(t1[None], t2[None], *[g[None] for g in gates], rows)


def rows_back(t1, t2, back, extra, split=1):
    tokens = t1.shape[0]
    total, place = None, 0
    firsts = jnp.zeros((tokens, 1), F32)
    seconds = firsts
    peers = back[0].shape[0]
    parts = [(ref, 0, back[0].shape[1]) for ref in back]
    if split > 1:
        cap = back[0].shape[1] // split
        parts = [(back[0], n * cap, cap) for n in range(split)]
    for part, (ref, start, cap) in enumerate(parts):
        group = min(peers, max(1, 512 // cap))
        for b in range(0, peers, group):
            ids = lax.broadcasted_iota(jnp.int32, (tokens, group * cap), 1) + place
            place += group * cap
            first = ids == t1
            second = ids == t2
            hot = jnp.where(first | second, 1.0, 0.0).astype(BF)
            add = mm(hot, jnp.concatenate([ref[b + n, start : start + cap, :] for n in range(group)], axis=0))
            total = add if total is None else total + add
            if extra:
                lanes = slice(part * cap, (part + 1) * cap)
                dg = jnp.concatenate([get_extra(back[-1], b + n, lanes) for n in range(group)], axis=1)
                firsts += jnp.sum(jnp.where(first, dg, 0.0), axis=1, keepdims=True)
                seconds += jnp.sum(jnp.where(second, dg, 0.0), axis=1, keepdims=True)
    return total, firsts, seconds


def unseat_kernel(t1, t2, base, back, out_ref, *, split, sub):
    for r in range(0, t1.shape[0], sub):
        at = slice(r, r + sub)
        total, _, _ = rows_back(t1[at], t2[at], [back], False, split)
        out_ref[at] = (base[at] + total).astype(BF)


def unseat(t1, t2, base, back, split, block=512, sub=512):
    tokens, width = base.shape
    col = pl.BlockSpec((block, 1), lambda i: (i, 0))
    rows = pl.BlockSpec((block, width), lambda i: (i, 0))
    return pl.pallas_call(
        functools.partial(unseat_kernel, split=split, sub=sub),
        grid=(tokens // block,),
        in_specs=[col, col, rows, pl.BlockSpec(back.shape, lambda i: (0, 0, 0))],
        out_specs=rows,
        out_shape=jax.ShapeDtypeStruct((tokens, width), BF),
        compiler_params=pltpu.CompilerParams(vmem_limit_bytes=VMEM_BYTES),
        cost_estimate=estimate(tokens * width, tokens * width),
        name="unseat",
    )(t1, t2, base, back)


def route_back_kernel(
    t1, t2, ids, probs, dy, middle, gain, w_router, w_out, *refs, sub
):
    dmiddle_ref, dbranch_ref, dmixed_ref, small_ref = refs[-4:]
    experts = probs.shape[1]
    to_router, to_gain = 0.0, 0.0
    for r in range(0, t1.shape[0], sub):
        at = slice(r, r + sub)
        d_routed, dg1, dg2 = rows_back(t1[at], t2[at], refs[:-4], True)
        p = probs[at]
        lane = lax.broadcasted_iota(jnp.int32, p.shape, 1)
        d_gates = jnp.where(lane == ids[at, 0:1], dg1, 0.0) + jnp.where(lane == ids[at, 1:2], dg2, 0.0)
        d_logits = p * (d_gates - jnp.sum(p * d_gates, axis=1, keepdims=True))
        for piece in three_parts(d_logits):
            d_routed = d_routed + mm(piece, w_router[...], NT)
        normed, unit, inv = norm_forward(middle[at], gain[...])
        routed = normed.astype(BF)
        scaled = d_routed * gain[...]
        d_norm = inv * (
            scaled
            - jnp.mean(scaled, axis=1, keepdims=True)
            - unit * jnp.mean(scaled * unit, axis=1, keepdims=True)
        )
        d_middle = dy[at].astype(F32) + d_norm
        d_branch = d_middle.astype(BF)
        dmiddle_ref[at] = d_middle
        dbranch_ref[at] = d_branch
        dmixed_ref[at] = mm(d_branch, w_out[...], NT).astype(BF)
        for piece in three_parts(d_logits.T):
            to_router = to_router + mm(piece, routed)
        to_gain = to_gain + jnp.sum(d_routed * unit, axis=0, keepdims=True)

    @pl.when(pl.program_id(0) == 0)
    def _():
        small_ref[...] = jnp.zeros_like(small_ref)

    small_ref[0:experts, :] += to_router
    small_ref[experts : experts + 1, :] += to_gain


def route_back(t1, t2, ids, probs, dy, middle, gain, w_router, w_out, parts, block=512, sub=256):
    tokens, width = dy.shape
    experts = probs.shape[1]
    line = lambda cols: pl.BlockSpec((block, cols), lambda i: (i, 0))
    full = lambda a: pl.BlockSpec(a.shape, lambda i: (0,) * a.ndim)
    gain = gain[None]
    return pl.pallas_call(
        functools.partial(route_back_kernel, sub=sub),
        grid=(tokens // block,),
        in_specs=[
            line(1), line(1), line(2), line(experts), line(width), line(width),
            full(gain), full(w_router), full(w_out),
        ]
        + [full(part) for part in parts],
        out_specs=[
            line(width), line(width), line(width),
            pl.BlockSpec((experts + 8, width), lambda i: (0, 0)),
        ],
        out_shape=[
            jax.ShapeDtypeStruct((tokens, width), F32),
            jax.ShapeDtypeStruct((tokens, width), BF),
            jax.ShapeDtypeStruct((tokens, width), BF),
            jax.ShapeDtypeStruct((experts + 8, width), F32),
        ],
        compiler_params=pltpu.CompilerParams(vmem_limit_bytes=VMEM_BYTES),
        cost_estimate=estimate(tokens * width, tokens * width),
        name="route_back",
    )(t1, t2, ids, probs, dy, middle, gain, w_router, w_out, *parts)


def swap(value):
    n = lax.axis_size("ctx")
    return lax.ppermute(value, "ctx", [(i, (i + 1) % n) for i in range(n)])


def exchange(value, axes):
    return lax.all_to_all(value, axes, 0, 0, tiled=True)


def shift(value, axis, by):
    n = lax.axis_size(axis)
    return lax.ppermute(value, axis, [(i, (i + by) % n) for i in range(n)])


def scatter_begin(value, axis):
    n = lax.axis_size(axis)
    me = lax.axis_index(axis)
    x = value.reshape(n, value.shape[0] // n, value.shape[1])
    pick = lambda at: lax.dynamic_index_in_dim(x, at, 0, keepdims=False)
    return [pick(me)] + [shift(pick(lax.rem(me + s, n)), axis, s) for s in range(1, n)]


def add_up(pieces):
    total = pieces[0].astype(F32)
    for piece in pieces[1:]:
        total = total + piece.astype(F32)
    return total.astype(BF)


def gather_back(x, axis):
    n = lax.axis_size(axis)
    return [x] + [shift(x, axis, s) for s in range(1, n)]


def assemble_kernel(at, w_ref, *refs, groups, spans):
    ins, outs = refs[: 2 * groups], refs[2 * groups :]
    me = at[2]
    owners, rows = ins[0].shape[1], ins[0].shape[2]

    def write(held):
        for z in range(owners):
            back = lax.rem(me + owners - z, owners)
            for ref, span in zip(held, spans):
                piece = ref[0, back].astype(F32)
                for src, which, dst, size in span:
                    outs[which][z * rows : (z + 1) * rows, dst : dst + size] = piece[:, src : src + size]

    is_mine = pl.program_id(0) == at[0]
    pl.when(is_mine)(lambda: write(ins[:groups]))
    pl.when(jnp.logical_not(is_mine))(lambda: write(ins[groups:]))
    outs[-1][...] = jnp.sum(outs[0][...] * w_ref[...].astype(F32), axis=1, keepdims=True)


def assemble(sums, spans, widths, w_qkv):
    n_dp, owners, rows, _ = sums[0][0].shape
    n_ctx = lax.axis_size("ctx")
    block = owners * rows
    height = n_ctx * n_dp * block
    at = jnp.stack([lax.axis_index(axis) for axis in ("ctx", "dp", "expert")]).astype(jnp.int32)

    def back(mine):
        def place(c, d, at):
            edge = jnp.where(c == 0, 0, n_dp - 1)
            return ((at[1] + n_dp - jnp.where((c == at[0]) == mine, d, edge)) % n_dp, 0, 0, 0)

        return place

    line = lambda cols: pl.BlockSpec((block, cols), lambda c, d, at: (c * n_dp + d, 0))
    widths = [*widths, 1]
    return pl.pallas_call(
        functools.partial(assemble_kernel, groups=len(sums), spans=spans),
        grid_spec=pltpu.PrefetchScalarGridSpec(
            num_scalar_prefetch=1,
            grid=(n_ctx, n_dp),
            in_specs=[line(w_qkv.shape[1])]
            + [pl.BlockSpec((1,) + mine.shape[1:], back(True)) for mine, _ in sums]
            + [pl.BlockSpec((1,) + mine.shape[1:], back(False)) for mine, _ in sums],
            out_specs=[line(cols) for cols in widths],
        ),
        out_shape=[jax.ShapeDtypeStruct((height, cols), F32) for cols in widths],
        compiler_params=pltpu.CompilerParams(vmem_limit_bytes=VMEM_BYTES),
        cost_estimate=estimate(height * 2304, 12 * height * 2304),
        name="assemble",
    )(at, w_qkv, *[mine for mine, _ in sums], *[other for _, other in sums])


def spread_kernel(at, *refs):
    *ins, up_ref, down_ref = refs
    j = pl.program_id(0)
    for s, src in enumerate(ins):

        @pl.when(lax.rem(at[0] + len(ins) - s, len(ins)) == j)
        def _():
            up_ref[0] = src[0].astype(F32)
            down_ref[0] = src[1].astype(F32).T


def spread(pieces, place):
    count = len(pieces)
    _, width, cols = pieces[0].shape
    return pl.pallas_call(
        spread_kernel,
        grid_spec=pltpu.PrefetchScalarGridSpec(
            num_scalar_prefetch=1,
            grid=(count,),
            in_specs=[pl.BlockSpec((2, width, cols), lambda j, at: (0, 0, 0))] * count,
            out_specs=[
                pl.BlockSpec((1, width, cols), lambda j, at: (j, 0, 0)),
                pl.BlockSpec((1, cols, width), lambda j, at: (j, 0, 0)),
            ],
        ),
        out_shape=[
            jax.ShapeDtypeStruct((count, width, cols), F32),
            jax.ShapeDtypeStruct((count, cols, width), F32),
        ],
        compiler_params=pltpu.CompilerParams(vmem_limit_bytes=VMEM_BYTES),
        cost_estimate=estimate(width * cols, 12 * count * width * cols),
        name="spread",
    )(place.astype(jnp.int32)[None], *pieces)


def after(value, *others):
    return lax.optimization_barrier((value, others))[0]


def body(
    tokens,
    cotangent,
    router_noise,
    expert_ids,
    seat_order,
    gain_attn,
    w_qkv,
    w_out,
    gain_moe,
    w_router,
    w_up,
    w_down,
):
    image_count, half_len, width = tokens.shape
    rows = image_count * half_len
    expert_count = router_noise.shape[-1]
    n_owner = lax.axis_size("expert")
    n_ctx = lax.axis_size("ctx")
    n_dp = lax.axis_size("dp")
    here = lax.axis_index("ctx")
    my_dp = lax.axis_index("dp")
    held = w_up.shape[0]
    capacity = (2 * rows + expert_count - 1) // expert_count
    one_each = held == n_dp
    if one_each:
        parts, peers, axes = 2, n_owner * n_dp, ("expert", "dp")
        cap = capacity // parts
        slot_of = lambda e, at: (at // cap * peers + e) * cap + at % cap
        which = [my_dp] * parts
    else:
        parts, peers, axes = held // n_ctx, n_owner * n_ctx, ("expert", "ctx")
        cap = capacity
        slot_of = lambda e, at: ((e % parts) * peers + e // parts) * cap + at
        which = [here * parts + part for part in range(parts)]

    t1, t2, first_hot, second_hot = seats(
        expert_ids.reshape(rows, 2), seat_order.reshape(rows), expert_count, capacity, slot_of
    )
    dy_b = cotangent.reshape(rows, width)
    every = tuple(range(parts))
    dy_slots = seat_rows(t1, t2, dy_b, (), every, parts, peers, cap)
    dy_got = exchange(dy_slots, axes)

    tokens_b = after(tokens, dy_slots).reshape(rows, width)
    normed_ab, q_b, kv_b = project(tokens_b, gain_attn, w_qkv)
    kv_other = swap(kv_b)
    mixed_b, probs, inv_sum = attend(q_b, kv_b, kv_other, rows)

    middle = tokens_b.astype(F32) + mm(mixed_b, w_out)
    normed_m, _, _ = norm_forward(middle, gain_moe)
    routed_b = normed_m.astype(BF)
    logits = mm(routed_b, w_router) + router_noise.reshape(rows, expert_count)
    gate_probs = jax.nn.softmax(logits, axis=-1)
    gate_first = jnp.sum(jnp.where(first_hot, gate_probs, 0.0), axis=-1)
    gate_second = jnp.sum(jnp.where(second_hot, gate_probs, 0.0), axis=-1)

    sent = [
        seat_rows(
            t1, t2, routed_b, () if part else (gate_first, gate_second), (part,), parts, peers, cap
        )
        for part in every
    ]
    sent[0], dy_got = lax.optimization_barrier((sent[0], dy_got))
    x_got = [exchange(sent[0], axes)]
    outs, dx_back, dgates, kept = None, [], [], []
    t1c, t2c = t1[:, None], t2[:, None]
    for part in every:
        last = part == parts - 1
        x = x_got[part]
        if not last:
            x, following, t1c, t2c = lax.optimization_barrier((x, sent[part + 1], t1c, t2c))
            x_got.append(exchange(following, axes))
        outs, dx, act, dhid, dp, *dg = run_expert(
            which[part].astype(jnp.int32)[None], part, parts, x, x_got[0], dy_got, outs, dgates, w_up, w_down
        )
        dgates += dg
        if not last:
            dx, x_got[-1] = lax.optimization_barrier((dx, x_got[-1]))
        if dx_back:
            dx, dx_back[-1], act = lax.optimization_barrier((dx, dx_back[-1], act))
        dx_back.append(exchange(dx, axes))
        kept.append((x_got[part], dp, act, dhid))
    if one_each:
        give, keep = both_weight_grads(kept, here, n_ctx, n_dp)
        dx_back, give, keep = lax.optimization_barrier((dx_back, give, keep))
        other = swap(give)
    else:
        mine, far = [], []
        for group in kept:
            give, keep = (
                lax.psum_scatter(
                    g.reshape(-1, g.shape[-1]), "dp", scatter_dimension=0, tiled=True
                ).reshape(g.shape[1:])
                for g in both_weight_grads([group], here, n_ctx, n_dp)
            )
            mine.append(keep)
            far.append(swap(give))
        pieces = [
            jnp.where(here == n // parts, mine[n % parts], far[n % parts]) for n in reversed(range(held))
        ]
    outs, dx_back = lax.optimization_barrier((outs, dx_back))
    returned = exchange(outs, axes)
    if one_each:
        blocks = []
        for n in range(n_dp):
            pick = lambda v: lax.dynamic_index_in_dim(v, lax.rem(my_dp + n, n_dp), 0, keepdims=False)
            blocks.append(add_up([pick(keep), pick(other)]))
        dx_back, blocks[1:] = lax.optimization_barrier((dx_back, blocks[1:]))
        pieces = [block if n == 0 else shift(block, "dp", n) for n, block in enumerate(blocks)]

    d_middle, d_branch_b, d_mixed_b, small = route_back(
        t1c, t2c, expert_ids.reshape(rows, 2), gate_probs, dy_b, middle, gain_moe, w_router, w_out, dx_back
    )

    pairs = width // 128
    calls = [(first, pairs // 3) for first in range(0, pairs, pairs // 3)]

    def call(n, grad):
        return attend_back(q_b, kv_b, kv_other, mixed_b, grad, inv_sum, probs, rows, *calls[n])

    dq0, own0, far0 = call(0, d_mixed_b)
    dq1, own1, far1 = call(1, after(d_mixed_b, dq0))
    fars = [swap(far0), swap(far1)]
    result = unseat(t1c, t2c, after(middle, dq1), returned, parts)
    fars, result = lax.optimization_barrier((fars, result))
    grad_a, d_qkv_a = grad_qkv(
        normed_ab, [dq0, dq1], [own0, own1], fars, (mixed_b, d_branch_b, small)
    )
    grad_a, pieces = lax.optimization_barrier((grad_a, pieces))
    sum_a = add_up(scatter_begin(grad_a, "ctx"))
    d_mixed_b, sum_a = lax.optimization_barrier((d_mixed_b, sum_a))
    got_a = scatter_begin(sum_a, "dp")
    dq2, own2, far2 = call(2, d_mixed_b)
    got_a, dq2, own2, far2 = lax.optimization_barrier((got_a, dq2, own2, far2))
    got_a = scatter_begin(add_up(got_a), "expert")
    far2 = swap(far2)
    got_b, d_qkv_b = grad_qkv_halves(normed_ab, [dq2], [own2], [far2])
    got_a, got_b[0] = lax.optimization_barrier((got_a, got_b[0]))
    got_a = gather_back(add_up(got_a), "expert")
    got_b = scatter_begin(add_up(got_b), "dp")
    got_a, got_b[0] = lax.optimization_barrier((got_a, got_b[0]))
    got_a = gather_back(jnp.stack(got_a), "dp")
    got_b, got_a[0] = lax.optimization_barrier((got_b, got_a[0]))
    got_b = scatter_begin(add_up(got_b), "expert")
    grad_up, grad_down = spread(after(pieces, got_a[0]), my_dp if one_each else jnp.int32(held - 1))
    got_b, grad_up = lax.optimization_barrier((got_b, grad_up))
    got_b = gather_back(add_up(got_b), "expert")
    got_b = gather_back(jnp.stack(got_b), "dp")
    got_a, got_b[0] = lax.optimization_barrier((got_a, got_b[0]))
    all_a = jnp.stack(got_a)
    all_a = (all_a, swap(all_a))

    d_normed_a = 0.0
    for first, d_qkv in ((0, d_qkv_a), (calls[2][0], after(d_qkv_b, all_a[0]))):
        start, wide = 128 * first, d_qkv.shape[1] // 3
        columns = [w_qkv[:, m * width + start : m * width + start + wide] for m in range(3)]
        d_normed_a = d_normed_a + mm(d_qkv, jnp.concatenate(columns, axis=1), NT)
    _, unit_a, inv_a = norm_forward(tokens_b.astype(F32), gain_attn)
    d_tokens = d_middle + norm_backward(d_normed_a, unit_a, inv_a, gain_attn)[0]
    d_tokens, got_b = lax.optimization_barrier((d_tokens, got_b))

    all_b = jnp.stack(got_b)
    all_b = (all_b, swap(all_b))
    cols_a, cols_b, start_b = d_qkv_a.shape[1], d_qkv_b.shape[1], 128 * calls[2][0]
    spans = [
        [(m * cols_a // 3, 0, m * width, cols_a // 3) for m in range(3)]
        + [(cols_a, 1, 0, width), (cols_a + width, 2, 0, SMALL)],
        [(m * cols_b // 3, 0, m * width + start_b, cols_b // 3) for m in range(3)],
    ]
    grad_w_qkv, grad_w_out, small_sum, gain_sum = assemble(
        [all_a, all_b], spans, (3 * width, width, SMALL), w_qkv
    )
    n_small = small.shape[0]
    small_sum = small_sum[:, :n_small] + small_sum[:, n_small : 2 * n_small]
    return (
        result.reshape(image_count, half_len, width),
        d_tokens.reshape(image_count, half_len, width),
        gain_sum[:, 0] / gain_attn,
        grad_w_qkv,
        grad_w_out,
        small_sum[:, expert_count],
        small_sum[:, :expert_count],
        grad_up,
        grad_down,
    )


def solution(mesh):
    placed = (
        P(("expert", "dp"), "ctx", None),
        P(("expert", "dp"), "ctx", None),
        P(("expert", "dp"), "ctx", None),
        P(("expert", "dp"), "ctx", None),
        P(("expert", "dp"), "ctx"),
        P(),
        P(),
        P(),
        P(),
        P(),
        P("expert", None, None),
        P("expert", None, None),
    )
    return jax.shard_map(
        body,
        mesh=mesh,
        in_specs=placed,
        out_specs=(
            P(("expert", "dp"), "ctx", None),
            P(("expert", "dp"), "ctx", None),
            P(),
            P(),
            P(),
            P(),
            P(),
            P("expert", None, ("ctx", "dp")),
            P("expert", ("ctx", "dp"), None),
        ),
        check_vma=False,
    )
```

```python
import functools
import math

import jax
import jax.numpy as jnp
from jax import lax
from jax.experimental import pallas as pl
from jax.experimental.pallas import tpu as pltpu
from jax.sharding import PartitionSpec as P

HEADS = 12
NORM_EPS = 1e-06
BF = jnp.bfloat16
F32 = jnp.float32
NN = (((1,), (0,)), ((), ()))
NT = (((1,), (1,)), ((), ()))
VMEM_BYTES = 60 << 20
EXTRA = 8
SMALL = 128
SAFE = 40.0


def estimate(flops, moved, slow=0):
    return pl.CostEstimate(flops=flops // 4, bytes_accessed=moved // 4, transcendentals=slow // 4)


def mm(left, right, dims=NN):
    return lax.dot_general(left, right, dims, preferred_element_type=F32)


def norm_forward(values_in, gain_vec):
    centre_mean = jnp.mean(values_in, axis=-1, keepdims=True)
    centred = values_in - centre_mean
    inv_scale = lax.rsqrt(jnp.mean(centred * centred, axis=-1, keepdims=True) + NORM_EPS)
    unit_rows = centred * inv_scale
    return (unit_rows * gain_vec, unit_rows, inv_scale)


def norm_backward(gradient, unit_rows, inv_scale, gain_vec):
    scaled = gradient * gain_vec
    inner_sum = (
        scaled
        - jnp.mean(scaled, axis=-1, keepdims=True)
        - unit_rows * jnp.mean(scaled * unit_rows, axis=-1, keepdims=True)
    )
    return (inner_sum * inv_scale, jnp.sum(gradient * unit_rows, axis=0))


def project_kernel(x_ref, gain, w_ref, normed_ref, q_ref, kv_ref):
    width = x_ref.shape[1]
    normed = norm_forward(x_ref[...].astype(F32), gain[...])[0].astype(BF)
    normed_ref[...] = normed
    out = mm(normed, w_ref[...]).astype(BF)
    q_ref[...] = out[:, 0:width]
    kv_ref[...] = out[:, width:]


def project(x, gain, w_qkv, block=256):
    rows, width = x.shape
    line = lambda cols: pl.BlockSpec((block, cols), lambda i: (i, 0))
    return pl.pallas_call(
        project_kernel,
        grid=(rows // block,),
        in_specs=[
            line(width),
            pl.BlockSpec((1, width), lambda i: (0, 0)),
            pl.BlockSpec(w_qkv.shape, lambda i: (0, 0)),
        ],
        out_specs=[line(width), line(width), line(2 * width)],
        out_shape=[jax.ShapeDtypeStruct((rows, n * width), BF) for n in (1, 1, 2)],
        compiler_params=pltpu.CompilerParams(vmem_limit_bytes=VMEM_BYTES),
        cost_estimate=estimate(6 * rows * width * width, 20 * rows * width),
        name="project",
    )(x, gain[None], w_qkv)


def attend_kernel(q_ref, k0, k1, v0, v1, o_ref, p_ref, li_ref, vext, ksize, *, scale):
    half = k0.shape[0]

    def largest(v):
        same = lax.broadcasted_iota(jnp.int32, (128, 128), 0) // 64 == (
            lax.broadcasted_iota(jnp.int32, (128, 128), 1) // 64
        )
        squares = (v.astype(F32) * v.astype(F32)).astype(BF)
        return 1.01 * jnp.max(mm(squares, same.astype(BF)), axis=0, keepdims=True)

    @pl.when(pl.program_id(1) == 0)
    def _():
        ones = jnp.ones((half, 128), BF)
        vext[0:half, 0:128] = v0[...]
        vext[half:, 0:128] = v1[...]
        vext[0:half, 128:256] = ones
        vext[half:, 128:256] = ones
        ksize[...] = jnp.maximum(largest(k0[...]), largest(k1[...]))

    low = lax.broadcasted_iota(jnp.int32, q_ref.shape, 1) < 64
    q = q_ref[...]
    factor = scale * math.log2(math.e)
    small = jnp.max(largest(q) * ksize[...]) * (factor * factor) < SAFE * SAFE

    def run(shifted):
        outs, sums = [], []
        for h in range(2):
            picked = jnp.where(low if h == 0 else jnp.logical_not(low), q, jnp.zeros_like(q))
            s0 = mm(picked, k0[...], NT) * factor
            s1 = mm(picked, k1[...], NT) * factor
            if shifted:
                peak = jnp.maximum(
                    jnp.max(s0, axis=1, keepdims=True), jnp.max(s1, axis=1, keepdims=True)
                )
                s0 = s0 - peak
                s1 = s1 - peak
            p_ref[h, :, 0:half] = jnp.exp2(s0).astype(BF)
            p_ref[h, :, half:] = jnp.exp2(s1).astype(BF)
            both = mm(p_ref[h], vext[...])
            outs.append(both[:, 0:128])
            sums.append(both[:, 128:256])
        inv = 1.0 / jnp.where(low, sums[0], sums[1])
        o_ref[...] = (jnp.where(low, outs[0], outs[1]) * inv).astype(BF)
        li_ref[...] = inv

    pl.when(small)(lambda: run(False))
    pl.when(jnp.logical_not(small))(lambda: run(True))


def attend(q, kv, kv_other, block):
    rows, width = q.shape
    pairs = width // 128
    tile = pl.BlockSpec((block, 128), lambda h, i: (i, h))
    return pl.pallas_call(
        functools.partial(attend_kernel, scale=1.0 / math.sqrt(width // HEADS)),
        grid=(pairs, rows // block),
        in_specs=[
            tile,
            pl.BlockSpec((rows, 128), lambda h, i: (0, h)),
            pl.BlockSpec((rows, 128), lambda h, i: (0, h)),
            pl.BlockSpec((rows, 128), lambda h, i: (0, pairs + h)),
            pl.BlockSpec((rows, 128), lambda h, i: (0, pairs + h)),
        ],
        out_specs=[tile, pl.BlockSpec((2, block, 2 * rows), lambda h, i: (h, i, 0)), tile],
        out_shape=[
            jax.ShapeDtypeStruct((rows, width), BF),
            jax.ShapeDtypeStruct((HEADS, rows, 2 * rows), BF),
            jax.ShapeDtypeStruct((rows, width), F32),
        ],
        scratch_shapes=[pltpu.VMEM((2 * rows, 256), BF), pltpu.VMEM((1, 128), F32)],
        compiler_params=pltpu.CompilerParams(vmem_limit_bytes=VMEM_BYTES),
        cost_estimate=estimate(rows * width, rows * width),
        name="attend",
    )(q, kv, kv_other, kv, kv_other)


def attend_back_kernel(
    q_ref, k0, k1, v0, v1, o_ref, g_ref, li_ref, p_ref,
    dq_ref, own_ref, far_ref, vext, kacc, vacc, *, scale, steps,
):
    i = pl.program_id(1)
    half = k0.shape[0]
    lane = lax.broadcasted_iota(jnp.int32, q_ref.shape, 1)
    low = lane < 64

    @pl.when(i == 0)
    def _():
        ones = jnp.where(lax.broadcasted_iota(jnp.int32, (half, 128), 1) < 2, 1.0, 0.0).astype(BF)
        vext[0:half, 0:128] = v0[...]
        vext[half:, 0:128] = v1[...]
        vext[0:half, 128:256] = ones
        vext[half:, 128:256] = ones

    g = g_ref[...].astype(F32) * li_ref[...]
    gb = g.astype(BF)
    go = g * o_ref[...].astype(F32)
    qt = q_ref[...].T
    gt = gb.T
    dqs = []
    for h in range(2):
        mine = low if h == 0 else jnp.logical_not(low)
        delta = -jnp.sum(jnp.where(mine, go, 0.0), axis=1, keepdims=True)
        high = delta.astype(BF).astype(F32)
        extra = jnp.where(lane == 0, high, jnp.where(lane == 1, delta - high, 0.0)).astype(BF)
        gext = jnp.concatenate([jnp.where(mine, gb, jnp.zeros_like(gb)), extra], axis=1)
        p = p_ref[h]
        ds = (p.astype(F32) * mm(gext, vext[...], NT)).astype(BF)
        dqs.append(mm(ds[:, 0:half], k0[...]) + mm(ds[:, half:], k1[...]))
        rows = slice(64 * h, 64 * h + 64)
        dk = mm(qt[rows], ds)
        dv = mm(gt[rows], p)

        @pl.when(i == 0)
        def _():
            kacc[rows] = dk
            vacc[rows] = dv

        @pl.when(i > 0)
        def _():
            kacc[rows] += dk
            vacc[rows] += dv

    dq_ref[...] = (jnp.where(low, dqs[0], dqs[1]) * scale).astype(BF)

    @pl.when(i == steps - 1)
    def _():
        own_ref[0] = (kacc[:, 0:half].T * scale).astype(BF)
        own_ref[1] = vacc[:, 0:half].T.astype(BF)
        far_ref[0] = (kacc[:, half:].T * scale).astype(BF)
        far_ref[1] = vacc[:, half:].T.astype(BF)


def attend_back(q, kv, kv_other, mixed, grad, inv_sum, probs, block, first, count):
    rows, width = q.shape
    pairs = width // 128
    steps = rows // block
    tile = pl.BlockSpec((block, 128), lambda h, i: (i, first + h))
    both = pl.BlockSpec((2, rows, 128), lambda h, i: (0, 0, h))
    return pl.pallas_call(
        functools.partial(attend_back_kernel, scale=1.0 / math.sqrt(width // HEADS), steps=steps),
        grid=(count, steps),
        in_specs=[
            tile,
            pl.BlockSpec((rows, 128), lambda h, i: (0, first + h)),
            pl.BlockSpec((rows, 128), lambda h, i: (0, first + h)),
            pl.BlockSpec((rows, 128), lambda h, i: (0, pairs + first + h)),
            pl.BlockSpec((rows, 128), lambda h, i: (0, pairs + first + h)),
            tile,
            tile,
            tile,
            pl.BlockSpec((2, block, 2 * rows), lambda h, i: (first + h, i, 0)),
        ],
        out_specs=[pl.BlockSpec((block, 128), lambda h, i: (i, h)), both, both],
        out_shape=[
            jax.ShapeDtypeStruct((rows, 128 * count), BF),
            jax.ShapeDtypeStruct((2, rows, 128 * count), BF),
            jax.ShapeDtypeStruct((2, rows, 128 * count), BF),
        ],
        scratch_shapes=[
            pltpu.VMEM((2 * rows, 256), BF),
            pltpu.VMEM((128, 2 * rows), F32),
            pltpu.VMEM((128, 2 * rows), F32),
        ],
        compiler_params=pltpu.CompilerParams(vmem_limit_bytes=VMEM_BYTES),
        cost_estimate=estimate(rows * width, rows * width),
        name="attend_back",
    )(q, kv, kv_other, kv, kv_other, mixed, grad, inv_sum, probs)


def grad_qkv_kernel(core, normed, *refs, count, with_out):
    if count:
        grad_ref, dqkv_ref = refs[-2:]
        cols = dqkv_ref.shape[1]
        wide = cols // 3
        at = 0
        for n in range(count):
            dq, own, far = refs[n], refs[count + n], refs[2 * count + n]
            size = dq.shape[1]
            dqkv_ref[:, at : at + size] = dq[...]
            for m in range(2):
                start = (m + 1) * wide + at
                dqkv_ref[:, start : start + size] = (own[m].astype(F32) + far[m].astype(F32)).astype(BF)
            at += size
        more = refs[3 * count :]
    else:
        dqkv_ref, grad_ref = refs[0], refs[-1]
        cols = dqkv_ref.shape[1]
        more = refs[1:]
    grad_ref[:, 0:cols] = mm(normed[...].T, dqkv_ref[...]).astype(BF)
    if with_out:
        mixed, branch, small = more[:3]
        width = branch.shape[1]
        grad_ref[:, cols : cols + width] = mm(mixed[...].T, branch[...]).astype(BF)
        value = small[...]
        high = value.astype(BF).astype(F32)
        rest = jnp.zeros((SMALL - 2 * value.shape[0], value.shape[1]), F32)
        grad_ref[:, cols + width :] = jnp.concatenate([high, value - high, rest], axis=0).T.astype(BF)


def grad_qkv_part(core, normed, sides, count, more, half):
    rows, width = normed.shape
    cols = sum(side.shape[-1] for side in sides[:count]) * 3 if count else sides[0].shape[1]
    out_cols = cols + (more[1].shape[1] + SMALL if more else 0)
    full = lambda a: pl.BlockSpec(a.shape, lambda i, core: (0,) * a.ndim)
    part = lambda a: pl.BlockSpec((a.shape[0], half), lambda i, core: (0, core[0]))
    out_specs = [pl.BlockSpec((half, out_cols), lambda i, core: (0, 0))]
    out_shape = [jax.ShapeDtypeStruct((half, out_cols), BF)]
    if count:
        out_specs.append(pl.BlockSpec((rows, cols), lambda i, core: (0, 0)))
        out_shape.append(jax.ShapeDtypeStruct((rows, cols), BF))
    return pl.pallas_call(
        functools.partial(grad_qkv_kernel, count=count, with_out=bool(more)),
        grid_spec=pltpu.PrefetchScalarGridSpec(
            num_scalar_prefetch=1,
            grid=(1,),
            in_specs=[part(normed)]
            + [full(side) for side in sides]
            + ([part(more[0]), full(more[1]), part(more[2])] if more else []),
            out_specs=out_specs,
        ),
        out_shape=out_shape,
        compiler_params=pltpu.CompilerParams(vmem_limit_bytes=VMEM_BYTES),
        cost_estimate=estimate(rows * width, rows * width),
        name="grad_qkv",
    )(core.astype(jnp.int32)[None], normed, *sides, *more)


def grad_qkv(normed, dqs, owns, fars, more=()):
    return grad_qkv_part(jnp.int32(0), normed, (*dqs, *owns, *fars), len(dqs), more, normed.shape[1])


def grad_qkv_halves(normed, dqs, owns, fars):
    here = lax.axis_index("ctx")
    half = normed.shape[1] // 2
    give, d_qkv = grad_qkv_part(1 - here, normed, (*dqs, *owns, *fars), len(dqs), (), half)
    other = swap(give)
    (keep,) = grad_qkv_part(here, normed, (d_qkv,), 0, (), half)
    return [keep, other], d_qkv


GELU_A = math.sqrt(2.0 / math.pi)
GELU_B = 0.044715


def gelu_both(v):
    square = v * v
    t = jnp.tanh(v * (GELU_A + GELU_A * GELU_B * square))
    half = 0.5 + 0.5 * t
    slope = half + (0.5 * v) * (1.0 - t * t) * (GELU_A + 3 * GELU_A * GELU_B * square)
    return v * half, slope


def put_extra(ref, r, row):
    width = ref.shape[2]
    cap = row.shape[1]
    line = lax.broadcasted_iota(jnp.int32, (EXTRA, cap), 0)
    full = jnp.zeros((EXTRA, cap), F32)
    for n, piece in enumerate(three_parts(row)):
        full = jnp.where(line == n, piece.astype(F32), full)
    full = jnp.concatenate([full, jnp.zeros((EXTRA, width - cap), F32)], axis=1)
    ref[r, ref.shape[1] - EXTRA :, :] = full.astype(BF)


def get_extra(ref, r, lanes):
    sent = ref[r, ref.shape[1] - EXTRA :, lanes].astype(F32)
    return sent[0:1] + sent[1:2] + sent[2:3]


def expert_kernel(which, x_in, gate_in, dy_in, *refs, part, parts, steps, first):
    last = part == parts - 1
    if not first:
        refs = refs[1:]
    dg_in = ()
    if last:
        dg_in, refs = refs[: parts - 1], refs[parts - 1 :]
    up_ref, down_ref, out_ref, dx_ref, act_ref, dhid_ref, dp_ref, *refs = refs
    if not last:
        dg_out, refs = refs[0], refs[1:]
    x, gate, out_acc, dx_acc = refs
    f = pl.program_id(0)
    peers, cap = dy_in.shape[0], dy_in.shape[1]

    @pl.when(f == 0)
    def _():
        lanes = slice(part * cap, (part + 1) * cap)
        gates = jnp.concatenate([get_extra(gate_in, r, lanes) for r in range(peers)], axis=0).T
        for r in range(peers):
            at = slice(r * cap, (r + 1) * cap)
            x[at] = x_in[r, 0:cap, :]
            g = gates[:, r : r + 1]
            gate[at] = g
            dp_ref[at] = (dy_in[r].astype(F32) * g).astype(BF)

    up = up_ref[0]
    down = down_ref[0]
    value, slope = gelu_both(mm(x[...], up))
    act_ref[...] = value.astype(BF)
    dhid_ref[...] = (mm(dp_ref[...], down, NT) * slope).astype(BF)

    @pl.when(f == 0)
    def _():
        dx_acc[...] = mm(dhid_ref[...], up, NT)
        out_acc[...] = mm(act_ref[...], down)

    @pl.when(f > 0)
    def _():
        dx_acc[...] += mm(dhid_ref[...], up, NT)
        out_acc[...] += mm(act_ref[...], down)

    @pl.when(f == steps - 1)
    def _():
        sums = []
        for r in range(peers):
            at = slice(r * cap, (r + 1) * cap)
            produced = out_acc[at].astype(BF).astype(F32)
            dx_ref[r, 0:cap, :] = dx_acc[at].astype(BF)
            out_ref[r] = (produced * gate[at]).astype(BF)
            sums.append(jnp.sum(produced * dy_in[r].astype(F32), axis=1, keepdims=True))
        sums = jnp.concatenate(sums, axis=1).T
        if last:
            full = jnp.concatenate([ref[...] for ref in dg_in] + [sums], axis=1)
            for r in range(peers):
                put_extra(dx_ref, r, full[r : r + 1])
        else:
            dg_out[...] = sums


def run_expert(which, part, parts, x, first_x, dy, outs, dgates, w_up, w_down, chunk=768):
    peers, width = x.shape[0], x.shape[2]
    cap = dy.shape[1] // parts
    rows = peers * cap
    hidden = w_up.shape[-1]
    last = part == parts - 1
    full = lambda shape: pl.BlockSpec(shape, lambda f, j: (0,) * len(shape))
    wide = pl.BlockSpec((rows, chunk), lambda f, j: (0, f))
    dx_shape = (peers, cap + (EXTRA if last else 0), width)
    extra_at = (first_x.shape[1] - EXTRA) // EXTRA
    out_specs = [
        pl.BlockSpec((peers, cap, width), lambda f, j: (0, part, 0)),
        full(dx_shape), wide, wide, full((rows, width)),
    ]
    out_shape = [
        jax.ShapeDtypeStruct(dy.shape, BF),
        jax.ShapeDtypeStruct(dx_shape, BF),
        jax.ShapeDtypeStruct((rows, hidden), BF),
        jax.ShapeDtypeStruct((rows, hidden), BF),
        jax.ShapeDtypeStruct((rows, width), BF),
    ]
    if not last:
        out_specs.append(full((peers, cap)))
        out_shape.append(jax.ShapeDtypeStruct((peers, cap), F32))
        dgates = []
    return pl.pallas_call(
        functools.partial(
            expert_kernel, part=part, parts=parts, steps=hidden // chunk, first=outs is None
        ),
        grid_spec=pltpu.PrefetchScalarGridSpec(
            num_scalar_prefetch=1,
            grid=(hidden // chunk,),
            in_specs=[
                full(x.shape),
                pl.BlockSpec((peers, EXTRA, width), lambda f, j: (0, extra_at, 0)),
                pl.BlockSpec((peers, cap, width), lambda f, j: (0, part, 0)),
                *[pl.BlockSpec(memory_space=pl.ANY)] * (outs is not None),
                *[full(d.shape) for d in dgates],
                pl.BlockSpec((1, width, chunk), lambda f, j: (j[0], 0, f)),
                pl.BlockSpec((1, chunk, width), lambda f, j: (j[0], f, 0)),
            ],
            out_specs=out_specs,
            scratch_shapes=[
                pltpu.VMEM((rows, width), BF),
                pltpu.VMEM((rows, 1), F32),
                pltpu.VMEM((rows, width), F32),
                pltpu.VMEM((rows, width), F32),
            ],
        ),
        out_shape=out_shape,
        compiler_params=pltpu.CompilerParams(vmem_limit_bytes=VMEM_BYTES),
        cost_estimate=estimate(8 * rows * width * hidden, 4 * width * hidden, rows * hidden),
        input_output_aliases={} if outs is None else {4: 0},
        name="expert",
    )(which, x, first_x, dy, *([] if outs is None else [outs]), *dgates, w_up, w_down)


def weights_kernel(at, *refs, count, pieces, turned):
    acts, dhids, refs = refs[:count], refs[count : 2 * count], refs[2 * count :]
    if turned:
        xt, dpt, out_ref = refs
    else:
        xs, dps, (out_ref, xt, dpt) = refs[:count], refs[count : 2 * count], refs[2 * count :]

        @pl.when(pl.program_id(0) == 0)
        def _():
            place = 0
            for x, dp in zip(xs, dps):
                rows = dp.shape[0]
                cap = rows // x.shape[0]
                held = jnp.concatenate([x[r, 0:cap, :] for r in range(x.shape[0])], axis=0)
                xt[:, place : place + rows] = held.T
                dpt[:, place : place + rows] = dp[...].T
                place += rows

    def product(left, rights):
        total, place = None, 0
        for right in rights:
            rows = right.shape[0]
            add = mm(left[:, place : place + rows], right[...])
            total = add if total is None else total + add
            place += rows
        return total.astype(BF)

    gup = product(xt, dhids)
    gdown = product(dpt, acts)
    wide = gup.shape[1] // pieces
    for s in range(pieces):
        out_ref[s, 0] = gup[:, s * wide : (s + 1) * wide]
        out_ref[s, 1] = gdown[:, s * wide : (s + 1) * wide]


def weight_grads(core, acts, dhids, sides, turned, n_ctx, n_dp, chunk=768):
    width, hidden = (sides[0].shape[0] if turned else sides[0].shape[2]), acts[0].shape[1]
    rows = sum(a.shape[0] for a in acts)
    half = hidden // n_ctx
    steps = half // chunk
    wide = half // n_dp
    pieces = chunk // wide
    full = lambda shape: pl.BlockSpec(shape, lambda f, at: (0,) * len(shape))
    out_specs = [pl.BlockSpec((pieces, 2, width, wide), lambda f, at: (f, 0, 0, 0))]
    out_shape = [jax.ShapeDtypeStruct((n_dp, 2, width, wide), BF)]
    if not turned:
        out_specs += [full((width, rows))] * 2
        out_shape += [jax.ShapeDtypeStruct((width, rows), BF)] * 2
    made = pl.pallas_call(
        functools.partial(weights_kernel, count=len(acts), pieces=pieces, turned=turned),
        grid_spec=pltpu.PrefetchScalarGridSpec(
            num_scalar_prefetch=1,
            grid=(steps,),
            in_specs=[
                pl.BlockSpec((a.shape[0], chunk), lambda f, at: (0, at[0] * steps + f))
                for a in (*acts, *dhids)
            ]
            + [full(a.shape) for a in sides],
            out_specs=out_specs,
        ),
        out_shape=out_shape,
        compiler_params=pltpu.CompilerParams(vmem_limit_bytes=VMEM_BYTES),
        cost_estimate=estimate(rows * width, rows * width),
        name="weight_grads",
    )(core.astype(jnp.int32)[None], *acts, *dhids, *sides)
    return made[0], made[1:]


def both_weight_grads(group, here, n_ctx, n_dp):
    xs, dps, acts, dhids = zip(*group)
    give, sides = weight_grads(1 - here, acts, dhids, (*xs, *dps), False, n_ctx, n_dp)
    keep, _ = weight_grads(here, acts, dhids, sides, True, n_ctx, n_dp)
    return give, keep


def seats(expert_ids, seat_order, expert_count, capacity, slot_of):
    token_count = expert_ids.shape[0]
    places = jnp.arange(token_count, dtype=jnp.int32)
    earlier = (seat_order[:, None] < seat_order[None, :]) | (
        seat_order[:, None] == seat_order[None, :]
    ) & (places[:, None] < places[None, :])
    earlier = earlier.astype(BF)
    lane_ids = jnp.arange(expert_count, dtype=jnp.int32)
    first_hot = expert_ids[:, 0:1] == lane_ids[None, :]
    second_hot = expert_ids[:, 1:2] == lane_ids[None, :]
    both_hot = jnp.concatenate([first_hot, second_hot], axis=1).astype(BF)
    ahead = jnp.einsum("st,se->te", earlier, both_hot, preferred_element_type=F32)
    ahead_first = ahead[:, :expert_count]
    ahead_second = ahead[:, expert_count:] + jnp.sum(first_hot.astype(F32), axis=0)[None, :]
    rank_first = jnp.sum(jnp.where(first_hot, ahead_first, 0.0), axis=-1)
    rank_second = jnp.sum(jnp.where(second_hot, ahead_second, 0.0), axis=-1)

    def slot(picked, rank):
        at = rank.astype(jnp.int32)
        return jnp.where(at < capacity, slot_of(picked, at), -1)

    return (
        slot(expert_ids[:, 0], rank_first),
        slot(expert_ids[:, 1], rank_second),
        first_hot,
        second_hot,
    )


def three_parts(v):
    high = v.astype(BF)
    rest = v - high.astype(F32)
    mid = rest.astype(BF)
    return high, mid, (rest - mid.astype(F32)).astype(BF)


def seat_rows_kernel(t1, t2, *refs, chosen, parts, cap):
    *gate_refs, rows_ref, out_ref = refs
    peers = out_ref.shape[0]
    tokens = t1.shape[1]
    group = min(peers, max(1, 256 // cap))

    def hot_of(t, part, r):
        ids = lax.broadcasted_iota(jnp.int32, (group * cap, tokens), 0) + (part * peers + r) * cap
        return ids == t[...]

    for n, part in enumerate(chosen):
        for r in range(0, peers, group):
            hot = hot_of(t1, part, r) | hot_of(t2, part, r)
            got = mm(jnp.where(hot, 1.0, 0.0).astype(BF), rows_ref[...]).astype(BF)
            for m in range(group):
                out_ref[r + m, n * cap : (n + 1) * cap, :] = got[m * cap : (m + 1) * cap]
    if gate_refs:
        lefts = [jnp.concatenate(three_parts(g[...]), axis=0) for g in gate_refs]
        for r in range(0, peers, group):
            got = []
            for part in range(parts):
                both = sum(
                    mm(left, jnp.where(hot_of(t, part, r), 1.0, 0.0).astype(BF), NT)
                    for left, t in zip(lefts, (t1, t2))
                )
                got.append(jnp.sum(both, axis=0, keepdims=True))
            for m in range(group):
                put_extra(
                    out_ref, r + m, jnp.concatenate([g[:, m * cap : (m + 1) * cap] for g in got], axis=1)
                )


def seat_rows(t1, t2, rows, gates, chosen, parts, peers, cap):
    tokens, width = rows.shape
    per_peer = len(chosen) * cap + (EXTRA if gates else 0)
    return pl.pallas_call(
        functools.partial(seat_rows_kernel, chosen=chosen, parts=parts, cap=cap),
        out_shape=jax.ShapeDtypeStruct((peers, per_peer, width), BF),
        compiler_params=pltpu.CompilerParams(vmem_limit_bytes=VMEM_BYTES),
        cost_estimate=estimate(2 * peers * per_peer * tokens * width, 4 * tokens * width),
        name="seat_rows",
    )(t1[None], t2[None], *[g[None] for g in gates], rows)


def rows_back(t1, t2, back, extra, split=1):
    tokens = t1.shape[0]
    total, place = None, 0
    firsts = jnp.zeros((tokens, 1), F32)
    seconds = firsts
    peers = back[0].shape[0]
    parts = [(ref, 0, back[0].shape[1]) for ref in back]
    if split > 1:
        cap = back[0].shape[1] // split
        parts = [(back[0], n * cap, cap) for n in range(split)]
    for part, (ref, start, cap) in enumerate(parts):
        group = min(peers, max(1, 512 // cap))
        for b in range(0, peers, group):
            ids = lax.broadcasted_iota(jnp.int32, (tokens, group * cap), 1) + place
            place += group * cap
            first = ids == t1
            second = ids == t2
            hot = jnp.where(first | second, 1.0, 0.0).astype(BF)
            add = mm(hot, jnp.concatenate([ref[b + n, start : start + cap, :] for n in range(group)], axis=0))
            total = add if total is None else total + add
            if extra:
                lanes = slice(part * cap, (part + 1) * cap)
                dg = jnp.concatenate([get_extra(back[-1], b + n, lanes) for n in range(group)], axis=1)
                firsts += jnp.sum(jnp.where(first, dg, 0.0), axis=1, keepdims=True)
                seconds += jnp.sum(jnp.where(second, dg, 0.0), axis=1, keepdims=True)
    return total, firsts, seconds


def unseat_kernel(t1, t2, base, back, out_ref, *, split, sub):
    for r in range(0, t1.shape[0], sub):
        at = slice(r, r + sub)
        total, _, _ = rows_back(t1[at], t2[at], [back], False, split)
        out_ref[at] = (base[at] + total).astype(BF)


def unseat(t1, t2, base, back, split, block=512, sub=512):
    tokens, width = base.shape
    col = pl.BlockSpec((block, 1), lambda i: (i, 0))
    rows = pl.BlockSpec((block, width), lambda i: (i, 0))
    return pl.pallas_call(
        functools.partial(unseat_kernel, split=split, sub=sub),
        grid=(tokens // block,),
        in_specs=[col, col, rows, pl.BlockSpec(back.shape, lambda i: (0, 0, 0))],
        out_specs=rows,
        out_shape=jax.ShapeDtypeStruct((tokens, width), BF),
        compiler_params=pltpu.CompilerParams(vmem_limit_bytes=VMEM_BYTES),
        cost_estimate=estimate(tokens * width, tokens * width),
        name="unseat",
    )(t1, t2, base, back)


def route_back_kernel(
    t1, t2, ids, probs, dy, middle, gain, w_router, w_out, *refs, sub
):
    dmiddle_ref, dbranch_ref, dmixed_ref, small_ref = refs[-4:]
    experts = probs.shape[1]
    to_router, to_gain = 0.0, 0.0
    for r in range(0, t1.shape[0], sub):
        at = slice(r, r + sub)
        d_routed, dg1, dg2 = rows_back(t1[at], t2[at], refs[:-4], True)
        p = probs[at]
        lane = lax.broadcasted_iota(jnp.int32, p.shape, 1)
        d_gates = jnp.where(lane == ids[at, 0:1], dg1, 0.0) + jnp.where(lane == ids[at, 1:2], dg2, 0.0)
        d_logits = p * (d_gates - jnp.sum(p * d_gates, axis=1, keepdims=True))
        for piece in three_parts(d_logits):
            d_routed = d_routed + mm(piece, w_router[...], NT)
        normed, unit, inv = norm_forward(middle[at], gain[...])
        routed = normed.astype(BF)
        scaled = d_routed * gain[...]
        d_norm = inv * (
            scaled
            - jnp.mean(scaled, axis=1, keepdims=True)
            - unit * jnp.mean(scaled * unit, axis=1, keepdims=True)
        )
        d_middle = dy[at].astype(F32) + d_norm
        d_branch = d_middle.astype(BF)
        dmiddle_ref[at] = d_middle
        dbranch_ref[at] = d_branch
        dmixed_ref[at] = mm(d_branch, w_out[...], NT).astype(BF)
        for piece in three_parts(d_logits.T):
            to_router = to_router + mm(piece, routed)
        to_gain = to_gain + jnp.sum(d_routed * unit, axis=0, keepdims=True)

    @pl.when(pl.program_id(0) == 0)
    def _():
        small_ref[...] = jnp.zeros_like(small_ref)

    small_ref[0:experts, :] += to_router
    small_ref[experts : experts + 1, :] += to_gain


def route_back(t1, t2, ids, probs, dy, middle, gain, w_router, w_out, parts, block=512, sub=256):
    tokens, width = dy.shape
    experts = probs.shape[1]
    line = lambda cols: pl.BlockSpec((block, cols), lambda i: (i, 0))
    full = lambda a: pl.BlockSpec(a.shape, lambda i: (0,) * a.ndim)
    gain = gain[None]
    return pl.pallas_call(
        functools.partial(route_back_kernel, sub=sub),
        grid=(tokens // block,),
        in_specs=[
            line(1), line(1), line(2), line(experts), line(width), line(width),
            full(gain), full(w_router), full(w_out),
        ]
        + [full(part) for part in parts],
        out_specs=[
            line(width), line(width), line(width),
            pl.BlockSpec((experts + 8, width), lambda i: (0, 0)),
        ],
        out_shape=[
            jax.ShapeDtypeStruct((tokens, width), F32),
            jax.ShapeDtypeStruct((tokens, width), BF),
            jax.ShapeDtypeStruct((tokens, width), BF),
            jax.ShapeDtypeStruct((experts + 8, width), F32),
        ],
        compiler_params=pltpu.CompilerParams(vmem_limit_bytes=VMEM_BYTES),
        cost_estimate=estimate(tokens * width, tokens * width),
        name="route_back",
    )(t1, t2, ids, probs, dy, middle, gain, w_router, w_out, *parts)


def swap(value):
    n = lax.axis_size("ctx")
    return lax.ppermute(value, "ctx", [(i, (i + 1) % n) for i in range(n)])


def exchange(value, axes):
    return lax.all_to_all(value, axes, 0, 0, tiled=True)


def shift(value, axis, by):
    n = lax.axis_size(axis)
    return lax.ppermute(value, axis, [(i, (i + by) % n) for i in range(n)])


def scatter_begin(value, axis):
    n = lax.axis_size(axis)
    me = lax.axis_index(axis)
    x = value.reshape(n, value.shape[0] // n, value.shape[1])
    pick = lambda at: lax.dynamic_index_in_dim(x, at, 0, keepdims=False)
    return [pick(me)] + [shift(pick(lax.rem(me + s, n)), axis, s) for s in range(1, n)]


def add_up(pieces):
    total = pieces[0].astype(F32)
    for piece in pieces[1:]:
        total = total + piece.astype(F32)
    return total.astype(BF)


def gather_back(x, axis):
    n = lax.axis_size(axis)
    return [x] + [shift(x, axis, s) for s in range(1, n)]


def assemble_kernel(at, w_ref, *refs, groups, spans, n_small):
    ins, outs = refs[: 2 * groups], refs[2 * groups :]
    me = at[2]
    owners, rows = ins[0].shape[1], ins[0].shape[2]

    def write(held):
        for z in range(owners):
            back = lax.rem(me + owners - z, owners)
            for ref, span in zip(held, spans):
                piece = ref[0, back].astype(F32)
                for src, which, dst, size in span:
                    outs[which][z * rows : (z + 1) * rows, dst : dst + size] = piece[:, src : src + size]

    is_mine = pl.program_id(0) == at[0]
    pl.when(is_mine)(lambda: write(ins[:groups]))
    pl.when(jnp.logical_not(is_mine))(lambda: write(ins[groups:]))
    both = outs[2][...]
    outs[2][:, 0:n_small] = both[:, 0:n_small] + both[:, n_small : 2 * n_small]
    outs[-1][...] = jnp.sum(outs[0][...] * w_ref[...].astype(F32), axis=1, keepdims=True)


def assemble(sums, spans, widths, w_qkv, n_small):
    n_dp, owners, rows, _ = sums[0][0].shape
    n_ctx = lax.axis_size("ctx")
    block = owners * rows
    height = n_ctx * n_dp * block
    at = jnp.stack([lax.axis_index(axis) for axis in ("ctx", "dp", "expert")]).astype(jnp.int32)

    def back(mine):
        def place(c, d, at):
            edge = jnp.where(c == 0, 0, n_dp - 1)
            return ((at[1] + n_dp - jnp.where((c == at[0]) == mine, d, edge)) % n_dp, 0, 0, 0)

        return place

    line = lambda cols: pl.BlockSpec((block, cols), lambda c, d, at: (c * n_dp + d, 0))
    widths = [*widths, 1]
    return pl.pallas_call(
        functools.partial(assemble_kernel, groups=len(sums), spans=spans, n_small=n_small),
        grid_spec=pltpu.PrefetchScalarGridSpec(
            num_scalar_prefetch=1,
            grid=(n_ctx, n_dp),
            in_specs=[line(w_qkv.shape[1])]
            + [pl.BlockSpec((1,) + mine.shape[1:], back(True)) for mine, _ in sums]
            + [pl.BlockSpec((1,) + mine.shape[1:], back(False)) for mine, _ in sums],
            out_specs=[line(cols) for cols in widths],
        ),
        out_shape=[jax.ShapeDtypeStruct((height, cols), F32) for cols in widths],
        compiler_params=pltpu.CompilerParams(vmem_limit_bytes=VMEM_BYTES),
        cost_estimate=estimate(height * 2304, 12 * height * 2304),
        name="assemble",
    )(at, w_qkv, *[mine for mine, _ in sums], *[other for _, other in sums])


def spread_kernel(at, *refs):
    *ins, up_ref, down_ref = refs
    j = pl.program_id(0)
    for s, src in enumerate(ins):

        @pl.when(lax.rem(at[0] + len(ins) - s, len(ins)) == j)
        def _():
            up_ref[0] = src[0].astype(F32)
            down_ref[0] = src[1].astype(F32).T


def spread(pieces, place):
    count = len(pieces)
    _, width, cols = pieces[0].shape
    return pl.pallas_call(
        spread_kernel,
        grid_spec=pltpu.PrefetchScalarGridSpec(
            num_scalar_prefetch=1,
            grid=(count,),
            in_specs=[pl.BlockSpec((2, width, cols), lambda j, at: (0, 0, 0))] * count,
            out_specs=[
                pl.BlockSpec((1, width, cols), lambda j, at: (j, 0, 0)),
                pl.BlockSpec((1, cols, width), lambda j, at: (j, 0, 0)),
            ],
        ),
        out_shape=[
            jax.ShapeDtypeStruct((count, width, cols), F32),
            jax.ShapeDtypeStruct((count, cols, width), F32),
        ],
        compiler_params=pltpu.CompilerParams(vmem_limit_bytes=VMEM_BYTES),
        cost_estimate=estimate(width * cols, 12 * count * width * cols),
        name="spread",
    )(place.astype(jnp.int32)[None], *pieces)


def after(value, *others):
    return lax.optimization_barrier((value, others))[0]


def body(
    tokens,
    cotangent,
    router_noise,
    expert_ids,
    seat_order,
    gain_attn,
    w_qkv,
    w_out,
    gain_moe,
    w_router,
    w_up,
    w_down,
):
    image_count, half_len, width = tokens.shape
    rows = image_count * half_len
    expert_count = router_noise.shape[-1]
    n_owner = lax.axis_size("expert")
    n_ctx = lax.axis_size("ctx")
    n_dp = lax.axis_size("dp")
    here = lax.axis_index("ctx")
    my_dp = lax.axis_index("dp")
    held = w_up.shape[0]
    capacity = (2 * rows + expert_count - 1) // expert_count
    one_each = held == n_dp
    if one_each:
        parts, peers, axes = 2, n_owner * n_dp, ("expert", "dp")
        cap = capacity // parts
        slot_of = lambda e, at: (at // cap * peers + e) * cap + at % cap
        which = [my_dp] * parts
    else:
        parts, peers, axes = held // n_ctx, n_owner * n_ctx, ("expert", "ctx")
        cap = capacity
        slot_of = lambda e, at: ((e % parts) * peers + e // parts) * cap + at
        which = [here * parts + part for part in range(parts)]

    t1, t2, first_hot, second_hot = seats(
        expert_ids.reshape(rows, 2), seat_order.reshape(rows), expert_count, capacity, slot_of
    )
    dy_b = cotangent.reshape(rows, width)
    every = tuple(range(parts))
    dy_slots = seat_rows(t1, t2, dy_b, (), every, parts, peers, cap)
    dy_got = exchange(dy_slots, axes)

    tokens_b = after(tokens, dy_slots).reshape(rows, width)
    normed_ab, q_b, kv_b = project(tokens_b, gain_attn, w_qkv)
    kv_other = swap(kv_b)
    mixed_b, probs, inv_sum = attend(q_b, kv_b, kv_other, rows)

    middle = tokens_b.astype(F32) + mm(mixed_b, w_out)
    normed_m, _, _ = norm_forward(middle, gain_moe)
    routed_b = normed_m.astype(BF)
    logits = mm(routed_b, w_router) + router_noise.reshape(rows, expert_count)
    gate_probs = jax.nn.softmax(logits, axis=-1)
    gate_first = jnp.sum(jnp.where(first_hot, gate_probs, 0.0), axis=-1)
    gate_second = jnp.sum(jnp.where(second_hot, gate_probs, 0.0), axis=-1)

    sent = [
        seat_rows(
            t1, t2, routed_b, () if part else (gate_first, gate_second), (part,), parts, peers, cap
        )
        for part in every
    ]
    sent[0], dy_got = lax.optimization_barrier((sent[0], dy_got))
    x_got = [exchange(sent[0], axes)]
    outs, dx_back, dgates, kept = None, [], [], []
    t1c, t2c = t1[:, None], t2[:, None]
    for part in every:
        last = part == parts - 1
        x = x_got[part]
        if not last:
            x, following, t1c, t2c = lax.optimization_barrier((x, sent[part + 1], t1c, t2c))
            x_got.append(exchange(following, axes))
        outs, dx, act, dhid, dp, *dg = run_expert(
            which[part].astype(jnp.int32)[None], part, parts, x, x_got[0], dy_got, outs, dgates, w_up, w_down
        )
        dgates += dg
        if not last:
            dx, x_got[-1] = lax.optimization_barrier((dx, x_got[-1]))
        if dx_back:
            dx, dx_back[-1], act = lax.optimization_barrier((dx, dx_back[-1], act))
        dx_back.append(exchange(dx, axes))
        kept.append((x_got[part], dp, act, dhid))
    if one_each:
        give, keep = both_weight_grads(kept, here, n_ctx, n_dp)
        dx_back, give, keep = lax.optimization_barrier((dx_back, give, keep))
        other = swap(give)
    else:
        mine, far = [], []
        for group in kept:
            give, keep = (
                lax.psum_scatter(
                    g.reshape(-1, g.shape[-1]), "dp", scatter_dimension=0, tiled=True
                ).reshape(g.shape[1:])
                for g in both_weight_grads([group], here, n_ctx, n_dp)
            )
            mine.append(keep)
            far.append(swap(give))
        pieces = [
            jnp.where(here == n // parts, mine[n % parts], far[n % parts]) for n in reversed(range(held))
        ]
    outs, dx_back = lax.optimization_barrier((outs, dx_back))
    returned = exchange(outs, axes)
    if one_each:
        blocks = []
        for n in range(n_dp):
            pick = lambda v: lax.dynamic_index_in_dim(v, lax.rem(my_dp + n, n_dp), 0, keepdims=False)
            blocks.append(add_up([pick(keep), pick(other)]))
        dx_back, blocks[1:] = lax.optimization_barrier((dx_back, blocks[1:]))
        pieces = [block if n == 0 else shift(block, "dp", n) for n, block in enumerate(blocks)]

    d_middle, d_branch_b, d_mixed_b, small = route_back(
        t1c, t2c, expert_ids.reshape(rows, 2), gate_probs, dy_b, middle, gain_moe, w_router, w_out, dx_back
    )

    pairs = width // 128
    calls = [(first, pairs // 3) for first in range(0, pairs, pairs // 3)]

    def call(n, grad):
        return attend_back(q_b, kv_b, kv_other, mixed_b, grad, inv_sum, probs, rows, *calls[n])

    dq0, own0, far0 = call(0, d_mixed_b)
    dq1, own1, far1 = call(1, after(d_mixed_b, dq0))
    fars = [swap(far0), swap(far1)]
    result = unseat(t1c, t2c, after(middle, dq1), returned, parts)
    fars, result = lax.optimization_barrier((fars, result))
    grad_a, d_qkv_a = grad_qkv(
        normed_ab, [dq0, dq1], [own0, own1], fars, (mixed_b, d_branch_b, small)
    )
    grad_a, pieces = lax.optimization_barrier((grad_a, pieces))
    sum_a = add_up(scatter_begin(grad_a, "ctx"))
    d_mixed_b, sum_a = lax.optimization_barrier((d_mixed_b, sum_a))
    got_a = scatter_begin(sum_a, "dp")
    dq2, own2, far2 = call(2, d_mixed_b)
    got_a, dq2, own2, far2 = lax.optimization_barrier((got_a, dq2, own2, far2))
    got_a = scatter_begin(add_up(got_a), "expert")
    far2 = swap(far2)
    got_b, d_qkv_b = grad_qkv_halves(normed_ab, [dq2], [own2], [far2])
    got_a, got_b[0] = lax.optimization_barrier((got_a, got_b[0]))
    got_a = gather_back(add_up(got_a), "expert")
    got_b = scatter_begin(add_up(got_b), "dp")
    got_a, got_b[0] = lax.optimization_barrier((got_a, got_b[0]))
    got_a = gather_back(jnp.stack(got_a), "dp")
    got_b, got_a[0] = lax.optimization_barrier((got_b, got_a[0]))
    got_b = scatter_begin(add_up(got_b), "expert")
    grad_up, grad_down = spread(after(pieces, got_a[0]), my_dp if one_each else jnp.int32(held - 1))
    got_b, grad_up = lax.optimization_barrier((got_b, grad_up))
    got_b = gather_back(add_up(got_b), "expert")
    got_b = gather_back(jnp.stack(got_b), "dp")
    got_a, got_b[0] = lax.optimization_barrier((got_a, got_b[0]))
    all_a = jnp.stack(got_a)
    all_a = (all_a, swap(all_a))

    d_normed_a = 0.0
    for first, d_qkv in ((0, d_qkv_a), (calls[2][0], after(d_qkv_b, all_a[0]))):
        start, wide = 128 * first, d_qkv.shape[1] // 3
        columns = [w_qkv[:, m * width + start : m * width + start + wide] for m in range(3)]
        d_normed_a = d_normed_a + mm(d_qkv, jnp.concatenate(columns, axis=1), NT)
    _, unit_a, inv_a = norm_forward(tokens_b.astype(F32), gain_attn)
    d_tokens = d_middle + norm_backward(d_normed_a, unit_a, inv_a, gain_attn)[0]
    d_tokens, got_b = lax.optimization_barrier((d_tokens, got_b))

    all_b = jnp.stack(got_b)
    all_b = (all_b, swap(all_b))
    cols_a, cols_b, start_b = d_qkv_a.shape[1], d_qkv_b.shape[1], 128 * calls[2][0]
    spans = [
        [(m * cols_a // 3, 0, m * width, cols_a // 3) for m in range(3)]
        + [(cols_a, 1, 0, width), (cols_a + width, 2, 0, SMALL)],
        [(m * cols_b // 3, 0, m * width + start_b, cols_b // 3) for m in range(3)],
    ]
    grad_w_qkv, grad_w_out, small_sum, gain_sum = assemble(
        [all_a, all_b], spans, (3 * width, width, SMALL), w_qkv, small.shape[0]
    )
    return (
        result.reshape(image_count, half_len, width),
        d_tokens.reshape(image_count, half_len, width),
        gain_sum[:, 0] / gain_attn,
        grad_w_qkv,
        grad_w_out,
        small_sum[:, expert_count],
        small_sum[:, :expert_count],
        grad_up,
        grad_down,
    )


def solution(mesh):
    placed = (
        P(("expert", "dp"), "ctx", None),
        P(("expert", "dp"), "ctx", None),
        P(("expert", "dp"), "ctx", None),
        P(("expert", "dp"), "ctx", None),
        P(("expert", "dp"), "ctx"),
        P(),
        P(),
        P(),
        P(),
        P(),
        P("expert", None, None),
        P("expert", None, None),
    )
    return jax.shard_map(
        body,
        mesh=mesh,
        in_specs=placed,
        out_specs=(
            P(("expert", "dp"), "ctx", None),
            P(("expert", "dp"), "ctx", None),
            P(),
            P(),
            P(),
            P(),
            P(),
            P("expert", None, ("ctx", "dp")),
            P("expert", ("ctx", "dp"), None),
        ),
        check_vma=False,
    )
```
